32 devices in a mesh: slab: 8 (over z, x), grp: 4 (over y, core).
Axes of the slice: x: 2, y: 2, z: 4, core: 2. Of those that a mesh axis runs over, the one named last changes fastest.
Arguments:
- fine_input: bfloat16 [16, 128, 128, 128], P('slab', 'grp'), may hold values from -6 to 6
- out_grad: bfloat16 [16, 128, 128, 128], P('slab', 'grp')
- pre_norm: bfloat16 [256, 8, 4096], P('slab', None, 'grp')
- act_out: bfloat16 [256, 8, 4096], P('slab', None, 'grp'), as said below
- norm_gain: float32 [256], P('slab'), may hold values from 0.5 to 2
- w_down: bfloat16 [27, 128, 256], replicated, may hold values from -0.109375 to 0.109375
- w_up: bfloat16 [8, 256, 128], replicated, may hold values from -0.375 to 0.375
Outputs:
- grad_input: bfloat16 [16, 128, 128, 128], P('slab', 'grp')
- grad_down: float32 [256, 27, 128], P(('slab', 'grp'))
- grad_gain: float32 [256], P('slab')
- grad_shift: float32 [256], P('slab')
The draws below stay inside these ranges and needn't reach their ends.
Inputs may be any that keep to these rules, and one draw needn't show every extreme that they name: `act_out`: the ReLU's output saved by the forward pass, zero where a unit was off.
All inputs are finite; a program needn't handle non-finite values.
Results may differ from the reference program's by a relative error of at most 0.0095.
Values may be sent and summed in bfloat16 or wider, within the bound.
No kernel may reach another device: no remote copies, remote signals or barrier semaphores. Data moves between devices by JAX's collectives and lax.ppermute only.
A program may use at most 64 MiB of HBM per device.

```python
import math
import jax
import jax.numpy as jnp
from jax import lax

C1 = 128
C2 = 256
MZ = 64
MX = 8
MY = 64
NX = 16
NY = 128
NZ = 128


def saved_fields(key):
    noise_key = jax.random.fold_in(key, 11)
    shift_key = jax.random.fold_in(key, 12)
    offset_key = jax.random.fold_in(key, 13)
    scale_key = jax.random.fold_in(key, 14)
    noise_field = jax.random.normal(noise_key, (C2, MX, MY, MZ), jnp.float32)
    shifts = jax.random.uniform(shift_key, (C2, 1, 1, 1), jnp.float32, -0.5, 0.5)
    offsets = jax.random.uniform(offset_key, (C2, 1, 1, 1), jnp.float32, -1.0, 1.0)
    scales = jnp.exp(jax.random.uniform(scale_key, (C2, 1, 1, 1), jnp.float32, math.log(0.5), math.log(5.0)))
    along_x = jnp.arange(MX, dtype=jnp.float32).reshape(1, MX, 1, 1) / (MX - 1)
    along_y = jnp.arange(MY, dtype=jnp.float32).reshape(1, 1, MY, 1) / (MY - 1)
    ramp_field = jnp.exp(math.log(3.0) * (along_x + along_y))
    return (noise_field, shifts, offsets, scales, ramp_field)


def draw_pre_norm(key, part):
    noise_field, shifts, offsets, scales, ramp_field = saved_fields(key)
    values = offsets + scales * ramp_field * noise_field
    return values.reshape(C2, MX, MY * MZ).astype(jnp.bfloat16)


def draw_act_out(key, part):
    noise_field, shifts, offsets, scales, ramp_field = saved_fields(key)
    values = jnp.maximum(noise_field + shifts, 0.0)
    return values.reshape(C2, MX, MY * MZ).astype(jnp.bfloat16)


def draw_out_grad(key, part):
    noise_key = jax.random.fold_in(key, 21)
    means_key = jax.random.fold_in(key, 22)
    noise_field = jax.random.normal(noise_key, (NX, NY, NZ, C1), jnp.float32)
    channel_means = jax.random.uniform(means_key, (1, 1, 1, C1), jnp.float32, -1.0, 1.0)
    along_x = 0.5 + jnp.arange(NX, dtype=jnp.float32).reshape(NX, 1, 1, 1) / (NX - 1)
    along_y = 0.5 + jnp.arange(NY, dtype=jnp.float32).reshape(1, NY, 1, 1) / (NY - 1)
    return (noise_field + channel_means * along_x * along_y).astype(jnp.bfloat16)


def block_scale(own_key, shape, split, least, high):
    def one(position, shards_of):
        steps = jax.random.uniform(jax.random.fold_in(jax.random.fold_in(own_key, 6), position), (shards_of,), jnp.float32, least / len(split), high / len(split))
        return jnp.repeat(jnp.exp(steps), shape[position] // shards_of).reshape((-1,) + (1,) * (len(shape) - position - 1))

    loudness = one(*split[0])
    for cut in split[1:]:
        loudness = loudness * one(*cut)
    return loudness


def gaussian(key, extent, width, reach, shards=(), kind=jnp.bfloat16):
    values = width * jax.random.normal(key, extent, jnp.float32)
    if shards:
        values = values * block_scale(key, extent, shards, -0.22, 0.18)
    return jnp.clip(values, -reach, reach).astype(kind)


def setup_inputs(seed: int = 0) -> dict:
    seeds = jax.random.split(jax.random.key(seed), 8)
    return {
        "fine_input": gaussian(seeds[0], (NX, NY, NZ, C1), 1.0, 6.0, ((0, 8), (1, 4))),
        "out_grad": draw_out_grad(jax.random.fold_in(seeds[7], 71), 0),
        "pre_norm": draw_pre_norm(jax.random.fold_in(seeds[7], 71), 0),
        "act_out": draw_act_out(jax.random.fold_in(seeds[7], 71), 0),
        "norm_gain": jnp.clip(0.5 + 1.5 * jax.random.uniform(seeds[4], (C2,), jnp.float32) ** block_scale(seeds[4], (C2,), ((0, 8),), -0.2, 0.2), 0.5, 2.0),
        "w_down": gaussian(seeds[5], (27, C1, C2), (27 * C1) ** -0.5, 0.109375),
        "w_up": gaussian(seeds[6], (8, C2, C1), C2 ** -0.5, 0.375),
    }


tap_places = ((1, 1), (0, 0), (1, 0))

def reference(fine_input, out_grad, pre_norm, act_out, norm_gain, w_down, w_up):
    cells = MX * MY * MZ
    grad_split = out_grad.reshape(MX, 2, MY, 2, MZ, 2, C1)
    deep_grad = jnp.zeros((cells, C2), jnp.float32)
    for tap_index in range(8):
        pick_x, pick_y, pick_z = (tap_index // 4, tap_index // 2 % 2, tap_index % 2)
        piece = grad_split[:, pick_x, :, pick_y, :, pick_z, :].reshape(cells, C1)
        deep_grad = deep_grad + jnp.dot(piece, w_up[tap_index].T, preferred_element_type=jnp.float32)
    deep_bf = deep_grad.astype(jnp.bfloat16)
    channel_grad = deep_bf.reshape(MX, MY * MZ, C2).transpose(2, 0, 1).astype(jnp.float32)
    values = pre_norm.astype(jnp.float32)
    channel_mean = lax.optimization_barrier(jnp.sum(values, axis=(1, 2))) / cells
    variance = lax.optimization_barrier(jnp.sum(values * values, axis=(1, 2))) / cells - channel_mean * channel_mean
    inv_std = lax.rsqrt(variance + 1e-05)
    normed = (values - channel_mean[:, None, None]) * inv_std[:, None, None]
    masked = jnp.where(act_out > 0, channel_grad, jnp.zeros_like(channel_grad))
    grad_shift = lax.optimization_barrier(jnp.sum(masked, axis=(1, 2))) / cells
    grad_gain = lax.optimization_barrier(jnp.sum(masked * normed, axis=(1, 2))) / cells
    grad_act = ((norm_gain * inv_std)[:, None, None] * (masked - grad_shift[:, None, None] - normed * grad_gain[:, None, None])).astype(jnp.bfloat16)
    extended = jnp.pad(grad_act.reshape(C2, MX, MY, MZ), ((0, 0), (0, 1), (0, 1), (0, 1)))
    fine_split = fine_input.reshape(MX, 2, MY, 2, MZ, 2, C1)
    blocks = {}
    weights = []
    for tap_index in range(27):
        par_x, off_x = tap_places[tap_index // 9]
        par_y, off_y = tap_places[tap_index // 3 % 3]
        par_z, off_z = tap_places[tap_index % 3]
        window = extended[:, off_x:off_x + MX, off_y:off_y + MY, off_z:off_z + MZ].reshape(C2, cells)
        fine_part = fine_split[:, par_x, :, par_y, :, par_z, :].reshape(cells, C1)
        term = jnp.dot(window.T, w_down[tap_index].T, preferred_element_type=jnp.float32)
        parity = (par_x, par_y, par_z)
        if parity in blocks:
            blocks[parity] = blocks[parity] + term
        else:
            blocks[parity] = term
        weights.append(jnp.dot(window, fine_part, preferred_element_type=jnp.float32))
    ordered = [blocks[par_x, par_y, par_z] for par_x in range(2) for par_y in range(2) for par_z in range(2)]
    stacked = jnp.stack(ordered, 0).reshape(2, 2, 2, MX, MY, MZ, C1)
    grad_input = stacked.transpose(3, 0, 4, 1, 5, 2, 6).reshape(2 * MX, 2 * MY, 2 * MZ, C1).astype(jnp.bfloat16)
    grad_down = jnp.stack(weights, 1) * (1.0 / math.sqrt(cells))
    return (grad_input, grad_down, grad_gain, grad_shift)
```

```python
import math

import jax
import jax.numpy as jnp
from jax import lax
from jax.sharding import PartitionSpec as P

tap_places = ((1, 1), (0, 0), (1, 0))


def from_behind(shard, axis, by):
    devices = lax.axis_size(axis)
    pairs = [(i, i + by) for i in range(devices) if 0 <= i + by < devices]
    return lax.ppermute(shard, axis, pairs)


def bit_pairs(slabs, groups, slab_bits, grp_bits):
    return [
        (s * groups + g, (s ^ slab_bits) * groups + (g ^ grp_bits))
        for s in range(slabs)
        for g in range(groups)
    ]


def sum_over_grp(values):
    groups = lax.axis_size("grp")
    parts = {0: values}
    for step in range(1, groups):
        parts[step] = lax.ppermute(values, "grp", [(i, i ^ step) for i in range(groups)])
    width = 1
    while width < groups:
        for step in range(0, groups, 2 * width):
            parts[step] = parts[step] + parts[step + width]
        width *= 2
    return parts[0]


def sum_to_owner(partial):
    slabs = lax.axis_size("slab")
    groups = lax.axis_size("grp")
    slab = lax.axis_index("slab")
    grp = lax.axis_index("grp")
    slab_bits = slabs.bit_length() - 1
    grp_bits = groups.bit_length() - 1
    bits = slab_bits + grp_bits
    place = slab * groups + grp
    columns = partial.shape[1]
    rows = partial.shape[0] // (slabs * groups)
    held = partial.astype(jnp.bfloat16).reshape((2,) * bits + (rows, columns))
    stages = [[0]]
    left = list(range(1, bits))
    while left:
        stages.append(left[:2])
        left = left[2:]

    def pick(array, dims, flips):
        for dim, flip in zip(dims, flips):
            bit = (place >> (bits - 1 - dim)) & 1
            array = lax.dynamic_slice_in_dim(array, bit ^ flip, 1, dim)
        return array

    for stage in stages:
        dims = [bits - 1 - b for b in stage]
        total = pick(held, dims, [0] * len(dims)).astype(jnp.float32)
        for code in range((1 << len(stage)) - 1, 0, -1):
            flips = [code >> n & 1 for n in range(len(stage))]
            mask = sum(f << b for f, b in zip(flips, stage))
            arrived = lax.ppermute(
                pick(held, dims, flips),
                ("slab", "grp"),
                bit_pairs(slabs, groups, mask >> grp_bits, mask & (groups - 1)),
            )
            total = total + arrived.astype(jnp.float32)
        held = total if stage is stages[-1] else total.astype(jnp.bfloat16)
    return held.reshape(rows, columns)


def norm_backward(
    values, grad_vals, saved_act, gain_vals, cell_total, reduce_moments, reduce_terms
):
    moment_one, moment_two = reduce_moments(
        jnp.sum(values, axis=(1, 2)), jnp.sum(values * values, axis=(1, 2))
    )
    channel_mean = moment_one / cell_total
    variance = moment_two / cell_total - channel_mean * channel_mean
    inv_std = lax.rsqrt(variance + 1e-05)
    normed = (values - channel_mean[:, None, None]) * inv_std[:, None, None]
    masked = jnp.where(saved_act > 0, grad_vals, jnp.zeros_like(grad_vals))
    total_one, total_two = reduce_terms(
        jnp.sum(masked, axis=(1, 2)), jnp.sum(masked * normed, axis=(1, 2))
    )
    shift_grad = total_one / cell_total
    gain_grad = total_two / cell_total
    grad_act = (
        (gain_vals * inv_std)[:, None, None]
        * (masked - shift_grad[:, None, None] - normed * gain_grad[:, None, None])
    ).astype(jnp.bfloat16)
    return (grad_act, gain_grad, shift_grad)


def local(fine_input, out_grad, pre_norm, act_out, norm_gain, w_down, w_up):
    fine_planes, fine_rows, fine_depth, width_in = fine_input.shape
    plane_count = fine_planes // 2
    row_count = fine_rows // 2
    depth = fine_depth // 2
    width_deep = w_up.shape[1]
    cell_count = plane_count * row_count * depth
    cell_total = pre_norm.shape[1] * pre_norm.shape[2] * lax.axis_size("grp")
    parity_grad = (
        out_grad.reshape(plane_count, 2, row_count, 2, depth, 2, width_in)
        .transpose(1, 3, 5, 0, 2, 4, 6)
        .reshape(8, cell_count, width_in)
    )
    deep_grad = jnp.einsum("poj,pnj->on", w_up, parity_grad, preferred_element_type=jnp.float32)
    deep_shape = (width_deep, plane_count, row_count * depth)
    deep_bf = deep_grad.astype(jnp.bfloat16).reshape(deep_shape)
    channel_grad = lax.all_to_all(deep_bf, "slab", split_axis=0, concat_axis=1, tiled=True)
    grad_channels, grad_gain, grad_shift = norm_backward(
        pre_norm.astype(jnp.float32),
        channel_grad.astype(jnp.float32),
        act_out,
        norm_gain,
        cell_total,
        lambda first_sum, second_sum: sum_over_grp(jnp.stack((first_sum, second_sum))),
        lambda first_sum, second_sum: sum_over_grp(jnp.stack((first_sum, second_sum))),
    )
    back_first = lax.all_to_all(grad_channels, "slab", split_axis=1, concat_axis=0, tiled=True)
    upper = from_behind(back_first, "slab", -1)
    with_plane = jnp.concatenate([back_first, upper], axis=1)
    row_data = from_behind(with_plane[:, :, :depth], "grp", -1)
    extended = jnp.concatenate([with_plane, row_data], axis=2)
    positions = lax.broadcasted_iota(jnp.int32, (1, 1, extended.shape[2]), 2) % depth
    tail_zero = jnp.zeros((width_deep, plane_count + 1, 1), jnp.bfloat16)
    shifted = jnp.where(
        positions != depth - 1,
        jnp.concatenate([extended[:, :, 1:], tail_zero], axis=2),
        jnp.zeros_like(extended),
    )
    fine_split = fine_input.reshape(plane_count, 2, row_count, 2, depth, 2, width_in)

    def window(sources, offsets):
        off_x, off_y, off_z = offsets
        source = sources[1] if off_z else sources[0]
        start_yz = off_y * depth
        return source[
            :, off_x : off_x + plane_count, start_yz : start_yz + row_count * depth
        ].reshape(source.shape[0], cell_count)

    tap_list = []
    for tap_index in range(27):
        par_x, off_x = tap_places[tap_index // 9]
        par_y, off_y = tap_places[tap_index // 3 % 3]
        par_z, off_z = tap_places[tap_index % 3]
        tap_list.append((tap_index, (par_x, par_y, par_z), (off_x, off_y, off_z)))
    fine_blocks = {}
    for par_x in range(2):
        for par_y in range(2):
            for par_z in range(2):
                fine_blocks[par_x, par_y, par_z] = fine_split[
                    :, par_x, :, par_y, :, par_z, :
                ].reshape(cell_count, width_in)
    blocks = {}
    for tap_index, parity, offsets in tap_list:
        term = jnp.einsum(
            "on,jo->nj",
            window((extended, shifted), offsets),
            w_down[tap_index],
            preferred_element_type=jnp.float32,
        )
        if parity in blocks:
            blocks[parity] = blocks[parity] + term
        else:
            blocks[parity] = term
    ordered = [
        blocks[par_x, par_y, par_z]
        for par_x in range(2)
        for par_y in range(2)
        for par_z in range(2)
    ]
    stacked = jnp.stack(ordered, 0).reshape(2, 2, 2, plane_count, row_count, depth, width_in)
    grad_input = (
        stacked.transpose(3, 0, 4, 1, 5, 2, 6)
        .reshape(fine_planes, fine_rows, fine_depth, width_in)
        .astype(jnp.bfloat16)
    )
    grad_scale = 1.0 / math.sqrt(cell_total)
    pieces = (extended, shifted)
    rows_out = [
        jnp.dot(window(pieces, offsets), fine_blocks[parity], preferred_element_type=jnp.float32)
        for tap_index, parity, offsets in tap_list
    ]
    stacked_rows = jnp.stack(rows_out, 1) * grad_scale
    grad_down = sum_to_owner(stacked_rows.reshape(width_deep, -1)).reshape(-1, 27, width_in)
    return (grad_input, grad_down, grad_gain, grad_shift)


def solution(mesh):
    return jax.shard_map(
        local,
        mesh=mesh,
        in_specs=(
            P("slab", "grp", None, None),
            P("slab", "grp", None, None),
            P("slab", None, "grp"),
            P("slab", None, "grp"),
            P("slab"),
            P(),
            P(),
        ),
        out_specs=(
            P("slab", "grp", None, None),
            P(("slab", "grp"), None, None),
            P("slab"),
            P("slab"),
        ),
        check_vma=False,
    )
```

```python
import functools
import math

import jax
import jax.numpy as jnp
from jax import lax
from jax.experimental import pallas as pl
from jax.experimental.pallas import tpu as pltpu
from jax.sharding import PartitionSpec as P

LANES = 128


def bit_pairs(slabs, groups, slab_bits, grp_bits):
    return [
        (s * groups + g, (s ^ slab_bits) * groups + (g ^ grp_bits))
        for s in range(slabs)
        for g in range(groups)
    ]


def from_next(shard, axis):
    devices = lax.axis_size(axis)
    return lax.ppermute(shard, axis, [(i, i - 1) for i in range(1, devices)])


def sum_over_grp(values):
    groups = lax.axis_size("grp")
    parts = {0: values}
    for step in range(1, groups):
        parts[step] = lax.ppermute(values, "grp", [(i, i ^ step) for i in range(groups)])
    width = 1
    while width < groups:
        for step in range(0, groups, 2 * width):
            parts[step] = parts[step] + parts[step + width]
        width *= 2
    return parts[0]


def sum_to_owner(partial):
    slabs = lax.axis_size("slab")
    groups = lax.axis_size("grp")
    slab = lax.axis_index("slab")
    grp = lax.axis_index("grp")
    slab_bits = slabs.bit_length() - 1
    grp_bits = groups.bit_length() - 1
    bits = slab_bits + grp_bits
    place = slab * groups + grp
    columns = partial.shape[1]
    rows = partial.shape[0] // (slabs * groups)
    held = partial.reshape((2,) * bits + (rows, columns))
    stages = [[0]]
    left = list(range(1, bits))
    while left:
        stages.append(left[:2])
        left = left[2:]

    def pick(array, dims, flips):
        for dim, flip in zip(dims, flips):
            bit = (place >> (bits - 1 - dim)) & 1
            array = lax.dynamic_slice_in_dim(array, bit ^ flip, 1, dim)
        return array

    for stage in stages:
        dims = [bits - 1 - b for b in stage]
        total = pick(held, dims, [0] * len(dims)).astype(jnp.float32)
        for code in range((1 << len(stage)) - 1, 0, -1):
            flips = [code >> n & 1 for n in range(len(stage))]
            mask = sum(f << b for f, b in zip(flips, stage))
            arrived = lax.ppermute(
                pick(held, dims, flips),
                ("slab", "grp"),
                bit_pairs(slabs, groups, mask >> grp_bits, mask & (groups - 1)),
            )
            total = total + arrived.astype(jnp.float32)
        held = total if stage is stages[-1] else total.astype(jnp.bfloat16)
    return held.reshape(rows, columns)


def deep_kernel(rows_ref, taps_ref, out_ref, wide):
    depth = rows_ref.shape[2] // 2
    blocks = []
    for pair in range(rows_ref.shape[1] // 2):
        pieces = []
        for px in range(2):
            for py in range(2):
                wide[...] = rows_ref[px, 2 * pair + py].astype(jnp.float32)
                for pz in range(2):
                    pieces.append(wide[pl.ds(pz, depth, stride=2), :].astype(jnp.bfloat16))
        blocks.append(jnp.concatenate(pieces, axis=1))
    cells = jnp.concatenate(blocks, axis=0)
    taps = jnp.concatenate([taps_ref[p] for p in range(8)], axis=1)
    out_ref[...] = lax.dot_general(
        taps, cells, (((1,), (1,)), ((), ())), preferred_element_type=jnp.float32
    ).astype(jnp.bfloat16)


def deep_gradient(out_grad, w_up):
    _, rows, fine_depth, width_in = out_grad.shape
    width_deep = w_up.shape[1]
    cells = rows * fine_depth // 4
    step = 4
    return pl.pallas_call(
        deep_kernel,
        grid=(rows // (2 * step),),
        in_specs=[
            pl.BlockSpec((2, 2 * step, fine_depth, width_in), lambda i: (0, i, 0, 0)),
            pl.BlockSpec((8, width_deep, width_in), lambda i: (0, 0, 0)),
        ],
        out_specs=pl.BlockSpec((width_deep, step * fine_depth // 2), lambda i: (0, i)),
        out_shape=jax.ShapeDtypeStruct((width_deep, cells), jnp.bfloat16),
        scratch_shapes=[pltpu.VMEM((fine_depth, width_in), jnp.float32)],
        compiler_params=pltpu.CompilerParams(vmem_limit_bytes=32 << 20),
        cost_estimate=pl.CostEstimate(
            flops=2 * 8 * cells * width_deep * width_in,
            bytes_accessed=2 * (out_grad.size + w_up.size + width_deep * cells),
            transcendentals=0,
        ),
        name="deep_gradient",
    )(out_grad, w_up)


def shifted_kernel(fine_ref, out_ref, wide):
    fine_rows, fine_depth, width = fine_ref.shape[1:]
    depth = fine_depth // 2
    cells = fine_rows // 2 * depth
    wide[0:8, :] = jnp.zeros((8, width), jnp.float32)
    out_ref[0, 0:depth, 0 : 3 * width] = jnp.zeros((depth, 3 * width), jnp.bfloat16)
    tail = out_ref.shape[1] - cells
    out_ref[0, cells:, 3 * width :] = jnp.zeros((tail, 6 * width), jnp.bfloat16)
    out_ref[0, cells + depth :, 0 : 3 * width] = jnp.zeros((tail - depth, 3 * width), jnp.bfloat16)

    def row(y, carry):
        start = pl.multiple_of(y * depth, depth)
        for py in range(2):
            wide[8:, :] = fine_ref[0, 2 * y + py].astype(jnp.float32)
            for kz in range(3):
                piece = wide[pl.ds(7 + kz, depth, stride=2), :].astype(jnp.bfloat16)
                if py:
                    out_ref[0, pl.ds(start, depth), (6 + kz) * width : (7 + kz) * width] = piece
                    out_ref[0, pl.ds(start + depth, depth), kz * width : (kz + 1) * width] = piece
                else:
                    out_ref[0, pl.ds(start, depth), (3 + kz) * width : (4 + kz) * width] = piece
        return carry

    lax.fori_loop(0, fine_rows // 2, row, 0)


def shifted_fine(fine_input, padded):
    planes, fine_rows, fine_depth, width = fine_input.shape
    return pl.pallas_call(
        shifted_kernel,
        grid=(planes,),
        in_specs=[pl.BlockSpec((1, fine_rows, fine_depth, width), lambda i: (i, 0, 0, 0))],
        out_specs=pl.BlockSpec((1, padded, 9 * width), lambda i: (i, 0, 0)),
        out_shape=jax.ShapeDtypeStruct((planes, padded, 9 * width), jnp.bfloat16),
        scratch_shapes=[pltpu.VMEM((fine_depth + 8, width), jnp.float32)],
        compiler_params=pltpu.CompilerParams(vmem_limit_bytes=32 << 20),
        cost_estimate=pl.CostEstimate(
            flops=0,
            bytes_accessed=2 * (fine_input.size + planes * padded * 9 * width),
            transcendentals=0,
        ),
        name="shifted_fine",
    )(fine_input)


def input_kernel(here_ref, next_ref, taps_ref, out_ref, turned, product, wide):
    width = taps_ref.shape[1]
    fine_rows, fine_depth = out_ref.shape[1:3]
    depth = fine_depth // 2
    padded = here_ref.shape[1]
    px = pl.program_id(0)
    sides = ((0, here_ref), (1, next_ref))

    @pl.when(px == 0)
    def _():
        for slot, ref in sides:
            for start in range(0, padded, LANES):
                turned[slot, start : start + LANES, :] = ref[:, start : start + LANES].T

    def times(slot, kx, ky):
        taps = jnp.concatenate([taps_ref[9 * kx + 3 * ky + kz] for kz in range(3)], axis=0)
        return lax.dot_general(
            turned[slot],
            taps,
            (((1,), (1,)), ((), ())),
            preferred_element_type=jnp.float32,
        )

    for ky in range(3):
        columns = slice(3 * ky * width, (3 * ky + 3) * width)

        @pl.when(px == 0)
        def _(ky=ky, columns=columns):
            product[:, columns] = times(0, 1, ky)

        @pl.when(px == 1)
        def _(ky=ky, columns=columns):
            product[:, columns] = times(0, 2, ky) + times(1, 0, ky)

    inside = lax.broadcasted_iota(jnp.int32, (depth, width), 0) < depth - 1

    def row(y, carry):
        start = pl.multiple_of(y * depth, depth)

        def part(ky, kz):
            return slice((3 * ky + kz) * width, (3 * ky + kz + 1) * width)

        for py in range(2):
            if py:
                even = product[pl.ds(start, depth), part(2, 1)] + product[
                    pl.ds(start + depth, depth), part(0, 1)
                ]
                odd = product[pl.ds(start, depth), part(2, 2)] + product[
                    pl.ds(start + depth, depth), part(0, 2)
                ]
                after = product[pl.ds(start, depth), part(2, 0)] + product[
                    pl.ds(start + depth, depth), part(0, 0)
                ]
            else:
                even = product[pl.ds(start, depth), part(1, 1)]
                odd = product[pl.ds(start, depth), part(1, 2)]
                after = product[pl.ds(start, depth), part(1, 0)]
            wide[pl.ds(0, depth, stride=2), :] = even
            after = pltpu.roll(after, depth - 1, 0)
            wide[pl.ds(1, depth, stride=2), :] = odd + jnp.where(inside, after, 0.0)
            out_ref[0, 2 * y + py] = wide[...].astype(jnp.bfloat16)
        return carry

    lax.fori_loop(0, fine_rows // 2, row, 0)


def input_gradient(here, after, w_down, fine_shape):
    planes, fine_rows, fine_depth, width = fine_shape
    width_deep, padded = here.shape
    whole = pl.BlockSpec((width_deep, padded), lambda i: (0, 0))
    return pl.pallas_call(
        input_kernel,
        grid=(planes,),
        in_specs=[whole, whole, pl.BlockSpec(w_down.shape, lambda i: (0, 0, 0))],
        out_specs=pl.BlockSpec((1, fine_rows, fine_depth, width), lambda i: (i, 0, 0, 0)),
        out_shape=jax.ShapeDtypeStruct(fine_shape, jnp.bfloat16),
        scratch_shapes=[
            pltpu.VMEM((2, padded, width_deep), jnp.bfloat16),
            pltpu.VMEM((padded, 9 * width), jnp.float32),
            pltpu.VMEM((fine_depth, width), jnp.float32),
        ],
        compiler_params=pltpu.CompilerParams(vmem_limit_bytes=40 << 20),
        cost_estimate=pl.CostEstimate(
            flops=2 * 27 * padded * width_deep * width,
            bytes_accessed=2 * (2 * here.size + w_down.size + math.prod(fine_shape)),
            transcendentals=0,
        ),
        name="input_gradient",
    )(here, after, w_down)


def local(fine_input, out_grad, pre_norm, act_out, norm_gain, w_down, w_up):
    slabs = lax.axis_size("slab")
    groups = lax.axis_size("grp")
    fine_rows, fine_depth, width_in = fine_input.shape[1:]
    depth = fine_depth // 2
    width_deep = w_up.shape[1]
    channels, slab_planes, cells = pre_norm.shape
    cell_total = slab_planes * cells * groups
    padded = -(-(cells + depth) // LANES) * LANES

    deep_bf = deep_gradient(out_grad, w_up).reshape(slabs, channels, cells)
    grad_vals = lax.all_to_all(deep_bf, "slab", split_axis=0, concat_axis=0, tiled=True)

    values = pre_norm.transpose(1, 0, 2)
    saved = act_out.transpose(1, 0, 2)
    edge_values, edge_saved = from_next(jnp.stack((values[:, :, :depth], saved[:, :, :depth])), "grp")
    wide_values = values.astype(jnp.float32)
    moments = sum_over_grp(
        jnp.stack((jnp.sum(wide_values, axis=(0, 2)), jnp.sum(wide_values * wide_values, axis=(0, 2))))
    )
    channel_mean = moments[0] / cell_total
    variance = moments[1] / cell_total - channel_mean * channel_mean
    inv_std = lax.rsqrt(variance + 1e-05)

    def per_channel(array):
        return array[None, :, None]

    def normed_of(array):
        return (array.astype(jnp.float32) - per_channel(channel_mean)) * per_channel(inv_std)

    def masked_of(grads, acts):
        return jnp.where(acts > 0, grads, jnp.zeros_like(grads)).astype(jnp.float32)

    edge_grads = from_next(grad_vals[:, :, :depth], "grp")
    masked = masked_of(grad_vals, saved)
    normed = normed_of(values)
    totals = sum_over_grp(
        jnp.stack((jnp.sum(masked, axis=(0, 2)), jnp.sum(masked * normed, axis=(0, 2))))
    )
    grad_shift = totals[0] / cell_total
    grad_gain = totals[1] / cell_total

    def grad_of(masked, normed):
        return (
            per_channel(norm_gain * inv_std)
            * (masked - per_channel(grad_shift) - normed * per_channel(grad_gain))
        ).astype(jnp.bfloat16)

    edge = grad_of(masked_of(edge_grads, edge_saved), normed_of(edge_values))
    edge = jnp.where(lax.axis_index("grp") < groups - 1, edge, jnp.zeros_like(edge))
    spare = jnp.zeros((slab_planes, channels, padded - cells - depth), jnp.bfloat16)
    act_grads = jnp.concatenate((grad_of(masked, normed), edge, spare), axis=2)
    here = lax.all_to_all(act_grads, "slab", split_axis=0, concat_axis=0, tiled=True)
    here = here.reshape(width_deep, padded)
    after = from_next(here, "slab")

    shifted = shifted_fine(fine_input, padded)
    grad_scale = 1.0 / math.sqrt(cell_total)

    def tap_sums(grads, planes):
        sums = [
            jnp.dot(grads, shifted[plane], preferred_element_type=jnp.float32) for plane in planes
        ]
        return (jnp.concatenate(sums, axis=1) * grad_scale).astype(jnp.bfloat16)

    later_taps = sum_to_owner(tap_sums(here, (0, 1)))
    first_taps = sum_to_owner(tap_sums(after, (1,)))
    grad_down = jnp.concatenate((first_taps, later_taps), axis=1).reshape(-1, 27, width_in)
    grad_input = input_gradient(here, after, w_down, fine_input.shape)
    return (grad_input, grad_down, grad_gain, grad_shift)


def solution(mesh):
    return jax.shard_map(
        local,
        mesh=mesh,
        in_specs=(
            P("slab", "grp", None, None),
            P("slab", "grp", None, None),
            P("slab", None, "grp"),
            P("slab", None, "grp"),
            P("slab"),
            P(),
            P(),
        ),
        out_specs=(
            P("slab", "grp", None, None),
            P(("slab", "grp"), None, None),
            P("slab"),
            P("slab"),
        ),
        check_vma=False,
    )
```

```python
import functools
import math

import jax
import jax.numpy as jnp
from jax import lax
from jax.experimental import pallas as pl
from jax.experimental.pallas import tpu as pltpu
from jax.sharding import PartitionSpec as P

LANES = 128


def bit_pairs(slabs, groups, slab_bits, grp_bits):
    return [
        (s * groups + g, (s ^ slab_bits) * groups + (g ^ grp_bits))
        for s in range(slabs)
        for g in range(groups)
    ]


def from_next(shard, axis):
    devices = lax.axis_size(axis)
    return lax.ppermute(shard, axis, [(i, i - 1) for i in range(1, devices)])


def grp_parts(values):
    groups = lax.axis_size("grp")
    return [values] + [
        lax.ppermute(values, "grp", [(i, i ^ step) for i in range(groups)])
        for step in range(1, groups)
    ]


def pair_sum(parts):
    while len(parts) > 1:
        parts = [first + second for first, second in zip(parts[::2], parts[1::2])]
    return parts[0]


def place_bits():
    return (lax.axis_size("slab") * lax.axis_size("grp")).bit_length() - 1


def split_places(partial):
    bits = place_bits()
    return partial.reshape((2,) * bits + (partial.shape[0] >> bits, partial.shape[1]))


def exchange(held, stage):
    slabs = lax.axis_size("slab")
    groups = lax.axis_size("grp")
    place = lax.axis_index("slab") * groups + lax.axis_index("grp")
    dims = [place_bits() - 1 - b for b in stage]

    def pick(flips):
        array = held
        for dim, bit, flip in zip(dims, stage, flips):
            array = lax.dynamic_slice_in_dim(array, (place >> bit & 1) ^ flip, 1, dim)
        return array

    total = pick([0] * len(dims)).astype(jnp.float32)
    for code in range((1 << len(stage)) - 1, 0, -1):
        flips = [code >> n & 1 for n in range(len(stage))]
        mask = sum(f << b for f, b in zip(flips, stage))
        pairs = bit_pairs(slabs, groups, mask // groups, mask % groups)
        arrived = lax.ppermute(pick(flips), ("slab", "grp"), pairs)
        total = total + arrived.astype(jnp.float32)
    return total.astype(jnp.bfloat16)


def halves(partial, bit):
    place = lax.axis_index("slab") * lax.axis_size("grp") + lax.axis_index("grp")
    held = split_places(partial)
    dim = place_bits() - 1 - bit
    own = place >> bit & 1
    return tuple(lax.dynamic_slice_in_dim(held, own ^ flip, 1, dim) for flip in range(2))


def exchange_halves(kept, sent, bit):
    slabs = lax.axis_size("slab")
    groups = lax.axis_size("grp")
    pairs = bit_pairs(slabs, groups, (1 << bit) // groups, (1 << bit) % groups)
    arrived = lax.ppermute(sent, ("slab", "grp"), pairs)
    return (kept.astype(jnp.float32) + arrived.astype(jnp.float32)).astype(jnp.bfloat16)


def deep_kernel(rows_ref, taps_ref, out_ref, rows, taps, wide, cells, row_sems, tap_sem):
    steps = row_sems.shape[0]
    depth = rows_ref.shape[2] // 2
    width = rows_ref.shape[3]
    step = rows_ref.shape[1] // steps
    count = step // 2 * depth
    taps_copy = pltpu.make_async_copy(taps_ref, taps, tap_sem)
    copies = [
        pltpu.make_async_copy(
            rows_ref.at[:, pl.ds(n * step, step)], rows.at[:, pl.ds(n * step, step)], row_sems.at[n]
        )
        for n in range(steps)
    ]
    copies[0].start()
    taps_copy.start()
    for copy in copies[1:]:
        copy.start()

    def split(n):
        for pair in range(step // 2):
            for px in range(2):
                for py in range(2):
                    tap = 4 * px + 2 * py
                    slot = wide.at[pair * 4 + px * 2 + py]
                    slot[...] = rows[px, n * step + 2 * pair + py].astype(jnp.float32)
                    for pz in range(2):
                        cells[
                            n % 2,
                            pair * depth : (pair + 1) * depth,
                            (tap + pz) * width : (tap + pz + 1) * width,
                        ] = slot[pl.ds(pz, depth, stride=2), :].astype(jnp.bfloat16)

    def multiply(n):
        sums = lax.dot_general(
            jnp.concatenate([taps[p] for p in range(8)], axis=1),
            cells[n % 2],
            (((1,), (1,)), ((), ())),
            preferred_element_type=jnp.float32,
        )
        out_ref[:, n * count : (n + 1) * count] = sums.astype(jnp.bfloat16)

    for n, copy in enumerate(copies):
        copy.wait()
        if n == 1:
            taps_copy.wait()
        if n:
            multiply(n - 1)
        split(n)
    multiply(steps - 1)


def deep_gradient(out_grad, w_up):
    _, rows, fine_depth, width_in = out_grad.shape
    width_deep = w_up.shape[1]
    cells = rows * fine_depth // 4
    steps = rows // 8
    return pl.pallas_call(
        deep_kernel,
        in_specs=[pl.BlockSpec(memory_space=pltpu.HBM)] * 2,
        out_specs=pl.BlockSpec(memory_space=pltpu.VMEM),
        out_shape=jax.ShapeDtypeStruct((width_deep, cells), jnp.bfloat16),
        scratch_shapes=[
            pltpu.VMEM(out_grad.shape, jnp.bfloat16),
            pltpu.VMEM(w_up.shape, jnp.bfloat16),
            pltpu.VMEM((rows // steps * 2, fine_depth, width_in), jnp.float32),
            pltpu.VMEM((2, cells // steps, 8 * width_in), jnp.bfloat16),
            pltpu.SemaphoreType.DMA((steps,)),
            pltpu.SemaphoreType.DMA,
        ],
        compiler_params=pltpu.CompilerParams(vmem_limit_bytes=60 << 20),
        cost_estimate=pl.CostEstimate(
            flops=2 * 8 * cells * width_deep * width_in,
            bytes_accessed=2 * (out_grad.size + w_up.size + width_deep * cells),
            transcendentals=0,
        ),
        name="deep_gradient",
    )(out_grad, w_up)


def shifted_kernel(fine_ref, out_ref, wide):
    planes, fine_rows, fine_depth, width = fine_ref.shape
    depth = fine_depth // 2
    cells = fine_rows // 2 * depth
    zeros = jnp.zeros((depth, out_ref.shape[1]), jnp.bfloat16)
    wide[:, 0:8, :] = jnp.zeros((wide.shape[0], 8, width), jnp.float32)
    out_ref[cells : cells + depth, :] = zeros
    out_ref[2 * cells + depth :, :] = zeros

    def row(y, carry):
        for px in range(planes):
            for py in range(2):
                slot = wide.at[2 * px + py]
                slot[8:, :] = fine_ref[px, 2 * y + py].astype(jnp.float32)
                start = pl.multiple_of(y * depth + py * (cells + depth), depth)
                for kz in range(3):
                    column = (3 * px + kz) * width
                    out_ref[pl.ds(start, depth), column : column + width] = slot[
                        pl.ds(7 + kz, depth, stride=2), :
                    ].astype(jnp.bfloat16)
        return carry

    lax.fori_loop(0, fine_rows // 2, row, 0)


def shifted_fine(fine_input, first):
    planes, fine_rows, fine_depth, width = fine_input.shape
    planes -= first
    depth = fine_depth // 2
    shape = (fine_rows * depth + 2 * depth, planes * 3 * width)
    return pl.pallas_call(
        shifted_kernel,
        grid=(1,),
        in_specs=[
            pl.BlockSpec((planes, fine_rows, fine_depth, width), lambda i: (first // planes, 0, 0, 0))
        ],
        out_specs=pl.BlockSpec(shape, lambda i: (0, 0)),
        out_shape=jax.ShapeDtypeStruct(shape, jnp.bfloat16),
        scratch_shapes=[pltpu.VMEM((2 * planes, fine_depth + 8, width), jnp.float32)],
        compiler_params=pltpu.CompilerParams(vmem_limit_bytes=16 << 20),
        cost_estimate=pl.CostEstimate(flops=0, bytes_accessed=0, transcendentals=0),
        name="shifted_fine",
    )(fine_input)


def tap_kernel(scale, depth, block, own_ref, grads_ref, shifted_ref, kept_ref, sent_ref=None):
    cells = (shifted_ref.shape[0] - 2 * depth) // 2
    width = 3 * LANES
    planes = shifted_ref.shape[1] // width
    own = own_ref[0] > 0
    for ky, start in ((1, 0), (0, cells), (2, cells + depth)):
        count = grads_ref.shape[1] if ky == 0 else cells
        grads = grads_ref[:, :count]
        for px in range(planes):
            sums = scale * jnp.dot(
                grads,
                shifted_ref[start : start + count, px * width : (px + 1) * width],
                preferred_element_type=jnp.float32,
            )
            first = (ky * planes + px) * width
            columns = slice(first, first + width)
            if not block:
                kept_ref[:, columns] = sums.astype(jnp.bfloat16)
                continue
            pairs = sums.reshape(sums.shape[0] // (2 * block), 2, block, width)
            low, high = (pairs[:, n].reshape(sums.shape[0] // 2, width) for n in range(2))
            kept_ref[:, columns] = jnp.where(own, high, low).astype(jnp.bfloat16)
            sent_ref[:, columns] = jnp.where(own, low, high).astype(jnp.bfloat16)


def tap_call(grads, shifted, depth, scale, bit, block):
    width_deep, padded = grads.shape
    columns = 3 * shifted.shape[1]
    place = lax.axis_index("slab") * lax.axis_size("grp") + lax.axis_index("grp")
    outs = 2 if block else 1
    return pl.pallas_call(
        functools.partial(tap_kernel, scale, depth, block),
        in_specs=[pl.BlockSpec(memory_space=pltpu.SMEM)]
        + [pl.BlockSpec(memory_space=pltpu.VMEM)] * 2,
        out_specs=[pl.BlockSpec(memory_space=pltpu.VMEM)] * outs,
        out_shape=[jax.ShapeDtypeStruct((width_deep // outs, columns), jnp.bfloat16)] * outs,
        compiler_params=pltpu.CompilerParams(vmem_limit_bytes=12 << 20),
        cost_estimate=pl.CostEstimate(
            flops=2 * width_deep * padded * columns,
            bytes_accessed=2 * (grads.size + padded * columns + width_deep * columns),
            transcendentals=0,
        ),
        name="tap_sums",
    )((place >> bit & 1).astype(jnp.int32).reshape(1), grads, shifted)


def tap_sums(grads, shifted, depth, scale):
    return tap_call(grads, shifted, depth, scale, 0, 0)[0]


def tap_halves(grads, shifted, depth, scale, bit):
    bits = place_bits()
    rows = grads.shape[0] >> bits
    if (rows << bit) % 8:
        return halves(tap_sums(grads, shifted, depth, scale), bit)
    dims = [2] * bits
    dims[bits - 1 - bit] = 1
    arrays = tap_call(grads, shifted, depth, scale, bit, rows << bit)
    return tuple(array.reshape(*dims, rows, array.shape[1]) for array in arrays)


def input_kernel(taps_of, *refs):
    grads_refs = refs[: len(taps_of)]
    taps_ref = refs[len(taps_of)]
    out_ref, turned, product, wide = refs[-4:]
    width = taps_ref.shape[1]
    fine_rows, fine_depth = out_ref.shape[1:3]
    depth = fine_depth // 2
    padded = turned.shape[1]
    for slot, ref in enumerate(grads_refs):
        for start in range(0, padded, LANES):
            turned[slot, start : start + LANES, :] = ref[:, start : start + LANES].T
    for ky in range(3):
        total = None
        for slot, kx in enumerate(taps_of):
            taps = jnp.concatenate([taps_ref[9 * kx + 3 * ky + kz] for kz in range(3)], axis=0)
            term = lax.dot_general(
                turned[slot],
                taps,
                (((1,), (1,)), ((), ())),
                preferred_element_type=jnp.float32,
            )
            total = term if total is None else total + term
        product[:, 3 * ky * width : (3 * ky + 3) * width] = total
    inside = lax.broadcasted_iota(jnp.int32, (depth, width), 0) < depth - 1

    def row(y, carry):
        start = pl.multiple_of(y * depth, depth)

        def at(ky, kz):
            offset = depth if ky == 0 else 0
            return product[
                pl.ds(start + offset, depth), (3 * ky + kz) * width : (3 * ky + kz + 1) * width
            ]

        for py in range(2):
            terms = (2, 0) if py else (1,)
            even, odd, following = (sum(at(ky, kz) for ky in terms) for kz in (1, 2, 0))
            following = pltpu.roll(following, depth - 1, 0)
            wide[pl.ds(0, depth, stride=2), :] = even
            wide[pl.ds(1, depth, stride=2), :] = odd + jnp.where(inside, following, 0.0)
            out_ref[0, 2 * y + py] = wide[...].astype(jnp.bfloat16)
        return carry

    lax.fori_loop(0, fine_rows // 2, row, 0)


def input_plane(px, grads, taps_of, w_down, fine_shape, earlier=None):
    _, fine_rows, fine_depth, width = fine_shape
    width_deep, padded = grads[0].shape
    operands = list(grads) + [w_down]
    in_specs = [pl.BlockSpec((width_deep, padded), lambda i: (0, 0)) for _ in grads]
    in_specs.append(pl.BlockSpec(w_down.shape, lambda i: (0, 0, 0)))
    aliases = {}
    if earlier is not None:
        aliases = {len(operands): 0}
        operands.append(earlier)
        in_specs.append(pl.BlockSpec(memory_space=pl.ANY))
    return pl.pallas_call(
        functools.partial(input_kernel, taps_of),
        grid=(1,),
        in_specs=in_specs,
        out_specs=pl.BlockSpec((1, fine_rows, fine_depth, width), lambda i: (px, 0, 0, 0)),
        out_shape=jax.ShapeDtypeStruct(fine_shape, jnp.bfloat16),
        input_output_aliases=aliases,
        scratch_shapes=[
            pltpu.VMEM((len(grads), padded, width_deep), jnp.bfloat16),
            pltpu.VMEM((padded, 9 * width), jnp.float32),
            pltpu.VMEM((fine_depth, width), jnp.float32),
        ],
        compiler_params=pltpu.CompilerParams(vmem_limit_bytes=20 << 20),
        cost_estimate=pl.CostEstimate(flops=0, bytes_accessed=0, transcendentals=0),
        name="input_gradient",
    )(*operands)


def mean_and_variance(first_sum, second_sum, count):
    mean = first_sum / count
    return mean, second_sum / count - mean * mean


def own_moments(first_sum, second_sum, count):
    mean, variance = mean_and_variance(first_sum, second_sum, count)
    return mean, lax.rsqrt(jnp.maximum(variance, 0.0) + 1e-05)


def norm_kernel(own_total, cell_total, parts, *refs):
    part_refs, refs = refs[:parts], refs[parts:]
    (gain_ref, edge_ref, values_ref, acts_ref, grads_ref, edge_values_ref, edge_acts_ref, edge_grads_ref) = refs[:8]
    out_ref, totals_ref = refs[8:]
    planes, channels, cells = values_ref.shape
    depth = edge_values_ref.shape[2]

    def columns(array):
        return [array[:, n : n + 1] for n in range(array.shape[1])]

    each = [ref[...] for ref in part_refs]
    sums = columns(pair_sum(each))
    mean, variance = mean_and_variance(sums[0], sums[1], cell_total)
    inv_std = lax.rsqrt(variance + 1e-05)

    def normed_total(part):
        own_mean, own_inv = own_moments(part[0], part[1], own_total)
        return inv_std * (part[3] / own_inv + (own_mean - mean) * part[2])

    shift = sums[2] / cell_total
    slope = pair_sum([normed_total(columns(part)) for part in each]) / cell_total
    totals_ref[:, 0:1] = slope
    totals_ref[:, 1:2] = shift
    gain = gain_ref[...] * inv_std
    edge_gain = gain * edge_ref[0]

    def grad_of(values, acts, grads, gain):
        normed = (values.astype(jnp.float32) - mean) * inv_std
        masked = jnp.where(acts.astype(jnp.float32) > 0, grads.astype(jnp.float32), 0.0)
        return (gain * (masked - shift - normed * slope)).astype(jnp.bfloat16)

    for plane in range(planes):
        out_ref[plane, :, 0:cells] = grad_of(
            values_ref[plane], acts_ref[plane], grads_ref[plane], gain
        )
        edge = grad_of(
            edge_values_ref[plane], edge_acts_ref[plane], edge_grads_ref[plane], edge_gain
        )
        spare = jnp.zeros((channels, out_ref.shape[2] - cells - depth), jnp.bfloat16)
        out_ref[plane, :, cells:] = jnp.concatenate((edge, spare), axis=1)


def local(fine_input, out_grad, pre_norm, act_out, norm_gain, w_down, w_up):
    slabs = lax.axis_size("slab")
    groups = lax.axis_size("grp")
    fine_rows, fine_depth, width_in = fine_input.shape[1:]
    depth = fine_depth // 2
    width_deep = w_up.shape[1]
    channels, slab_planes, cells = pre_norm.shape
    cell_total = slab_planes * cells * groups
    padded = -(-(cells + depth) // LANES) * LANES

    deep_bf = deep_gradient(out_grad, w_up)
    deep_bf, pre_norm, act_out, fine_input = lax.optimization_barrier(
        (deep_bf, pre_norm, act_out, fine_input)
    )
    deep_bf = deep_bf.reshape(slabs, channels, cells)
    grad_vals = lax.all_to_all(deep_bf, "slab", split_axis=0, concat_axis=0, tiled=True)

    values = pre_norm.transpose(1, 0, 2)
    acts = act_out.transpose(1, 0, 2)
    edge_values, edge_acts = from_next(jnp.stack((values[:, :, :depth], acts[:, :, :depth])), "grp")
    edge_grads = from_next(grad_vals[:, :, :depth], "grp")

    wide_values = values.astype(jnp.float32)
    first_sum = jnp.sum(wide_values, axis=(0, 2))
    second_sum = jnp.sum(wide_values * wide_values, axis=(0, 2))

    own_total = slab_planes * cells
    own_mean, own_inv = own_moments(first_sum, second_sum, own_total)
    masked = jnp.where(acts > 0, grad_vals, jnp.zeros_like(grad_vals)).astype(jnp.float32)
    own_normed = (wide_values - own_mean[None, :, None]) * own_inv[None, :, None]
    parts = grp_parts(
        jnp.stack(
            (
                first_sum,
                second_sum,
                jnp.sum(masked, axis=(0, 2)),
                jnp.sum(masked * own_normed, axis=(0, 2)),
            ),
            axis=1,
        )
    )
    inner = (lax.axis_index("grp") < groups - 1).astype(jnp.float32).reshape(1)
    vmem = pl.BlockSpec(memory_space=pltpu.VMEM)
    act_grads, totals = pl.pallas_call(
        functools.partial(norm_kernel, own_total, cell_total, len(parts)),
        in_specs=[vmem] * (len(parts) + 1) + [pl.BlockSpec(memory_space=pltpu.SMEM)] + [vmem] * 6,
        out_specs=[vmem] * 2,
        out_shape=[
            jax.ShapeDtypeStruct((slab_planes, channels, padded), jnp.bfloat16),
            jax.ShapeDtypeStruct((channels, 2), jnp.float32),
        ],
        compiler_params=pltpu.CompilerParams(vmem_limit_bytes=12 << 20),
        cost_estimate=pl.CostEstimate(
            flops=8 * values.size, bytes_accessed=8 * values.size, transcendentals=0
        ),
        name="act_gradient",
    )(*parts, norm_gain[:, None], inner, values, acts, grad_vals, edge_values, edge_acts, edge_grads)
    grad_gain = totals[:, 0]
    grad_shift = totals[:, 1]
    here = lax.all_to_all(act_grads, "slab", split_axis=0, concat_axis=0, tiled=True)
    here = here.reshape(width_deep, padded)
    ready, fine_now = lax.optimization_barrier((here, fine_input))
    shifted = shifted_fine(fine_now, 0)
    grad_scale = 1.0 / math.sqrt(cell_total)
    bits = place_bits()
    stages = [tuple(range(b, min(b + 2, bits))) for b in range(3, bits, 2)]
    later_taps = tap_sums(ready, shifted, depth, grad_scale)
    later_taps, fine_again = lax.optimization_barrier((later_taps, fine_input))
    later_taps = exchange(split_places(later_taps), (0, 1))
    after = from_next(here, "slab")
    shifted = shifted_fine(fine_again, fine_input.shape[0] - 1)
    first_taps = exchange_halves(*tap_halves(after, shifted, depth, grad_scale, 0), 0)
    grad_input = input_plane(0, (here,), (1,), w_down, fine_input.shape)
    first_taps, later_taps, after, grad_input = lax.optimization_barrier(
        (first_taps, later_taps, after, grad_input)
    )
    first_taps = exchange(first_taps, (1, 2))
    later_taps = exchange(later_taps, (2,))
    grad_input = input_plane(1, (here, after), (2, 0), w_down, fine_input.shape, grad_input)
    taps, grad_input = lax.optimization_barrier(
        (jnp.concatenate((first_taps, later_taps), axis=-1), grad_input)
    )
    for stage in stages:
        taps = exchange(taps, stage)
    rows = width_deep >> bits
    taps = taps.reshape(rows, 27, width_in)
    grad_down = jnp.concatenate(
        (taps[:, :9].reshape(rows, 3, 1, 3, width_in), taps[:, 9:].reshape(rows, 3, 2, 3, width_in)),
        axis=2,
    )
    grad_down = (
        grad_down.transpose(0, 2, 1, 3, 4).reshape(rows, 27, width_in).astype(jnp.float32)
    )

    return (grad_input, grad_down, grad_gain, grad_shift)


def solution(mesh):
    return jax.shard_map(
        local,
        mesh=mesh,
        in_specs=(
            P("slab", "grp", None, None),
            P("slab", "grp", None, None),
            P("slab", None, "grp"),
            P("slab", None, "grp"),
            P("slab"),
            P(),
            P(),
        ),
        out_specs=(
            P("slab", "grp", None, None),
            P(("slab", "grp"), None, None),
            P("slab"),
            P("slab"),
        ),
        check_vma=False,
    )
```

```python
import functools
import math

import jax
import jax.numpy as jnp
from jax import lax
from jax.experimental import pallas as pl
from jax.experimental.pallas import tpu as pltpu
from jax.sharding import PartitionSpec as P

LANES = 128


def bit_pairs(slabs, groups, slab_bits, grp_bits):
    return [
        (s * groups + g, (s ^ slab_bits) * groups + (g ^ grp_bits))
        for s in range(slabs)
        for g in range(groups)
    ]


def from_next(shard, axis):
    devices = lax.axis_size(axis)
    return lax.ppermute(shard, axis, [(i, i - 1) for i in range(1, devices)])


def grp_parts(values):
    groups = lax.axis_size("grp")
    return [values] + [
        lax.ppermute(values, "grp", [(i, i ^ step) for i in range(groups)])
        for step in range(1, groups)
    ]


def pair_sum(parts):
    while len(parts) > 1:
        parts = [first + second for first, second in zip(parts[::2], parts[1::2])]
    return parts[0]


def place_bits():
    return (lax.axis_size("slab") * lax.axis_size("grp")).bit_length() - 1


def exchange(held, stage):
    slabs = lax.axis_size("slab")
    groups = lax.axis_size("grp")
    place = lax.axis_index("slab") * groups + lax.axis_index("grp")
    dims = [place_bits() - 1 - b for b in stage]

    def pick(flips):
        array = held
        for dim, bit, flip in zip(dims, stage, flips):
            array = lax.dynamic_slice_in_dim(array, (place >> bit & 1) ^ flip, 1, dim)
        return array

    total = pick([0] * len(dims)).astype(jnp.float32)
    for code in range((1 << len(stage)) - 1, 0, -1):
        flips = [code >> n & 1 for n in range(len(stage))]
        mask = sum(f << b for f, b in zip(flips, stage))
        pairs = bit_pairs(slabs, groups, mask // groups, mask % groups)
        arrived = lax.ppermute(pick(flips), ("slab", "grp"), pairs)
        total = total + arrived.astype(jnp.float32)
    return total.astype(jnp.bfloat16)


def exchange_parts(parts, bits):
    slabs = lax.axis_size("slab")
    groups = lax.axis_size("grp")
    rows = parts[0].shape[0] >> (place_bits() - bits)
    total = parts[0].astype(jnp.float32)
    for mask, part in reversed(list(enumerate(parts[1:], 1))):
        pairs = bit_pairs(slabs, groups, mask // groups, mask % groups)
        total = total + lax.ppermute(part, ("slab", "grp"), pairs).astype(jnp.float32)
    dims = (2,) * (place_bits() - bits) + (1,) * bits
    return total.astype(jnp.bfloat16).reshape(*dims, rows, total.shape[1])


def deep_kernel(rows_ref, taps_ref, out_ref, rows, taps, wide, cells, row_sems, tap_sem):
    steps = row_sems.shape[0]
    depth = rows_ref.shape[2] // 2
    width = rows_ref.shape[3]
    step = rows_ref.shape[1] // steps
    count = step // 2 * depth
    taps_copy = pltpu.make_async_copy(taps_ref, taps, tap_sem)
    copies = [
        pltpu.make_async_copy(
            rows_ref.at[:, pl.ds(n * step, step)], rows.at[:, pl.ds(n * step, step)], row_sems.at[n]
        )
        for n in range(steps)
    ]
    copies[0].start()
    taps_copy.start()
    for copy in copies[1:]:
        copy.start()

    def split(n):
        for pair in range(step // 2):
            for px in range(2):
                for py in range(2):
                    tap = 4 * px + 2 * py
                    slot = wide.at[pair * 4 + px * 2 + py]
                    slot[...] = rows[px, n * step + 2 * pair + py].astype(jnp.float32)
                    for pz in range(2):
                        cells[
                            n % 2,
                            pair * depth : (pair + 1) * depth,
                            (tap + pz) * width : (tap + pz + 1) * width,
                        ] = slot[pl.ds(pz, depth, stride=2), :].astype(jnp.bfloat16)

    def multiply(n):
        sums = lax.dot_general(
            jnp.concatenate([taps[p] for p in range(8)], axis=1),
            cells[n % 2],
            (((1,), (1,)), ((), ())),
            preferred_element_type=jnp.float32,
        )
        out_ref[:, n * count : (n + 1) * count] = sums.astype(jnp.bfloat16)

    for n, copy in enumerate(copies):
        copy.wait()
        if n == 1:
            taps_copy.wait()
        if n:
            multiply(n - 1)
        split(n)
    multiply(steps - 1)


def deep_gradient(out_grad, w_up):
    _, rows, fine_depth, width_in = out_grad.shape
    width_deep = w_up.shape[1]
    cells = rows * fine_depth // 4
    steps = rows // 8
    return pl.pallas_call(
        deep_kernel,
        in_specs=[pl.BlockSpec(memory_space=pltpu.HBM)] * 2,
        out_specs=pl.BlockSpec(memory_space=pltpu.VMEM),
        out_shape=jax.ShapeDtypeStruct((width_deep, cells), jnp.bfloat16),
        scratch_shapes=[
            pltpu.VMEM(out_grad.shape, jnp.bfloat16),
            pltpu.VMEM(w_up.shape, jnp.bfloat16),
            pltpu.VMEM((rows // steps * 2, fine_depth, width_in), jnp.float32),
            pltpu.VMEM((2, cells // steps, 8 * width_in), jnp.bfloat16),
            pltpu.SemaphoreType.DMA((steps,)),
            pltpu.SemaphoreType.DMA,
        ],
        compiler_params=pltpu.CompilerParams(vmem_limit_bytes=60 << 20),
        cost_estimate=pl.CostEstimate(
            flops=2 * 8 * cells * width_deep * width_in,
            bytes_accessed=2 * (out_grad.size + w_up.size + width_deep * cells),
            transcendentals=0,
        ),
        name="deep_gradient",
    )(out_grad, w_up)


def shifted_kernel(fine_ref, out_ref, wide):
    planes, fine_rows, fine_depth, width = fine_ref.shape
    depth = fine_depth // 2
    cells = fine_rows // 2 * depth
    zeros = jnp.zeros((depth, out_ref.shape[1]), jnp.bfloat16)
    wide[:, 0:8, :] = jnp.zeros((wide.shape[0], 8, width), jnp.float32)
    out_ref[cells : cells + depth, :] = zeros
    out_ref[2 * cells + depth :, :] = zeros

    def row(y, carry):
        for px in range(planes):
            for py in range(2):
                slot = wide.at[2 * px + py]
                slot[8:, :] = fine_ref[px, 2 * y + py].astype(jnp.float32)
                start = pl.multiple_of(y * depth + py * (cells + depth), depth)
                for kz in range(3):
                    column = (3 * px + kz) * width
                    out_ref[pl.ds(start, depth), column : column + width] = slot[
                        pl.ds(7 + kz, depth, stride=2), :
                    ].astype(jnp.bfloat16)
        return carry

    lax.fori_loop(0, fine_rows // 2, row, 0)


def shifted_fine(fine_input, first):
    planes, fine_rows, fine_depth, width = fine_input.shape
    planes -= first
    depth = fine_depth // 2
    shape = shifted_shape(fine_input, planes)
    return pl.pallas_call(
        shifted_kernel,
        grid=(1,),
        in_specs=[
            pl.BlockSpec((planes, fine_rows, fine_depth, width), lambda i: (first // planes, 0, 0, 0))
        ],
        out_specs=pl.BlockSpec(shape, lambda i: (0, 0)),
        out_shape=jax.ShapeDtypeStruct(shape, jnp.bfloat16),
        scratch_shapes=[pltpu.VMEM((2 * planes, fine_depth + 8, width), jnp.float32)],
        compiler_params=pltpu.CompilerParams(vmem_limit_bytes=16 << 20),
        cost_estimate=pl.CostEstimate(flops=0, bytes_accessed=0, transcendentals=0),
        name="shifted_fine",
    )(fine_input)


def tap_kernel(scale, depth, rows, jobs, own_ref, grads_ref, shifted_ref, *out_refs):
    cells = (shifted_ref.shape[0] - 2 * depth) // 2
    width = 3 * LANES
    for px, bits in jobs:
        count = 1 << bits if rows else 1
        outs, out_refs = out_refs[:count], out_refs[count:]
        for ky, start in ((1, 0), (0, cells), (2, cells + depth)):
            span = grads_ref.shape[1] if ky == 0 else cells
            sums = scale * jnp.dot(
                grads_ref[:, :span],
                shifted_ref[start : start + span, px * width : (px + 1) * width],
                preferred_element_type=jnp.float32,
            )
            parts = [sums]
            if rows:
                sums = sums.reshape(-1, count, rows, width)
                parts = [sums[:, n].reshape(-1, width) for n in range(count)]
                for bit in range(bits):
                    own = (own_ref[0] >> bit & 1) > 0
                    parts = [
                        jnp.where(own, parts[n ^ (1 << bit)], part) for n, part in enumerate(parts)
                    ]
            for out_ref, part in zip(outs, parts):
                out_ref[:, ky * width : (ky + 1) * width] = part.astype(jnp.bfloat16)


def shift_and_tap_kernel(scale, depth, rows, jobs, own_ref, grads_ref, fine_ref, *refs):
    *out_refs, shifted, wide = refs
    shifted_kernel(fine_ref, shifted, wide)
    tap_kernel(scale, depth, rows, jobs, own_ref, grads_ref, shifted, *out_refs)


def shifted_shape(fine_input, planes):
    _, fine_rows, fine_depth, width = fine_input.shape
    return ((fine_rows + 2) * (fine_depth // 2), planes * 3 * width)


def tap_sums(grads, source, depth, scale, jobs):
    width_deep, padded = grads.shape
    scratch = []
    kernel = tap_kernel
    if source.ndim == 4:
        kernel = shift_and_tap_kernel
        planes, _, fine_depth, width = source.shape
        scratch = [
            pltpu.VMEM(shifted_shape(source, planes), jnp.bfloat16),
            pltpu.VMEM((2 * planes, fine_depth + 8, width), jnp.float32),
        ]
    columns = 9 * LANES
    rows = width_deep >> place_bits()
    place = lax.axis_index("slab") * lax.axis_size("grp") + lax.axis_index("grp")
    inside = rows % 8 == 0
    counts = [1 << bits if inside else 1 for _, bits in jobs]
    outs = [
        jax.ShapeDtypeStruct((width_deep // count, columns), jnp.bfloat16)
        for count in counts
        for _ in range(count)
    ]
    arrays = pl.pallas_call(
        functools.partial(kernel, scale, depth, rows if inside else 0, jobs),
        in_specs=[pl.BlockSpec(memory_space=pltpu.SMEM)]
        + [pl.BlockSpec(memory_space=pltpu.VMEM)] * 2,
        out_specs=[pl.BlockSpec(memory_space=pltpu.VMEM)] * len(outs),
        out_shape=outs,
        scratch_shapes=scratch,
        compiler_params=pltpu.CompilerParams(vmem_limit_bytes=20 << 20),
        cost_estimate=pl.CostEstimate(
            flops=2 * width_deep * padded * columns * len(jobs),
            bytes_accessed=2 * (grads.size + (padded + width_deep) * columns * len(jobs)),
            transcendentals=0,
        ),
        name="tap_sums",
    )(place.astype(jnp.int32).reshape(1), grads, source)
    results = []
    for (_, bits), count in zip(jobs, counts):
        parts, arrays = tuple(arrays[:count]), arrays[count:]
        if not inside:
            held = parts[0].reshape(-1, 1 << bits, rows, columns)
            own = place & ((1 << bits) - 1)
            parts = tuple(
                lax.dynamic_index_in_dim(held, own ^ n, 1, False).reshape(-1, columns)
                for n in range(1 << bits)
            )
        results.append(parts)
    return results


def input_kernel(taps_of, *refs):
    grads_refs = refs[: len(taps_of)]
    taps_ref = refs[len(taps_of)]
    out_ref, turned, product, wide = refs[-4:]
    width = taps_ref.shape[1]
    fine_rows, fine_depth = out_ref.shape[1:3]
    depth = fine_depth // 2
    padded = turned.shape[1]
    for slot, ref in enumerate(grads_refs):
        for start in range(0, padded, LANES):
            turned[slot, start : start + LANES, :] = ref[:, start : start + LANES].T
    for ky in range(3):
        total = None
        for slot, kx in enumerate(taps_of):
            taps = jnp.concatenate([taps_ref[9 * kx + 3 * ky + kz] for kz in range(3)], axis=0)
            term = lax.dot_general(
                turned[slot],
                taps,
                (((1,), (1,)), ((), ())),
                preferred_element_type=jnp.float32,
            )
            total = term if total is None else total + term
        product[:, 3 * ky * width : (3 * ky + 3) * width] = total
    inside = lax.broadcasted_iota(jnp.int32, (depth, width), 0) < depth - 1

    def row(y, carry):
        start = pl.multiple_of(y * depth, depth)

        def at(ky, kz):
            offset = depth if ky == 0 else 0
            return product[
                pl.ds(start + offset, depth), (3 * ky + kz) * width : (3 * ky + kz + 1) * width
            ]

        for py in range(2):
            terms = (2, 0) if py else (1,)
            even, odd, following = (sum(at(ky, kz) for ky in terms) for kz in (1, 2, 0))
            following = pltpu.roll(following, depth - 1, 0)
            wide[pl.ds(0, depth, stride=2), :] = even
            wide[pl.ds(1, depth, stride=2), :] = odd + jnp.where(inside, following, 0.0)
            out_ref[0, 2 * y + py] = wide[...].astype(jnp.bfloat16)
        return carry

    lax.fori_loop(0, fine_rows // 2, row, 0)


def input_plane(px, grads, taps_of, w_down, fine_shape, earlier=None):
    _, fine_rows, fine_depth, width = fine_shape
    width_deep, padded = grads[0].shape
    operands = list(grads) + [w_down]
    in_specs = [pl.BlockSpec((width_deep, padded), lambda i: (0, 0)) for _ in grads]
    in_specs.append(pl.BlockSpec(w_down.shape, lambda i: (0, 0, 0)))
    aliases = {}
    if earlier is not None:
        aliases = {len(operands): 0}
        operands.append(earlier)
        in_specs.append(pl.BlockSpec(memory_space=pl.ANY))
    return pl.pallas_call(
        functools.partial(input_kernel, taps_of),
        grid=(1,),
        in_specs=in_specs,
        out_specs=pl.BlockSpec((1, fine_rows, fine_depth, width), lambda i: (px, 0, 0, 0)),
        out_shape=jax.ShapeDtypeStruct(fine_shape, jnp.bfloat16),
        input_output_aliases=aliases,
        scratch_shapes=[
            pltpu.VMEM((len(grads), padded, width_deep), jnp.bfloat16),
            pltpu.VMEM((padded, 9 * width), jnp.float32),
            pltpu.VMEM((fine_depth, width), jnp.float32),
        ],
        compiler_params=pltpu.CompilerParams(vmem_limit_bytes=20 << 20),
        cost_estimate=pl.CostEstimate(flops=0, bytes_accessed=0, transcendentals=0),
        name="input_gradient",
    )(*operands)


def mean_and_variance(first_sum, second_sum, count):
    mean = first_sum / count
    return mean, second_sum / count - mean * mean


def own_moments(first_sum, second_sum, count):
    mean, variance = mean_and_variance(first_sum, second_sum, count)
    return mean, lax.rsqrt(jnp.maximum(variance, 0.0) + 1e-05)


def norm_kernel(own_total, cell_total, parts, *refs):
    part_refs, refs = refs[:parts], refs[parts:]
    gain_ref, edge_ref, values_ref, masked_ref, edge_values_ref, edge_masked_ref = refs[:6]
    out_ref, totals_ref = refs[6:]
    planes, channels, cells = values_ref.shape
    depth = edge_values_ref.shape[2]

    def columns(array):
        return [array[:, n : n + 1] for n in range(array.shape[1])]

    each = [ref[...] for ref in part_refs]
    sums = columns(pair_sum(each))
    mean, variance = mean_and_variance(sums[0], sums[1], cell_total)
    inv_std = lax.rsqrt(variance + 1e-05)

    def normed_total(part):
        own_mean, own_inv = own_moments(part[0], part[1], own_total)
        return inv_std * (part[3] / own_inv + (own_mean - mean) * part[2])

    shift = sums[2] / cell_total
    slope = pair_sum([normed_total(columns(part)) for part in each]) / cell_total
    totals_ref[:, 0:1] = slope
    totals_ref[:, 1:2] = shift
    gain = gain_ref[...] * inv_std
    edge_gain = gain * edge_ref[0]

    def grad_of(values, masked, gain):
        normed = (values.astype(jnp.float32) - mean) * inv_std
        return (gain * (masked.astype(jnp.float32) - shift - normed * slope)).astype(jnp.bfloat16)

    for plane in range(planes):
        out_ref[plane, :, 0:cells] = grad_of(values_ref[plane], masked_ref[plane], gain)
        edge = grad_of(edge_values_ref[plane], edge_masked_ref[plane], edge_gain)
        spare = jnp.zeros((channels, out_ref.shape[2] - cells - depth), jnp.bfloat16)
        out_ref[plane, :, cells:] = jnp.concatenate((edge, spare), axis=1)


def local(fine_input, out_grad, pre_norm, act_out, norm_gain, w_down, w_up):
    slabs = lax.axis_size("slab")
    groups = lax.axis_size("grp")
    fine_rows, fine_depth, width_in = fine_input.shape[1:]
    depth = fine_depth // 2
    width_deep = w_up.shape[1]
    channels, slab_planes, cells = pre_norm.shape
    cell_total = slab_planes * cells * groups
    padded = -(-(cells + depth) // LANES) * LANES

    deep_bf = deep_gradient(out_grad, w_up)
    deep_bf, pre_norm, act_out, fine_input = lax.optimization_barrier(
        (deep_bf, pre_norm, act_out, fine_input)
    )
    deep_bf = deep_bf.reshape(slabs, channels, cells)
    grad_vals = lax.all_to_all(deep_bf, "slab", split_axis=0, concat_axis=0, tiled=True)

    values = pre_norm.transpose(1, 0, 2)
    acts = act_out.transpose(1, 0, 2)
    values, acts = lax.optimization_barrier((values, acts))
    edge_values, edge_acts = from_next(jnp.stack((values[:, :, :depth], acts[:, :, :depth])), "grp")
    edge_grads = from_next(grad_vals[:, :, :depth], "grp")

    wide_values = values.astype(jnp.float32)
    first_sum = jnp.sum(wide_values, axis=(0, 2))
    second_sum = jnp.sum(wide_values * wide_values, axis=(0, 2))

    own_total = slab_planes * cells
    own_mean, own_inv = own_moments(first_sum, second_sum, own_total)
    def masked_of(grads, acts):
        return jnp.where(acts > 0, grads, jnp.zeros_like(grads))

    masked_bf = masked_of(grad_vals, acts)
    masked = masked_bf.astype(jnp.float32)
    own_normed = (wide_values - own_mean[None, :, None]) * own_inv[None, :, None]
    parts = grp_parts(
        jnp.stack(
            (
                first_sum,
                second_sum,
                jnp.sum(masked, axis=(0, 2)),
                jnp.sum(masked * own_normed, axis=(0, 2)),
            ),
            axis=1,
        )
    )
    inner = (lax.axis_index("grp") < groups - 1).astype(jnp.float32).reshape(1)
    vmem = pl.BlockSpec(memory_space=pltpu.VMEM)
    act_grads, totals = pl.pallas_call(
        functools.partial(norm_kernel, own_total, cell_total, len(parts)),
        in_specs=[vmem] * (len(parts) + 1) + [pl.BlockSpec(memory_space=pltpu.SMEM)] + [vmem] * 4,
        out_specs=[vmem] * 2,
        out_shape=[
            jax.ShapeDtypeStruct((slab_planes, channels, padded), jnp.bfloat16),
            jax.ShapeDtypeStruct((channels, 2), jnp.float32),
        ],
        compiler_params=pltpu.CompilerParams(vmem_limit_bytes=12 << 20),
        cost_estimate=pl.CostEstimate(
            flops=8 * values.size, bytes_accessed=8 * values.size, transcendentals=0
        ),
        name="act_gradient",
    )(*parts, norm_gain[:, None], inner, values, masked_bf, edge_values, masked_of(edge_grads, edge_acts))
    grad_gain = totals[:, 0]
    grad_shift = totals[:, 1]
    here = lax.all_to_all(act_grads, "slab", split_axis=0, concat_axis=0, tiled=True)
    here = here.reshape(width_deep, padded)
    grad_scale = 1.0 / math.sqrt(cell_total)
    bits = place_bits()
    stages = [tuple(range(b, min(b + 2, bits))) for b in range(3, bits, 2)]
    parts = tap_sums(here, fine_input, depth, grad_scale, ((0, 2), (1, 1)))
    parts, here_again = lax.optimization_barrier((parts, here))
    middle_parts, last_parts = parts
    after = from_next(here, "slab")
    grad_input = input_plane(0, (here_again,), (1,), w_down, fine_input.shape)
    grad_input, fine_again = lax.optimization_barrier((grad_input, fine_input))
    shifted = shifted_fine(fine_again, fine_input.shape[0] - 1)
    (parts,) = tap_sums(after, shifted, depth, grad_scale, ((0, 1),))
    kept, last_kept, parts = lax.optimization_barrier((middle_parts[0], last_parts[0], parts))
    middle_taps = exchange_parts((kept, *middle_parts[1:]), 2)
    last_taps = exchange_parts((last_kept, *last_parts[1:]), 1)
    first_taps = exchange_parts(parts, 1)
    first_taps, middle_taps, last_taps, after, grad_input = lax.optimization_barrier(
        (first_taps, middle_taps, last_taps, after, grad_input)
    )
    outer_taps = exchange(jnp.concatenate((first_taps, last_taps), axis=-1), (1, 2))
    middle_taps = exchange(middle_taps, (2,))
    grad_input = input_plane(1, (here, after), (2, 0), w_down, fine_input.shape, grad_input)
    taps, grad_input = lax.optimization_barrier(
        (jnp.concatenate((outer_taps, middle_taps), axis=-1), grad_input)
    )
    for stage in stages:
        taps = exchange(taps, stage)
    rows = width_deep >> bits
    taps = taps.reshape(rows, 27, width_in)
    grad_down = jnp.concatenate((taps[:, :9], taps[:, 18:], taps[:, 9:18]), axis=1).astype(jnp.float32)
    return (grad_input, grad_down, grad_gain, grad_shift)


def solution(mesh):
    return jax.shard_map(
        local,
        mesh=mesh,
        in_specs=(
            P("slab", "grp", None, None),
            P("slab", "grp", None, None),
            P("slab", None, "grp"),
            P("slab", None, "grp"),
            P("slab"),
            P(),
            P(),
        ),
        out_specs=(
            P("slab", "grp", None, None),
            P(("slab", "grp"), None, None),
            P("slab"),
            P("slab"),
        ),
        check_vma=False,
    )
```

```python
import functools
import math

import jax
import jax.numpy as jnp
from jax import lax
from jax.experimental import pallas as pl
from jax.experimental.pallas import tpu as pltpu
from jax.sharding import PartitionSpec as P

LANES = 128


def bit_pairs(slabs, groups, slab_bits, grp_bits):
    return [
        (s * groups + g, (s ^ slab_bits) * groups + (g ^ grp_bits))
        for s in range(slabs)
        for g in range(groups)
    ]


def from_next(shard, axis):
    devices = lax.axis_size(axis)
    return lax.ppermute(shard, axis, [(i, i - 1) for i in range(1, devices)])


def grp_parts(values):
    groups = lax.axis_size("grp")
    return [values] + [
        lax.ppermute(values, "grp", [(i, i ^ step) for i in range(groups)])
        for step in range(1, groups)
    ]


def pair_sum(parts):
    while len(parts) > 1:
        parts = [first + second for first, second in zip(parts[::2], parts[1::2])]
    return parts[0]


def place_bits():
    return (lax.axis_size("slab") * lax.axis_size("grp")).bit_length() - 1


def exchange(held, stage):
    slabs = lax.axis_size("slab")
    groups = lax.axis_size("grp")
    place = lax.axis_index("slab") * groups + lax.axis_index("grp")
    dims = [place_bits() - 1 - b for b in stage]

    def pick(flips):
        array = held
        for dim, bit, flip in zip(dims, stage, flips):
            array = lax.dynamic_slice_in_dim(array, (place >> bit & 1) ^ flip, 1, dim)
        return array

    total = pick([0] * len(dims)).astype(jnp.float32)
    for code in range((1 << len(stage)) - 1, 0, -1):
        flips = [code >> n & 1 for n in range(len(stage))]
        mask = sum(f << b for f, b in zip(flips, stage))
        pairs = bit_pairs(slabs, groups, mask // groups, mask % groups)
        arrived = lax.ppermute(pick(flips), ("slab", "grp"), pairs)
        total = total + arrived.astype(jnp.float32)
    return total.astype(jnp.bfloat16)


def exchange_parts(parts, bits):
    slabs = lax.axis_size("slab")
    groups = lax.axis_size("grp")
    rows = parts[0].shape[0] >> (place_bits() - bits)
    total = parts[0].astype(jnp.float32)
    for mask, part in reversed(list(enumerate(parts[1:], 1))):
        pairs = bit_pairs(slabs, groups, mask // groups, mask % groups)
        total = total + lax.ppermute(part, ("slab", "grp"), pairs).astype(jnp.float32)
    dims = (2,) * (place_bits() - bits) + (1,) * bits
    return total.astype(jnp.bfloat16).reshape(*dims, rows, total.shape[1])


def deep_kernel(rows_ref, taps_ref, out_ref, rows, taps, wide, cells, row_sems, tap_sem):
    steps = row_sems.shape[0]
    depth = rows_ref.shape[2] // 2
    width = rows_ref.shape[3]
    step = rows_ref.shape[1] // steps
    count = step // 2 * depth
    taps_copy = pltpu.make_async_copy(taps_ref, taps, tap_sem)
    copies = [
        pltpu.make_async_copy(
            rows_ref.at[:, pl.ds(n * step, step)], rows.at[:, pl.ds(n * step, step)], row_sems.at[n]
        )
        for n in range(steps)
    ]
    copies[0].start()
    taps_copy.start()
    for copy in copies[1:]:
        copy.start()

    def split(n):
        for pair in range(step // 2):
            for px in range(2):
                for py in range(2):
                    tap = 4 * px + 2 * py
                    slot = wide.at[pair * 4 + px * 2 + py]
                    slot[...] = rows[px, n * step + 2 * pair + py].astype(jnp.float32)
                    for pz in range(2):
                        cells[
                            n % 2,
                            pair * depth : (pair + 1) * depth,
                            (tap + pz) * width : (tap + pz + 1) * width,
                        ] = slot[pl.ds(pz, depth, stride=2), :].astype(jnp.bfloat16)

    def multiply(n):
        sums = lax.dot_general(
            jnp.concatenate([taps[p] for p in range(8)], axis=1),
            cells[n % 2],
            (((1,), (1,)), ((), ())),
            preferred_element_type=jnp.float32,
        )
        out_ref[:, n * count : (n + 1) * count] = sums.astype(jnp.bfloat16)

    for n, copy in enumerate(copies):
        copy.wait()
        if n == 1:
            taps_copy.wait()
        if n:
            multiply(n - 1)
        split(n)
    multiply(steps - 1)


def deep_gradient(out_grad, w_up):
    _, rows, fine_depth, width_in = out_grad.shape
    width_deep = w_up.shape[1]
    cells = rows * fine_depth // 4
    steps = rows // 8
    return pl.pallas_call(
        deep_kernel,
        in_specs=[pl.BlockSpec(memory_space=pltpu.HBM)] * 2,
        out_specs=pl.BlockSpec(memory_space=pltpu.VMEM),
        out_shape=jax.ShapeDtypeStruct((width_deep, cells), jnp.bfloat16),
        scratch_shapes=[
            pltpu.VMEM(out_grad.shape, jnp.bfloat16),
            pltpu.VMEM(w_up.shape, jnp.bfloat16),
            pltpu.VMEM((rows // steps * 2, fine_depth, width_in), jnp.float32),
            pltpu.VMEM((2, cells // steps, 8 * width_in), jnp.bfloat16),
            pltpu.SemaphoreType.DMA((steps,)),
            pltpu.SemaphoreType.DMA,
        ],
        compiler_params=pltpu.CompilerParams(vmem_limit_bytes=60 << 20),
        cost_estimate=pl.CostEstimate(
            flops=2 * 8 * cells * width_deep * width_in,
            bytes_accessed=2 * (out_grad.size + w_up.size + width_deep * cells),
            transcendentals=0,
        ),
        name="deep_gradient",
    )(out_grad, w_up)


def shifted_kernel(fine_ref, out_ref, wide):
    planes, fine_rows, fine_depth, width = fine_ref.shape
    depth = fine_depth // 2
    cells = fine_rows // 2 * depth
    zeros = jnp.zeros((depth, out_ref.shape[1]), jnp.bfloat16)
    wide[:, 0:8, :] = jnp.zeros((wide.shape[0], 8, width), jnp.float32)
    out_ref[cells : cells + depth, :] = zeros
    out_ref[2 * cells + depth :, :] = zeros

    def row(y, carry):
        for px in range(planes):
            for py in range(2):
                slot = wide.at[2 * px + py]
                slot[8:, :] = fine_ref[px, 2 * y + py].astype(jnp.float32)
                start = pl.multiple_of(y * depth + py * (cells + depth), depth)
                for kz in range(3):
                    column = (3 * px + kz) * width
                    out_ref[pl.ds(start, depth), column : column + width] = slot[
                        pl.ds(7 + kz, depth, stride=2), :
                    ].astype(jnp.bfloat16)
        return carry

    lax.fori_loop(0, fine_rows // 2, row, 0)


def shifted_fine(fine_input, first):
    planes, fine_rows, fine_depth, width = fine_input.shape
    planes -= first
    depth = fine_depth // 2
    shape = shifted_shape(fine_input, planes)
    return pl.pallas_call(
        shifted_kernel,
        grid=(1,),
        in_specs=[
            pl.BlockSpec((planes, fine_rows, fine_depth, width), lambda i: (first // planes, 0, 0, 0))
        ],
        out_specs=pl.BlockSpec(shape, lambda i: (0, 0)),
        out_shape=jax.ShapeDtypeStruct(shape, jnp.bfloat16),
        scratch_shapes=[pltpu.VMEM((2 * planes, fine_depth + 8, width), jnp.float32)],
        compiler_params=pltpu.CompilerParams(vmem_limit_bytes=16 << 20),
        cost_estimate=pl.CostEstimate(flops=0, bytes_accessed=0, transcendentals=0),
        name="shifted_fine",
    )(fine_input)


def block_of(ref, block, width_deep):
    if len(ref.shape) == 2:
        return ref[:, block * LANES : (block + 1) * LANES]
    slabs = ref.shape[0]
    channels = width_deep // slabs
    start = block * channels
    if start + channels <= ref.shape[1]:
        return jnp.concatenate([ref[t, start : start + channels, :] for t in range(slabs)], axis=0)
    left = lax.broadcasted_iota(jnp.int32, (channels // 2, LANES), 1) < LANES // 2
    pieces = []
    for t in range(slabs):
        both = ref[t, start:, :].astype(jnp.float32)
        for half in (both, pltpu.roll(both, LANES // 2, 1)):
            pieces.append(jnp.where(left, half, 0.0))
    return jnp.concatenate(pieces, axis=0).astype(jnp.bfloat16)


def tap_kernel(scale, depth, rows, jobs, own_ref, packed_ref, shifted_ref, *refs):
    *out_refs, grads_ref = refs
    for block in range(grads_ref.shape[1] // LANES):
        columns = slice(block * LANES, (block + 1) * LANES)
        grads_ref[:, columns] = block_of(packed_ref, block, grads_ref.shape[0])
    cells = (shifted_ref.shape[0] - 2 * depth) // 2
    width = 3 * LANES
    for px, bits in jobs:
        count = 1 << bits if rows else 1
        outs, out_refs = out_refs[:count], out_refs[count:]
        for ky, start in ((1, 0), (0, cells), (2, cells + depth)):
            span = grads_ref.shape[1] if ky == 0 else cells
            sums = scale * jnp.dot(
                grads_ref[:, :span],
                shifted_ref[start : start + span, px * width : (px + 1) * width],
                preferred_element_type=jnp.float32,
            )
            parts = [sums]
            if rows:
                sums = sums.reshape(-1, count, rows, width)
                parts = [sums[:, n].reshape(-1, width) for n in range(count)]
                for bit in range(bits):
                    own = (own_ref[0] >> bit & 1) > 0
                    parts = [
                        jnp.where(own, parts[n ^ (1 << bit)], part) for n, part in enumerate(parts)
                    ]
            for out_ref, part in zip(outs, parts):
                out_ref[:, ky * width : (ky + 1) * width] = part.astype(jnp.bfloat16)


def shift_and_tap_kernel(scale, depth, rows, jobs, own_ref, grads_ref, fine_ref, *refs):
    *out_refs, shifted, wide, grads = refs
    shifted_kernel(fine_ref, shifted, wide)
    tap_kernel(scale, depth, rows, jobs, own_ref, grads_ref, shifted, *out_refs, grads)


def shifted_shape(fine_input, planes):
    _, fine_rows, fine_depth, width = fine_input.shape
    return ((fine_rows + 2) * (fine_depth // 2), planes * 3 * width)


def tap_sums(grads, source, depth, scale, jobs, shape):
    width_deep, padded = shape
    scratch = []
    kernel = tap_kernel
    if source.ndim == 4:
        kernel = shift_and_tap_kernel
        planes, _, fine_depth, width = source.shape
        scratch = [
            pltpu.VMEM(shifted_shape(source, planes), jnp.bfloat16),
            pltpu.VMEM((2 * planes, fine_depth + 8, width), jnp.float32),
        ]
    columns = 9 * LANES
    rows = width_deep >> place_bits()
    place = lax.axis_index("slab") * lax.axis_size("grp") + lax.axis_index("grp")
    inside = rows % 8 == 0
    counts = [1 << bits if inside else 1 for _, bits in jobs]
    outs = [
        jax.ShapeDtypeStruct((width_deep // count, columns), jnp.bfloat16)
        for count in counts
        for _ in range(count)
    ]
    arrays = pl.pallas_call(
        functools.partial(kernel, scale, depth, rows if inside else 0, jobs),
        in_specs=[pl.BlockSpec(memory_space=pltpu.SMEM)]
        + [pl.BlockSpec(memory_space=pltpu.VMEM)] * 2,
        out_specs=[pl.BlockSpec(memory_space=pltpu.VMEM)] * len(outs),
        out_shape=outs,
        scratch_shapes=[*scratch, pltpu.VMEM(shape, jnp.bfloat16)],
        compiler_params=pltpu.CompilerParams(vmem_limit_bytes=20 << 20),
        cost_estimate=pl.CostEstimate(
            flops=2 * width_deep * padded * columns * len(jobs),
            bytes_accessed=2 * (width_deep * padded + (padded + width_deep) * columns * len(jobs)),
            transcendentals=0,
        ),
        name="tap_sums",
    )(place.astype(jnp.int32).reshape(1), grads, source)
    results = []
    for (_, bits), count in zip(jobs, counts):
        parts, arrays = tuple(arrays[:count]), arrays[count:]
        if not inside:
            held = parts[0].reshape(-1, 1 << bits, rows, columns)
            own = place & ((1 << bits) - 1)
            parts = tuple(
                lax.dynamic_index_in_dim(held, own ^ n, 1, False).reshape(-1, columns)
                for n in range(1 << bits)
            )
        results.append(parts)
    return results


def input_kernel(taps_of, *refs):
    grads_refs = refs[: len(taps_of)]
    taps_ref = refs[len(taps_of)]
    out_ref, turned, product, wide = refs[-4:]
    width = taps_ref.shape[1]
    fine_rows, fine_depth = out_ref.shape[1:3]
    depth = fine_depth // 2
    padded = turned.shape[1]
    for slot, ref in enumerate(grads_refs):
        for block in range(padded // LANES):
            rows = slice(block * LANES, (block + 1) * LANES)
            turned[slot, rows, :] = block_of(ref, block, turned.shape[2]).T
    for ky in range(3):
        total = None
        for slot, kx in enumerate(taps_of):
            taps = jnp.concatenate([taps_ref[9 * kx + 3 * ky + kz] for kz in range(3)], axis=0)
            term = lax.dot_general(
                turned[slot],
                taps,
                (((1,), (1,)), ((), ())),
                preferred_element_type=jnp.float32,
            )
            total = term if total is None else total + term
        product[:, 3 * ky * width : (3 * ky + 3) * width] = total
    inside = lax.broadcasted_iota(jnp.int32, (depth, width), 0) < depth - 1

    def row(y, carry):
        start = pl.multiple_of(y * depth, depth)

        def at(ky, kz):
            offset = depth if ky == 0 else 0
            return product[
                pl.ds(start + offset, depth), (3 * ky + kz) * width : (3 * ky + kz + 1) * width
            ]

        for py in range(2):
            terms = (2, 0) if py else (1,)
            even, odd, following = (sum(at(ky, kz) for ky in terms) for kz in (1, 2, 0))
            following = pltpu.roll(following, depth - 1, 0)
            wide[pl.ds(0, depth, stride=2), :] = even
            wide[pl.ds(1, depth, stride=2), :] = odd + jnp.where(inside, following, 0.0)
            out_ref[0, 2 * y + py] = wide[...].astype(jnp.bfloat16)
        return carry

    lax.fori_loop(0, fine_rows // 2, row, 0)


def input_plane(px, grads, taps_of, w_down, fine_shape, padded, earlier=None):
    _, fine_rows, fine_depth, width = fine_shape
    width_deep = w_down.shape[2]
    operands = list(grads) + [w_down]
    in_specs = [pl.BlockSpec(array.shape, lambda i, n=array.ndim: (0,) * n) for array in grads]
    in_specs.append(pl.BlockSpec(w_down.shape, lambda i: (0, 0, 0)))
    aliases = {}
    if earlier is not None:
        aliases = {len(operands): 0}
        operands.append(earlier)
        in_specs.append(pl.BlockSpec(memory_space=pl.ANY))
    return pl.pallas_call(
        functools.partial(input_kernel, taps_of),
        grid=(1,),
        in_specs=in_specs,
        out_specs=pl.BlockSpec((1, fine_rows, fine_depth, width), lambda i: (px, 0, 0, 0)),
        out_shape=jax.ShapeDtypeStruct(fine_shape, jnp.bfloat16),
        input_output_aliases=aliases,
        scratch_shapes=[
            pltpu.VMEM((len(grads), padded, width_deep), jnp.bfloat16),
            pltpu.VMEM((padded, 9 * width), jnp.float32),
            pltpu.VMEM((fine_depth, width), jnp.float32),
        ],
        compiler_params=pltpu.CompilerParams(vmem_limit_bytes=20 << 20),
        cost_estimate=pl.CostEstimate(flops=0, bytes_accessed=0, transcendentals=0),
        name="input_gradient",
    )(*operands)


def mean_and_variance(first_sum, second_sum, count):
    mean = first_sum / count
    return mean, second_sum / count - mean * mean


def own_moments(first_sum, second_sum, count):
    mean, variance = mean_and_variance(first_sum, second_sum, count)
    return mean, lax.rsqrt(jnp.maximum(variance, 0.0) + 1e-05)


def norm_kernel(own_total, cell_total, parts, *refs):
    part_refs, refs = refs[:parts], refs[parts:]
    gain_ref, take_ref, values_ref, masked_ref, edge_values_ref, edge_acts_ref, *edge_refs = refs[:-2]
    out_ref, totals_ref = refs[-2:]
    planes, channels, cells = values_ref.shape
    depth = edge_values_ref.shape[2]

    def columns(array):
        return [array[:, n : n + 1] for n in range(array.shape[1])]

    each = [ref[...] for ref in part_refs]
    sums = columns(pair_sum(each))
    mean, variance = mean_and_variance(sums[0], sums[1], cell_total)
    inv_std = lax.rsqrt(variance + 1e-05)

    def normed_total(part):
        own_mean, own_inv = own_moments(part[0], part[1], own_total)
        return inv_std * (part[3] / own_inv + (own_mean - mean) * part[2])

    shift = sums[2] / cell_total
    slope = pair_sum([normed_total(columns(part)) for part in each]) / cell_total
    totals_ref[:, 0:1] = slope
    totals_ref[:, 1:2] = shift
    gain = gain_ref[...] * inv_std

    def grad_of(values, masked, gain):
        normed = (values.astype(jnp.float32) - mean) * inv_std
        return gain * (masked.astype(jnp.float32) - shift - normed * slope)

    for plane in range(planes):
        main = grad_of(values_ref[plane], masked_ref[plane], gain).astype(jnp.bfloat16)
        edge_grads = jnp.zeros(edge_values_ref.shape[1:], jnp.float32)
        for n, ref in enumerate(edge_refs):
            edge_grads = jnp.where(take_ref[n] > 0, ref[plane].astype(jnp.float32), edge_grads)
        edge_masked = jnp.where(edge_acts_ref[plane].astype(jnp.float32) > 0, edge_grads, 0.0)
        edge = grad_of(edge_values_ref[plane], edge_masked, gain)
        edge = jnp.where(take_ref[len(edge_refs)] > 0, jnp.zeros_like(edge), edge)
        if out_ref.shape[2] > LANES:
            spare = jnp.zeros((channels, out_ref.shape[2] - cells - depth), jnp.float32)
            out_ref[plane, :, 0:cells] = main
            out_ref[plane, :, cells:] = jnp.concatenate((edge, spare), axis=1).astype(jnp.bfloat16)
            continue
        for block in range(cells // LANES):
            out_ref[plane, block * channels : (block + 1) * channels, :] = main[
                :, block * LANES : (block + 1) * LANES
            ]
        half = channels // 2
        out_ref[plane, cells // LANES * channels :, :] = jnp.concatenate(
            (edge[:half], edge[half:]), axis=1
        ).astype(jnp.bfloat16)


def local(fine_input, out_grad, pre_norm, act_out, norm_gain, w_down, w_up):
    slabs = lax.axis_size("slab")
    groups = lax.axis_size("grp")
    fine_rows, fine_depth, width_in = fine_input.shape[1:]
    depth = fine_depth // 2
    width_deep = w_up.shape[1]
    channels, slab_planes, cells = pre_norm.shape
    cell_total = slab_planes * cells * groups
    padded = -(-(cells + depth) // LANES) * LANES

    deep_bf = deep_gradient(out_grad, w_up)
    deep_bf, pre_norm, act_out, fine_input = lax.optimization_barrier(
        (deep_bf, pre_norm, act_out, fine_input)
    )
    deep_bf = deep_bf.reshape(slabs, channels, cells)
    grad_vals = lax.all_to_all(deep_bf, "slab", split_axis=0, concat_axis=0, tiled=True)

    values = pre_norm.transpose(1, 0, 2)
    acts = act_out.transpose(1, 0, 2)
    values, acts = lax.optimization_barrier((values, acts))
    edge_values, edge_acts = from_next(jnp.stack((values[:, :, :depth], acts[:, :, :depth])), "grp")
    first_row = grad_vals[:, :, :depth]
    masks = [(2 << n) - 1 for n in range(groups.bit_length() - 1)]

    wide_values = values.astype(jnp.float32)
    first_sum = jnp.sum(wide_values, axis=(0, 2))
    second_sum = jnp.sum(wide_values * wide_values, axis=(0, 2))

    own_total = slab_planes * cells
    own_mean, own_inv = own_moments(first_sum, second_sum, own_total)
    masked_bf = jnp.where(acts > 0, grad_vals, jnp.zeros_like(grad_vals))
    masked = masked_bf.astype(jnp.float32)
    own_normed = (wide_values - own_mean[None, :, None]) * own_inv[None, :, None]
    parts = grp_parts(
        jnp.stack(
            (
                first_sum,
                second_sum,
                jnp.sum(masked, axis=(0, 2)),
                jnp.sum(masked * own_normed, axis=(0, 2)),
            ),
            axis=1,
        )
    )
    edge_grads = [
        lax.ppermute(first_row, "grp", [(i, i ^ mask) for i in range(groups)]) for mask in masks
    ]
    grp = lax.axis_index("grp")
    takes = jnp.stack([grp ^ (grp + 1) == mask for mask in masks] + [grp == groups - 1])
    vmem = pl.BlockSpec(memory_space=pltpu.VMEM)
    packed = channels % 32 == 0 and 2 * depth == LANES
    act_shape = (slab_planes, channels, padded)
    if packed:
        act_shape = (slab_planes, channels * cells // LANES + channels // 2, LANES)
    act_grads, totals = pl.pallas_call(
        functools.partial(norm_kernel, own_total, cell_total, len(parts)),
        in_specs=[vmem] * (len(parts) + 1) + [pl.BlockSpec(memory_space=pltpu.SMEM)] + [vmem] * (4 + len(masks)),
        out_specs=[vmem] * 2,
        out_shape=[
            jax.ShapeDtypeStruct(act_shape, jnp.bfloat16),
            jax.ShapeDtypeStruct((channels, 2), jnp.float32),
        ],
        compiler_params=pltpu.CompilerParams(vmem_limit_bytes=12 << 20),
        cost_estimate=pl.CostEstimate(
            flops=8 * values.size, bytes_accessed=8 * values.size, transcendentals=0
        ),
        name="act_gradient",
    )(*parts, norm_gain[:, None], takes.astype(jnp.int32), values, masked_bf, edge_values, edge_acts, *edge_grads)
    grad_gain = totals[:, 0]
    grad_shift = totals[:, 1]
    here = lax.all_to_all(act_grads, "slab", split_axis=0, concat_axis=0, tiled=True)
    if not packed:
        here = here.reshape(width_deep, padded)
    grad_scale = 1.0 / math.sqrt(cell_total)
    bits = place_bits()
    stages = [tuple(range(b, min(b + 2, bits))) for b in range(3, bits, 2)]
    parts = tap_sums(here, fine_input, depth, grad_scale, ((0, 2), (1, 1)), (width_deep, padded))
    parts, here_again = lax.optimization_barrier((parts, here))
    middle_parts, last_parts = parts
    after = from_next(here, "slab")
    grad_input = input_plane(0, (here_again,), (1,), w_down, fine_input.shape, padded)
    grad_input, fine_again = lax.optimization_barrier((grad_input, fine_input))
    shifted = shifted_fine(fine_again, fine_input.shape[0] - 1)
    (parts,) = tap_sums(after, shifted, depth, grad_scale, ((0, 1),), (width_deep, padded))
    kept, last_kept, parts = lax.optimization_barrier((middle_parts[0], last_parts[0], parts))
    middle_taps = exchange_parts((kept, *middle_parts[1:]), 2)
    last_taps = exchange_parts((last_kept, *last_parts[1:]), 1)
    first_taps = exchange_parts(parts, 1)
    first_taps, middle_taps, last_taps, after, grad_input = lax.optimization_barrier(
        (first_taps, middle_taps, last_taps, after, grad_input)
    )
    outer_taps = exchange(jnp.concatenate((first_taps, last_taps), axis=-1), (1, 2))
    middle_taps = exchange(middle_taps, (2,))
    grad_input = input_plane(1, (here, after), (2, 0), w_down, fine_input.shape, padded, grad_input)
    taps, grad_input = lax.optimization_barrier(
        (jnp.concatenate((outer_taps, middle_taps), axis=-1), grad_input)
    )
    for stage in stages:
        taps = exchange(taps, stage)
    rows = width_deep >> bits
    taps = taps.reshape(rows, 27, width_in)
    grad_down = jnp.concatenate((taps[:, :9], taps[:, 18:], taps[:, 9:18]), axis=1).astype(jnp.float32)
    return (grad_input, grad_down, grad_gain, grad_shift)


def solution(mesh):
    return jax.shard_map(
        local,
        mesh=mesh,
        in_specs=(
            P("slab", "grp", None, None),
            P("slab", "grp", None, None),
            P("slab", None, "grp"),
            P("slab", None, "grp"),
            P("slab"),
            P(),
            P(),
        ),
        out_specs=(
            P("slab", "grp", None, None),
            P(("slab", "grp"), None, None),
            P("slab"),
            P("slab"),
        ),
        check_vma=False,
    )
```

```python
import functools
import math

import jax
import jax.numpy as jnp
from jax import lax
from jax.experimental import pallas as pl
from jax.experimental.pallas import tpu as pltpu
from jax.sharding import PartitionSpec as P

LANES = 128


def bit_pairs(slabs, groups, slab_bits, grp_bits):
    return [
        (s * groups + g, (s ^ slab_bits) * groups + (g ^ grp_bits))
        for s in range(slabs)
        for g in range(groups)
    ]


def from_next(shard, axis):
    devices = lax.axis_size(axis)
    return lax.ppermute(shard, axis, [(i, i - 1) for i in range(1, devices)])


def grp_parts(values):
    groups = lax.axis_size("grp")
    return [values] + [
        lax.ppermute(values, "grp", [(i, i ^ step) for i in range(groups)])
        for step in range(1, groups)
    ]


def pair_sum(parts):
    while len(parts) > 1:
        parts = [first + second for first, second in zip(parts[::2], parts[1::2])]
    return parts[0]


def place_bits():
    return (lax.axis_size("slab") * lax.axis_size("grp")).bit_length() - 1


def exchange(held, stage):
    slabs = lax.axis_size("slab")
    groups = lax.axis_size("grp")
    place = lax.axis_index("slab") * groups + lax.axis_index("grp")
    dims = [place_bits() - 1 - b for b in stage]

    def pick(flips):
        array = held
        for dim, bit, flip in zip(dims, stage, flips):
            array = lax.dynamic_slice_in_dim(array, (place >> bit & 1) ^ flip, 1, dim)
        return array

    total = pick([0] * len(dims)).astype(jnp.float32)
    for code in (3, 1, 2) if len(stage) == 2 else (1,):
        flips = [code >> n & 1 for n in range(len(stage))]
        mask = sum(f << b for f, b in zip(flips, stage))
        pairs = bit_pairs(slabs, groups, mask // groups, mask % groups)
        arrived = lax.ppermute(pick(flips), ("slab", "grp"), pairs)
        total = total + arrived.astype(jnp.float32)
    return total.astype(jnp.bfloat16)


def exchange_parts(parts, bits):
    slabs = lax.axis_size("slab")
    groups = lax.axis_size("grp")
    rows = parts[0].shape[0] >> (place_bits() - bits)
    total = parts[0].astype(jnp.float32)
    for mask, part in reversed(list(enumerate(parts[1:], 1))):
        pairs = bit_pairs(slabs, groups, mask // groups, mask % groups)
        total = total + lax.ppermute(part, ("slab", "grp"), pairs).astype(jnp.float32)
    dims = (2,) * (place_bits() - bits) + (1,) * bits
    return total.astype(jnp.bfloat16).reshape(*dims, rows, total.shape[1])


def deep_kernel(rows_ref, taps_ref, out_ref, rows, taps, wide, cells, row_sems, tap_sem):
    steps = row_sems.shape[0]
    depth = rows_ref.shape[2] // 2
    width = rows_ref.shape[3]
    step = rows_ref.shape[1] // steps
    count = step // 2 * depth
    taps_copy = pltpu.make_async_copy(taps_ref, taps, tap_sem)
    copies = [
        pltpu.make_async_copy(
            rows_ref.at[:, pl.ds(n * step, step)], rows.at[:, pl.ds(n * step, step)], row_sems.at[n]
        )
        for n in range(steps)
    ]
    copies[0].start()
    taps_copy.start()
    for copy in copies[1:]:
        copy.start()

    def split(n):
        for pair in range(step // 2):
            for px in range(2):
                for py in range(2):
                    tap = 4 * px + 2 * py
                    slot = wide.at[pair * 4 + px * 2 + py]
                    slot[...] = rows[px, n * step + 2 * pair + py].astype(jnp.float32)
                    for pz in range(2):
                        cells[
                            n % 2,
                            pair * depth : (pair + 1) * depth,
                            (tap + pz) * width : (tap + pz + 1) * width,
                        ] = slot[pl.ds(pz, depth, stride=2), :].astype(jnp.bfloat16)

    def multiply(n):
        sums = lax.dot_general(
            jnp.concatenate([taps[p] for p in range(8)], axis=1),
            cells[n % 2],
            (((1,), (1,)), ((), ())),
            preferred_element_type=jnp.float32,
        )
        out_ref[:, n * count : (n + 1) * count] = sums.astype(jnp.bfloat16)

    for n, copy in enumerate(copies):
        copy.wait()
        if n == 1:
            taps_copy.wait()
        if n:
            multiply(n - 1)
        split(n)
    multiply(steps - 1)


def deep_gradient(out_grad, w_up):
    _, rows, fine_depth, width_in = out_grad.shape
    width_deep = w_up.shape[1]
    cells = rows * fine_depth // 4
    steps = rows // 8
    return pl.pallas_call(
        deep_kernel,
        in_specs=[pl.BlockSpec(memory_space=pltpu.HBM)] * 2,
        out_specs=pl.BlockSpec(memory_space=pltpu.VMEM),
        out_shape=jax.ShapeDtypeStruct((width_deep, cells), jnp.bfloat16),
        scratch_shapes=[
            pltpu.VMEM(out_grad.shape, jnp.bfloat16),
            pltpu.VMEM(w_up.shape, jnp.bfloat16),
            pltpu.VMEM((rows // steps * 2, fine_depth, width_in), jnp.float32),
            pltpu.VMEM((2, cells // steps, 8 * width_in), jnp.bfloat16),
            pltpu.SemaphoreType.DMA((steps,)),
            pltpu.SemaphoreType.DMA,
        ],
        compiler_params=pltpu.CompilerParams(vmem_limit_bytes=60 << 20),
        cost_estimate=pl.CostEstimate(
            flops=2 * 8 * cells * width_deep * width_in,
            bytes_accessed=2 * (out_grad.size + w_up.size + width_deep * cells),
            transcendentals=0,
        ),
        name="deep_gradient",
    )(out_grad, w_up)


def shifted_kernel(fine_ref, out_ref, wide):
    planes, fine_rows, fine_depth, width = fine_ref.shape
    depth = fine_depth // 2
    cells = fine_rows // 2 * depth
    zeros = jnp.zeros((depth, out_ref.shape[1]), jnp.bfloat16)
    wide[:, 0:8, :] = jnp.zeros((wide.shape[0], 8, width), jnp.float32)
    out_ref[cells : cells + depth, :] = zeros
    out_ref[2 * cells + depth :, :] = zeros

    def row(y, carry):
        for px in range(planes):
            for py in range(2):
                slot = wide.at[2 * px + py]
                slot[8:, :] = fine_ref[px, 2 * y + py].astype(jnp.float32)
                start = pl.multiple_of(y * depth + py * (cells + depth), depth)
                for kz in range(3):
                    column = (3 * px + kz) * width
                    out_ref[pl.ds(start, depth), column : column + width] = slot[
                        pl.ds(7 + kz, depth, stride=2), :
                    ].astype(jnp.bfloat16)
        return carry

    lax.fori_loop(0, fine_rows // 2, row, 0)


def shifted_fine(fine_input, first):
    planes, fine_rows, fine_depth, width = fine_input.shape
    planes -= first
    depth = fine_depth // 2
    shape = shifted_shape(fine_input, planes)
    return pl.pallas_call(
        shifted_kernel,
        grid=(1,),
        in_specs=[
            pl.BlockSpec((planes, fine_rows, fine_depth, width), lambda i: (first // planes, 0, 0, 0))
        ],
        out_specs=pl.BlockSpec(shape, lambda i: (0, 0)),
        out_shape=jax.ShapeDtypeStruct(shape, jnp.bfloat16),
        scratch_shapes=[pltpu.VMEM((2 * planes, fine_depth + 8, width), jnp.float32)],
        compiler_params=pltpu.CompilerParams(vmem_limit_bytes=16 << 20),
        cost_estimate=pl.CostEstimate(flops=0, bytes_accessed=0, transcendentals=0),
        name="shifted_fine",
    )(fine_input)


def block_of(ref, block, width_deep):
    if len(ref.shape) == 2:
        return ref[:, block * LANES : (block + 1) * LANES]
    slabs = ref.shape[0]
    channels = width_deep // slabs
    start = block * channels
    if start + channels <= ref.shape[1]:
        return jnp.concatenate([ref[t, start : start + channels, :] for t in range(slabs)], axis=0)
    left = lax.broadcasted_iota(jnp.int32, (channels // 2, LANES), 1) < LANES // 2
    pieces = []
    for t in range(slabs):
        both = ref[t, start:, :].astype(jnp.float32)
        for half in (both, pltpu.roll(both, LANES // 2, 1)):
            pieces.append(jnp.where(left, half, 0.0))
    return jnp.concatenate(pieces, axis=0).astype(jnp.bfloat16)


def tap_kernel(scale, depth, rows, jobs, own_ref, packed_ref, shifted_ref, *refs):
    *out_refs, grads_ref = refs
    for block in range(grads_ref.shape[1] // LANES):
        columns = slice(block * LANES, (block + 1) * LANES)
        grads_ref[:, columns] = block_of(packed_ref, block, grads_ref.shape[0])
    cells = (shifted_ref.shape[0] - 2 * depth) // 2
    width = 3 * LANES
    for px, bits in jobs:
        count = 1 << bits if rows else 1
        outs, out_refs = out_refs[:count], out_refs[count:]
        for ky, start in ((1, 0), (0, cells), (2, cells + depth)):
            span = grads_ref.shape[1] if ky == 0 else cells
            sums = scale * jnp.dot(
                grads_ref[:, :span],
                shifted_ref[start : start + span, px * width : (px + 1) * width],
                preferred_element_type=jnp.float32,
            )
            parts = [sums]
            if rows:
                sums = sums.reshape(-1, count, rows, width)
                parts = [sums[:, n].reshape(-1, width) for n in range(count)]
                for bit in range(bits):
                    own = (own_ref[0] >> bit & 1) > 0
                    parts = [
                        jnp.where(own, parts[n ^ (1 << bit)], part) for n, part in enumerate(parts)
                    ]
            for out_ref, part in zip(outs, parts):
                out_ref[:, ky * width : (ky + 1) * width] = part.astype(jnp.bfloat16)


def shift_and_tap_kernel(scale, depth, rows, jobs, own_ref, grads_ref, fine_ref, *refs):
    *out_refs, shifted, wide, grads = refs
    shifted_kernel(fine_ref, shifted, wide)
    tap_kernel(scale, depth, rows, jobs, own_ref, grads_ref, shifted, *out_refs, grads)


def shifted_shape(fine_input, planes):
    _, fine_rows, fine_depth, width = fine_input.shape
    return ((fine_rows + 2) * (fine_depth // 2), planes * 3 * width)


def tap_sums(grads, source, depth, scale, jobs, shape):
    width_deep, padded = shape
    scratch = []
    kernel = tap_kernel
    if source.ndim == 4:
        kernel = shift_and_tap_kernel
        planes, _, fine_depth, width = source.shape
        scratch = [
            pltpu.VMEM(shifted_shape(source, planes), jnp.bfloat16),
            pltpu.VMEM((2 * planes, fine_depth + 8, width), jnp.float32),
        ]
    columns = 9 * LANES
    rows = width_deep >> place_bits()
    place = lax.axis_index("slab") * lax.axis_size("grp") + lax.axis_index("grp")
    inside = rows % 8 == 0
    counts = [1 << bits if inside else 1 for _, bits in jobs]
    outs = [
        jax.ShapeDtypeStruct((width_deep // count, columns), jnp.bfloat16)
        for count in counts
        for _ in range(count)
    ]
    arrays = pl.pallas_call(
        functools.partial(kernel, scale, depth, rows if inside else 0, jobs),
        in_specs=[pl.BlockSpec(memory_space=pltpu.SMEM)]
        + [pl.BlockSpec(memory_space=pltpu.VMEM)] * 2,
        out_specs=[pl.BlockSpec(memory_space=pltpu.VMEM)] * len(outs),
        out_shape=outs,
        scratch_shapes=[*scratch, pltpu.VMEM(shape, jnp.bfloat16)],
        compiler_params=pltpu.CompilerParams(vmem_limit_bytes=20 << 20),
        cost_estimate=pl.CostEstimate(
            flops=2 * width_deep * padded * columns * len(jobs),
            bytes_accessed=2 * (width_deep * padded + (padded + width_deep) * columns * len(jobs)),
            transcendentals=0,
        ),
        name="tap_sums",
    )(place.astype(jnp.int32).reshape(1), grads, source)
    results = []
    for (_, bits), count in zip(jobs, counts):
        parts, arrays = tuple(arrays[:count]), arrays[count:]
        if not inside:
            held = parts[0].reshape(-1, 1 << bits, rows, columns)
            own = place & ((1 << bits) - 1)
            parts = tuple(
                lax.dynamic_index_in_dim(held, own ^ n, 1, False).reshape(-1, columns)
                for n in range(1 << bits)
            )
        results.append(parts)
    return results


def input_kernel(taps_of, *refs):
    grads_refs = refs[: len(taps_of)]
    taps_ref = refs[len(taps_of)]
    out_ref, turned, product, wide = refs[-4:]
    width = taps_ref.shape[1]
    fine_rows, fine_depth = out_ref.shape[1:3]
    depth = fine_depth // 2
    padded = turned.shape[1]
    for slot, ref in enumerate(grads_refs):
        for block in range(padded // LANES):
            rows = slice(block * LANES, (block + 1) * LANES)
            turned[slot, rows, :] = block_of(ref, block, turned.shape[2]).T
    for ky in range(3):
        total = None
        for slot, kx in enumerate(taps_of):
            taps = jnp.concatenate([taps_ref[9 * kx + 3 * ky + kz] for kz in range(3)], axis=0)
            term = lax.dot_general(
                turned[slot],
                taps,
                (((1,), (1,)), ((), ())),
                preferred_element_type=jnp.float32,
            )
            total = term if total is None else total + term
        product[:, 3 * ky * width : (3 * ky + 3) * width] = total
    inside = lax.broadcasted_iota(jnp.int32, (depth, width), 0) < depth - 1

    def row(y, carry):
        start = pl.multiple_of(y * depth, depth)

        def at(ky, kz):
            offset = depth if ky == 0 else 0
            return product[
                pl.ds(start + offset, depth), (3 * ky + kz) * width : (3 * ky + kz + 1) * width
            ]

        for py in range(2):
            terms = (2, 0) if py else (1,)
            even, odd, following = (sum(at(ky, kz) for ky in terms) for kz in (1, 2, 0))
            following = pltpu.roll(following, depth - 1, 0)
            wide[pl.ds(0, depth, stride=2), :] = even
            wide[pl.ds(1, depth, stride=2), :] = odd + jnp.where(inside, following, 0.0)
            out_ref[0, 2 * y + py] = wide[...].astype(jnp.bfloat16)
        return carry

    lax.fori_loop(0, fine_rows // 2, row, 0)


def input_plane(px, grads, taps_of, w_down, fine_shape, padded, earlier=None):
    _, fine_rows, fine_depth, width = fine_shape
    width_deep = w_down.shape[2]
    operands = list(grads) + [w_down]
    in_specs = [pl.BlockSpec(array.shape, lambda i, n=array.ndim: (0,) * n) for array in grads]
    in_specs.append(pl.BlockSpec(w_down.shape, lambda i: (0, 0, 0)))
    aliases = {}
    if earlier is not None:
        aliases = {len(operands): 0}
        operands.append(earlier)
        in_specs.append(pl.BlockSpec(memory_space=pl.ANY))
    return pl.pallas_call(
        functools.partial(input_kernel, taps_of),
        grid=(1,),
        in_specs=in_specs,
        out_specs=pl.BlockSpec((1, fine_rows, fine_depth, width), lambda i: (px, 0, 0, 0)),
        out_shape=jax.ShapeDtypeStruct(fine_shape, jnp.bfloat16),
        input_output_aliases=aliases,
        scratch_shapes=[
            pltpu.VMEM((len(grads), padded, width_deep), jnp.bfloat16),
            pltpu.VMEM((padded, 9 * width), jnp.float32),
            pltpu.VMEM((fine_depth, width), jnp.float32),
        ],
        compiler_params=pltpu.CompilerParams(vmem_limit_bytes=20 << 20),
        cost_estimate=pl.CostEstimate(flops=0, bytes_accessed=0, transcendentals=0),
        name="input_gradient",
    )(*operands)


def mean_and_variance(first_sum, second_sum, count):
    mean = first_sum / count
    return mean, second_sum / count - mean * mean


def own_moments(first_sum, second_sum, count):
    mean, variance = mean_and_variance(first_sum, second_sum, count)
    return mean, lax.rsqrt(jnp.maximum(variance, 0.0) + 1e-05)


def norm_kernel(own_total, cell_total, parts, direct, *refs):
    part_refs, refs = refs[:parts], refs[parts:]
    gain_ref, inner_ref, slab_ref, values_ref, masked_ref, edge_values_ref, edge_masked_ref = refs[:7]
    *out_refs, totals_ref = refs[7:]
    planes, channels, cells = values_ref.shape
    depth = edge_values_ref.shape[2]

    def columns(array):
        return [array[:, n : n + 1] for n in range(array.shape[1])]

    each = [ref[...] for ref in part_refs]
    sums = columns(pair_sum(each))
    mean, variance = mean_and_variance(sums[0], sums[1], cell_total)
    inv_std = lax.rsqrt(variance + 1e-05)

    def normed_total(part):
        own_mean, own_inv = own_moments(part[0], part[1], own_total)
        return inv_std * (part[3] / own_inv + (own_mean - mean) * part[2])

    shift = sums[2] / cell_total
    slope = pair_sum([normed_total(columns(part)) for part in each]) / cell_total
    totals_ref[:, 0:1] = slope
    totals_ref[:, 1:2] = shift
    gain = gain_ref[...] * inv_std
    edge_gain = gain * inner_ref[0]

    def grad_of(values, masked, gain):
        normed = (values.astype(jnp.float32) - mean) * inv_std
        return gain * (masked.astype(jnp.float32) - shift - normed * slope)

    for n in range(planes):
        plane = n ^ slab_ref[0] if direct else n
        out_ref = out_refs[n] if direct else out_refs[0].at[n]
        main = grad_of(values_ref[plane], masked_ref[plane], gain).astype(jnp.bfloat16)
        edge = grad_of(edge_values_ref[plane], edge_masked_ref[plane], edge_gain)
        if out_ref.shape[1] > LANES:
            spare = jnp.zeros((channels, out_ref.shape[1] - cells - depth), jnp.float32)
            out_ref[:, 0:cells] = main
            out_ref[:, cells:] = jnp.concatenate((edge, spare), axis=1).astype(jnp.bfloat16)
            continue
        for block in range(cells // LANES):
            out_ref[block * channels : (block + 1) * channels, :] = main[
                :, block * LANES : (block + 1) * LANES
            ]
        half = channels // 2
        out_ref[cells // LANES * channels :, :] = jnp.concatenate(
            (edge[:half], edge[half:]), axis=1
        ).astype(jnp.bfloat16)


def place_kernel(slab_ref, *refs):
    *block_refs, out_ref = refs
    for n, block_ref in enumerate(block_refs):
        out_ref[n ^ slab_ref[0]] = block_ref[...]


def local(fine_input, out_grad, pre_norm, act_out, norm_gain, w_down, w_up):
    slabs = lax.axis_size("slab")
    groups = lax.axis_size("grp")
    fine_rows, fine_depth, width_in = fine_input.shape[1:]
    depth = fine_depth // 2
    width_deep = w_up.shape[1]
    channels, slab_planes, cells = pre_norm.shape
    cell_total = slab_planes * cells * groups
    padded = -(-(cells + depth) // LANES) * LANES

    deep_bf = deep_gradient(out_grad, w_up)
    deep_bf, pre_norm, act_out, fine_input = lax.optimization_barrier(
        (deep_bf, pre_norm, act_out, fine_input)
    )
    deep_bf = deep_bf.reshape(slabs, channels, cells)
    grad_vals = lax.all_to_all(deep_bf, "slab", split_axis=0, concat_axis=0, tiled=True)

    values = pre_norm.transpose(1, 0, 2)
    acts = act_out.transpose(1, 0, 2)
    values, acts = lax.optimization_barrier((values, acts))
    edge_values, edge_acts = from_next(jnp.stack((values[:, :, :depth], acts[:, :, :depth])), "grp")
    first_row = grad_vals[:, :, :depth]
    masks = [(2 << n) - 1 for n in range(groups.bit_length() - 1)]

    wide_values = values.astype(jnp.float32)
    first_sum = jnp.sum(wide_values, axis=(0, 2))
    second_sum = jnp.sum(wide_values * wide_values, axis=(0, 2))

    own_total = slab_planes * cells
    own_mean, own_inv = own_moments(first_sum, second_sum, own_total)
    masked_bf = jnp.where(acts > 0, grad_vals, jnp.zeros_like(grad_vals))
    masked = masked_bf.astype(jnp.float32)
    own_normed = (wide_values - own_mean[None, :, None]) * own_inv[None, :, None]
    parts = grp_parts(
        jnp.stack(
            (
                first_sum,
                second_sum,
                jnp.sum(masked, axis=(0, 2)),
                jnp.sum(masked * own_normed, axis=(0, 2)),
            ),
            axis=1,
        )
    )
    edge_grads = [
        lax.ppermute(first_row, "grp", [(i, i ^ mask) for i in range(groups)]) for mask in masks
    ]
    grp = lax.axis_index("grp")
    edge_masked = jnp.zeros_like(first_row)
    for mask, grads in zip(masks, edge_grads):
        edge_masked = jnp.where((grp ^ (grp + 1) == mask) & (edge_acts > 0), grads, edge_masked)
    inner = (grp < groups - 1).astype(jnp.float32).reshape(1)
    vmem = pl.BlockSpec(memory_space=pltpu.VMEM)
    packed = channels % 32 == 0 and 2 * depth == LANES
    act_shape = (slab_planes, channels, padded)
    if packed:
        act_shape = (slab_planes, channels * cells // LANES + channels // 2, LANES)
    direct = packed and slabs <= 8
    blocks = slab_planes if direct else 1
    smem = pl.BlockSpec(memory_space=pltpu.SMEM)
    slab = lax.axis_index("slab").astype(jnp.int32).reshape(1)
    *act_grads, totals = pl.pallas_call(
        functools.partial(norm_kernel, own_total, cell_total, len(parts), direct),
        in_specs=[vmem] * (len(parts) + 1) + [smem] * 2 + [vmem] * 4,
        out_specs=[vmem] * (blocks + 1),
        out_shape=[jax.ShapeDtypeStruct(act_shape[1:] if direct else act_shape, jnp.bfloat16)] * blocks
        + [jax.ShapeDtypeStruct((channels, 2), jnp.float32)],
        compiler_params=pltpu.CompilerParams(vmem_limit_bytes=12 << 20),
        cost_estimate=pl.CostEstimate(
            flops=8 * values.size, bytes_accessed=8 * values.size, transcendentals=0
        ),
        name="act_gradient",
    )(*parts, norm_gain[:, None], inner, slab, values, masked_bf, edge_values, edge_masked)
    grad_gain = totals[:, 0]
    grad_shift = totals[:, 1]
    if direct:
        for mask in sorted(range(1, slabs), key=lambda mask: -(mask >> 1)):
            act_grads[mask] = lax.ppermute(
                act_grads[mask], "slab", [(i, i ^ mask) for i in range(slabs)]
            )
        here = pl.pallas_call(
            place_kernel,
            in_specs=[smem] + [vmem] * slabs,
            out_specs=vmem,
            out_shape=jax.ShapeDtypeStruct(act_shape, jnp.bfloat16),
            compiler_params=pltpu.CompilerParams(vmem_limit_bytes=12 << 20),
            name="place_blocks",
        )(slab, *act_grads)
    else:
        here = lax.all_to_all(act_grads[0], "slab", split_axis=0, concat_axis=0, tiled=True)
    if not packed:
        here = here.reshape(width_deep, padded)
    grad_scale = 1.0 / math.sqrt(cell_total)
    bits = place_bits()
    stages = [tuple(range(b, min(b + 2, bits))) for b in range(3, bits, 2)]
    parts = tap_sums(here, fine_input, depth, grad_scale, ((0, 2), (1, 1)), (width_deep, padded))
    parts, here_again = lax.optimization_barrier((parts, here))
    middle_parts, last_parts = parts
    after = from_next(here, "slab")
    grad_input = input_plane(0, (here_again,), (1,), w_down, fine_input.shape, padded)
    grad_input, fine_again = lax.optimization_barrier((grad_input, fine_input))
    shifted = shifted_fine(fine_again, fine_input.shape[0] - 1)
    (parts,) = tap_sums(after, shifted, depth, grad_scale, ((0, 1),), (width_deep, padded))
    kept, last_kept, parts = lax.optimization_barrier((middle_parts[0], last_parts[0], parts))
    middle_taps = exchange_parts((kept, *middle_parts[1:]), 2)
    last_taps = exchange_parts((last_kept, *last_parts[1:]), 1)
    first_taps = exchange_parts(parts, 1)
    first_taps, middle_taps, last_taps, after, grad_input = lax.optimization_barrier(
        (first_taps, middle_taps, last_taps, after, grad_input)
    )
    outer_taps = exchange(jnp.concatenate((first_taps, last_taps), axis=-1), (1, 2))
    middle_taps = exchange(middle_taps, (2,))
    grad_input = input_plane(1, (here, after), (2, 0), w_down, fine_input.shape, padded, grad_input)
    taps, grad_input = lax.optimization_barrier(
        (jnp.concatenate((outer_taps, middle_taps), axis=-1), grad_input)
    )
    for stage in stages:
        taps = exchange(taps, stage)
    rows = width_deep >> bits
    taps = taps.reshape(rows, 27, width_in)
    grad_down = jnp.concatenate((taps[:, :9], taps[:, 18:], taps[:, 9:18]), axis=1).astype(jnp.float32)
    return (grad_input, grad_down, grad_gain, grad_shift)


def solution(mesh):
    return jax.shard_map(
        local,
        mesh=mesh,
        in_specs=(
            P("slab", "grp", None, None),
            P("slab", "grp", None, None),
            P("slab", None, "grp"),
            P("slab", None, "grp"),
            P("slab"),
            P(),
            P(),
        ),
        out_specs=(
            P("slab", "grp", None, None),
            P(("slab", "grp"), None, None),
            P("slab"),
            P("slab"),
        ),
        check_vma=False,
    )
```

```python
import functools
import math

import jax
import jax.numpy as jnp
from jax import lax
from jax.experimental import pallas as pl
from jax.experimental.pallas import tpu as pltpu
from jax.sharding import PartitionSpec as P

LANES = 128


def bit_pairs(slabs, groups, slab_bits, grp_bits):
    return [
        (s * groups + g, (s ^ slab_bits) * groups + (g ^ grp_bits))
        for s in range(slabs)
        for g in range(groups)
    ]


def from_next(shard, axis):
    devices = lax.axis_size(axis)
    return lax.ppermute(shard, axis, [(i, i - 1) for i in range(1, devices)])


def grp_parts(values):
    groups = lax.axis_size("grp")
    return [values] + [
        lax.ppermute(values, "grp", [(i, i ^ step) for i in range(groups)])
        for step in range(1, groups)
    ]


def pair_sum(parts):
    while len(parts) > 1:
        parts = [first + second for first, second in zip(parts[::2], parts[1::2])]
    return parts[0]


def place_bits():
    return (lax.axis_size("slab") * lax.axis_size("grp")).bit_length() - 1


def exchange(held, stage):
    slabs = lax.axis_size("slab")
    groups = lax.axis_size("grp")
    place = lax.axis_index("slab") * groups + lax.axis_index("grp")
    dims = [place_bits() - 1 - b for b in stage]

    def pick(flips):
        array = held
        for dim, bit, flip in zip(dims, stage, flips):
            array = lax.dynamic_slice_in_dim(array, (place >> bit & 1) ^ flip, 1, dim)
        return array

    total = pick([0] * len(dims)).astype(jnp.float32)
    for code in (3, 1, 2) if len(stage) == 2 else (1,):
        flips = [code >> n & 1 for n in range(len(stage))]
        mask = sum(f << b for f, b in zip(flips, stage))
        pairs = bit_pairs(slabs, groups, mask // groups, mask % groups)
        arrived = lax.ppermute(pick(flips), ("slab", "grp"), pairs)
        total = total + arrived.astype(jnp.float32)
    return total.astype(jnp.bfloat16)


def exchange_parts(parts, bits):
    slabs = lax.axis_size("slab")
    groups = lax.axis_size("grp")
    rows = parts[0].shape[0] >> (place_bits() - bits)
    total = parts[0].astype(jnp.float32)
    for mask, part in reversed(list(enumerate(parts[1:], 1))):
        pairs = bit_pairs(slabs, groups, mask // groups, mask % groups)
        total = total + lax.ppermute(part, ("slab", "grp"), pairs).astype(jnp.float32)
    dims = (2,) * (place_bits() - bits) + (1,) * bits
    return total.astype(jnp.bfloat16).reshape(*dims, rows, total.shape[1])


def deep_kernel(rows_ref, taps_ref, out_ref, rows, taps, wide, cells, row_sems, tap_sem):
    steps = row_sems.shape[0]
    depth = rows_ref.shape[2] // 2
    width = rows_ref.shape[3]
    step = rows_ref.shape[1] // steps
    count = step // 2 * depth
    taps_copy = pltpu.make_async_copy(taps_ref, taps, tap_sem)
    copies = [
        pltpu.make_async_copy(
            rows_ref.at[:, pl.ds(n * step, step)], rows.at[:, pl.ds(n * step, step)], row_sems.at[n]
        )
        for n in range(steps)
    ]
    copies[0].start()
    taps_copy.start()
    for copy in copies[1:]:
        copy.start()

    def split(n):
        for pair in range(step // 2):
            for px in range(2):
                for py in range(2):
                    tap = 4 * px + 2 * py
                    slot = wide.at[pair * 4 + px * 2 + py]
                    slot[...] = rows[px, n * step + 2 * pair + py].astype(jnp.float32)
                    for pz in range(2):
                        cells[
                            n % 2,
                            pair * depth : (pair + 1) * depth,
                            (tap + pz) * width : (tap + pz + 1) * width,
                        ] = slot[pl.ds(pz, depth, stride=2), :].astype(jnp.bfloat16)

    def multiply(n):
        sums = lax.dot_general(
            jnp.concatenate([taps[p] for p in range(8)], axis=1),
            cells[n % 2],
            (((1,), (1,)), ((), ())),
            preferred_element_type=jnp.float32,
        )
        out_ref[:, n * count : (n + 1) * count] = sums.astype(jnp.bfloat16)

    for n, copy in enumerate(copies):
        copy.wait()
        if n == 1:
            taps_copy.wait()
        if n:
            multiply(n - 1)
        split(n)
    multiply(steps - 1)


def deep_gradient(out_grad, w_up):
    _, rows, fine_depth, width_in = out_grad.shape
    width_deep = w_up.shape[1]
    cells = rows * fine_depth // 4
    steps = rows // 16
    return pl.pallas_call(
        deep_kernel,
        in_specs=[pl.BlockSpec(memory_space=pltpu.HBM)] * 2,
        out_specs=pl.BlockSpec(memory_space=pltpu.VMEM),
        out_shape=jax.ShapeDtypeStruct((width_deep, cells), jnp.bfloat16),
        scratch_shapes=[
            pltpu.VMEM(out_grad.shape, jnp.bfloat16),
            pltpu.VMEM(w_up.shape, jnp.bfloat16),
            pltpu.VMEM((rows // steps * 2, fine_depth, width_in), jnp.float32),
            pltpu.VMEM((2, cells // steps, 8 * width_in), jnp.bfloat16),
            pltpu.SemaphoreType.DMA((steps,)),
            pltpu.SemaphoreType.DMA,
        ],
        compiler_params=pltpu.CompilerParams(vmem_limit_bytes=60 << 20),
        cost_estimate=pl.CostEstimate(
            flops=2 * 8 * cells * width_deep * width_in,
            bytes_accessed=2 * (out_grad.size + w_up.size + width_deep * cells),
            transcendentals=0,
        ),
        name="deep_gradient",
    )(out_grad, w_up)


def shifted_kernel(fine_ref, out_ref, wide):
    planes, fine_rows, fine_depth, width = fine_ref.shape
    depth = fine_depth // 2
    cells = fine_rows // 2 * depth
    zeros = jnp.zeros((depth, out_ref.shape[1]), jnp.bfloat16)
    wide[:, 0:8, :] = jnp.zeros((wide.shape[0], 8, width), jnp.float32)
    out_ref[cells : cells + depth, :] = zeros
    out_ref[2 * cells + depth :, :] = zeros

    def row(y, carry):
        for px in range(planes):
            for py in range(2):
                slot = wide.at[2 * px + py]
                slot[8:, :] = fine_ref[px, 2 * y + py].astype(jnp.float32)
                start = pl.multiple_of(y * depth + py * (cells + depth), depth)
                for kz in range(3):
                    column = (3 * px + kz) * width
                    out_ref[pl.ds(start, depth), column : column + width] = slot[
                        pl.ds(7 + kz, depth, stride=2), :
                    ].astype(jnp.bfloat16)
        return carry

    lax.fori_loop(0, fine_rows // 2, row, 0)


def shifted_fine(fine_input, first):
    planes, fine_rows, fine_depth, width = fine_input.shape
    planes -= first
    depth = fine_depth // 2
    shape = shifted_shape(fine_input, planes)
    return pl.pallas_call(
        shifted_kernel,
        grid=(1,),
        in_specs=[
            pl.BlockSpec((planes, fine_rows, fine_depth, width), lambda i: (first // planes, 0, 0, 0))
        ],
        out_specs=pl.BlockSpec(shape, lambda i: (0, 0)),
        out_shape=jax.ShapeDtypeStruct(shape, jnp.bfloat16),
        scratch_shapes=[pltpu.VMEM((2 * planes, fine_depth + 8, width), jnp.float32)],
        compiler_params=pltpu.CompilerParams(vmem_limit_bytes=16 << 20),
        cost_estimate=pl.CostEstimate(flops=0, bytes_accessed=0, transcendentals=0),
        name="shifted_fine",
    )(fine_input)


def block_of(ref, block, width_deep):
    if len(ref.shape) == 2:
        return ref[:, block * LANES : (block + 1) * LANES]
    slabs = ref.shape[0]
    channels = width_deep // slabs
    start = block * channels
    if start + channels <= ref.shape[1]:
        return jnp.concatenate([ref[t, start : start + channels, :] for t in range(slabs)], axis=0)
    left = lax.broadcasted_iota(jnp.int32, (channels // 2, LANES), 1) < LANES // 2
    pieces = []
    for t in range(slabs):
        both = ref[t, start:, :].astype(jnp.float32)
        for half in (both, pltpu.roll(both, LANES // 2, 1)):
            pieces.append(jnp.where(left, half, 0.0))
    return jnp.concatenate(pieces, axis=0).astype(jnp.bfloat16)


def tap_kernel(scale, depth, rows, jobs, own_ref, packed_ref, shifted_ref, *refs):
    *out_refs, grads_ref = refs
    for block in range(grads_ref.shape[1] // LANES):
        columns = slice(block * LANES, (block + 1) * LANES)
        grads_ref[:, columns] = block_of(packed_ref, block, grads_ref.shape[0])
    cells = (shifted_ref.shape[0] - 2 * depth) // 2
    width = 3 * LANES
    starts = (cells, 0, cells + depth)
    for pieces, bits in jobs:
        count = 1 << bits if rows else 1
        outs, out_refs = out_refs[:count], out_refs[count:]
        for place, (px, ky) in enumerate(pieces):
            span = grads_ref.shape[1] if ky == 0 else cells
            sums = scale * jnp.dot(
                grads_ref[:, :span],
                shifted_ref[starts[ky] : starts[ky] + span, px * width : (px + 1) * width],
                preferred_element_type=jnp.float32,
            )
            parts = [sums]
            if rows:
                sums = sums.reshape(-1, count, rows, width)
                parts = [sums[:, n].reshape(-1, width) for n in range(count)]
                for bit in range(bits):
                    own = (own_ref[0] >> bit & 1) > 0
                    parts = [
                        jnp.where(own, parts[n ^ (1 << bit)], part) for n, part in enumerate(parts)
                    ]
            for out_ref, part in zip(outs, parts):
                out_ref[:, place * width : (place + 1) * width] = part.astype(jnp.bfloat16)


def shift_and_tap_kernel(scale, depth, rows, jobs, own_ref, grads_ref, fine_ref, *refs):
    *out_refs, shifted, wide, grads = refs
    shifted_kernel(fine_ref, shifted, wide)
    tap_kernel(scale, depth, rows, jobs, own_ref, grads_ref, shifted, *out_refs, grads)


def shifted_shape(fine_input, planes):
    _, fine_rows, fine_depth, width = fine_input.shape
    return ((fine_rows + 2) * (fine_depth // 2), planes * 3 * width)


def tap_sums(grads, source, depth, scale, jobs, shape):
    width_deep, padded = shape
    scratch = []
    kernel = tap_kernel
    if source.ndim == 4:
        kernel = shift_and_tap_kernel
        planes, _, fine_depth, width = source.shape
        scratch = [
            pltpu.VMEM(shifted_shape(source, planes), jnp.bfloat16),
            pltpu.VMEM((2 * planes, fine_depth + 8, width), jnp.float32),
        ]
    widths = [3 * LANES * len(pieces) for pieces, _ in jobs]
    rows = width_deep >> place_bits()
    place = lax.axis_index("slab") * lax.axis_size("grp") + lax.axis_index("grp")
    inside = rows % 8 == 0
    counts = [1 << bits if inside else 1 for _, bits in jobs]
    outs = [
        jax.ShapeDtypeStruct((width_deep // count, columns), jnp.bfloat16)
        for count, columns in zip(counts, widths)
        for _ in range(count)
    ]
    arrays = pl.pallas_call(
        functools.partial(kernel, scale, depth, rows if inside else 0, jobs),
        in_specs=[pl.BlockSpec(memory_space=pltpu.SMEM)]
        + [pl.BlockSpec(memory_space=pltpu.VMEM)] * 2,
        out_specs=[pl.BlockSpec(memory_space=pltpu.VMEM)] * len(outs),
        out_shape=outs,
        scratch_shapes=[*scratch, pltpu.VMEM(shape, jnp.bfloat16)],
        compiler_params=pltpu.CompilerParams(vmem_limit_bytes=20 << 20),
        cost_estimate=pl.CostEstimate(
            flops=2 * width_deep * padded * sum(widths),
            bytes_accessed=2 * (width_deep * padded + (padded + width_deep) * sum(widths)),
            transcendentals=0,
        ),
        name="tap_sums",
    )(place.astype(jnp.int32).reshape(1), grads, source)
    results = []
    for (_, bits), count, columns in zip(jobs, counts, widths):
        parts, arrays = tuple(arrays[:count]), arrays[count:]
        if not inside:
            held = parts[0].reshape(-1, 1 << bits, rows, columns)
            own = place & ((1 << bits) - 1)
            parts = tuple(
                lax.dynamic_index_in_dim(held, own ^ n, 1, False).reshape(-1, columns)
                for n in range(1 << bits)
            )
        results.append(parts)
    return results


def input_kernel(taps_of, *refs):
    grads_refs = refs[: len(taps_of)]
    taps_ref = refs[len(taps_of)]
    out_ref, turned, product, wide = refs[-4:]
    width = taps_ref.shape[1]
    fine_rows, fine_depth = out_ref.shape[1:3]
    depth = fine_depth // 2
    padded = turned.shape[1]
    for slot, ref in enumerate(grads_refs):
        for block in range(padded // LANES):
            rows = slice(block * LANES, (block + 1) * LANES)
            turned[slot, rows, :] = block_of(ref, block, turned.shape[2]).T
    for ky in range(3):
        total = None
        for slot, kx in enumerate(taps_of):
            taps = jnp.concatenate([taps_ref[9 * kx + 3 * ky + kz] for kz in range(3)], axis=0)
            term = lax.dot_general(
                turned[slot],
                taps,
                (((1,), (1,)), ((), ())),
                preferred_element_type=jnp.float32,
            )
            total = term if total is None else total + term
        product[:, 3 * ky * width : (3 * ky + 3) * width] = total
    inside = lax.broadcasted_iota(jnp.int32, (depth, width), 0) < depth - 1

    def row(y, carry):
        start = pl.multiple_of(y * depth, depth)

        def at(ky, kz):
            offset = depth if ky == 0 else 0
            return product[
                pl.ds(start + offset, depth), (3 * ky + kz) * width : (3 * ky + kz + 1) * width
            ]

        for py in range(2):
            terms = (2, 0) if py else (1,)
            even, odd, following = (sum(at(ky, kz) for ky in terms) for kz in (1, 2, 0))
            following = pltpu.roll(following, depth - 1, 0)
            wide[pl.ds(0, depth, stride=2), :] = even
            wide[pl.ds(1, depth, stride=2), :] = odd + jnp.where(inside, following, 0.0)
            out_ref[0, 2 * y + py] = wide[...].astype(jnp.bfloat16)
        return carry

    lax.fori_loop(0, fine_rows // 2, row, 0)


def input_plane(px, grads, taps_of, w_down, fine_shape, padded, earlier=None):
    _, fine_rows, fine_depth, width = fine_shape
    width_deep = w_down.shape[2]
    operands = list(grads) + [w_down]
    in_specs = [pl.BlockSpec(array.shape, lambda i, n=array.ndim: (0,) * n) for array in grads]
    in_specs.append(pl.BlockSpec(w_down.shape, lambda i: (0, 0, 0)))
    aliases = {}
    if earlier is not None:
        aliases = {len(operands): 0}
        operands.append(earlier)
        in_specs.append(pl.BlockSpec(memory_space=pl.ANY))
    return pl.pallas_call(
        functools.partial(input_kernel, taps_of),
        grid=(1,),
        in_specs=in_specs,
        out_specs=pl.BlockSpec((1, fine_rows, fine_depth, width), lambda i: (px, 0, 0, 0)),
        out_shape=jax.ShapeDtypeStruct(fine_shape, jnp.bfloat16),
        input_output_aliases=aliases,
        scratch_shapes=[
            pltpu.VMEM((len(grads), padded, width_deep), jnp.bfloat16),
            pltpu.VMEM((padded, 9 * width), jnp.float32),
            pltpu.VMEM((fine_depth, width), jnp.float32),
        ],
        compiler_params=pltpu.CompilerParams(vmem_limit_bytes=20 << 20),
        cost_estimate=pl.CostEstimate(flops=0, bytes_accessed=0, transcendentals=0),
        name="input_gradient",
    )(*operands)


def mean_and_variance(first_sum, second_sum, count):
    mean = first_sum / count
    return mean, second_sum / count - mean * mean


def own_moments(first_sum, second_sum, count):
    mean, variance = mean_and_variance(first_sum, second_sum, count)
    return mean, lax.rsqrt(jnp.maximum(variance, 0.0) + 1e-05)


def norm_kernel(own_total, cell_total, parts, direct, *refs):
    part_refs, refs = refs[:parts], refs[parts:]
    gain_ref, inner_ref, slab_ref, values_ref, masked_ref, edge_values_ref, edge_masked_ref = refs[:7]
    *out_refs, totals_ref = refs[7:]
    planes, channels, cells = values_ref.shape
    depth = edge_values_ref.shape[2]

    def columns(array):
        return [array[:, n : n + 1] for n in range(array.shape[1])]

    each = [ref[...] for ref in part_refs]
    sums = columns(pair_sum(each))
    mean, variance = mean_and_variance(sums[0], sums[1], cell_total)
    inv_std = lax.rsqrt(variance + 1e-05)

    def normed_total(part):
        own_mean, own_inv = own_moments(part[0], part[1], own_total)
        return inv_std * (part[3] / own_inv + (own_mean - mean) * part[2])

    shift = sums[2] / cell_total
    slope = pair_sum([normed_total(columns(part)) for part in each]) / cell_total
    totals_ref[:, 0:1] = slope
    totals_ref[:, 1:2] = shift
    gain = gain_ref[...] * inv_std
    edge_gain = gain * inner_ref[0]

    def grad_of(values, masked, gain):
        normed = (values.astype(jnp.float32) - mean) * inv_std
        return gain * (masked.astype(jnp.float32) - shift - normed * slope)

    for n in range(planes):
        plane = n ^ slab_ref[0] if direct else n
        out_ref = out_refs[n] if direct else out_refs[0].at[n]
        main = grad_of(values_ref[plane], masked_ref[plane], gain).astype(jnp.bfloat16)
        edge = grad_of(edge_values_ref[plane], edge_masked_ref[plane], edge_gain)
        if out_ref.shape[1] > LANES:
            spare = jnp.zeros((channels, out_ref.shape[1] - cells - depth), jnp.float32)
            out_ref[:, 0:cells] = main
            out_ref[:, cells:] = jnp.concatenate((edge, spare), axis=1).astype(jnp.bfloat16)
            continue
        for block in range(cells // LANES):
            out_ref[block * channels : (block + 1) * channels, :] = main[
                :, block * LANES : (block + 1) * LANES
            ]
        half = channels // 2
        out_ref[cells // LANES * channels :, :] = jnp.concatenate(
            (edge[:half], edge[half:]), axis=1
        ).astype(jnp.bfloat16)


def place_kernel(slab_ref, *refs):
    *block_refs, out_ref = refs
    for n, block_ref in enumerate(block_refs):
        out_ref[n ^ slab_ref[0]] = block_ref[...]


def local(fine_input, out_grad, pre_norm, act_out, norm_gain, w_down, w_up):
    slabs = lax.axis_size("slab")
    groups = lax.axis_size("grp")
    fine_rows, fine_depth, width_in = fine_input.shape[1:]
    depth = fine_depth // 2
    width_deep = w_up.shape[1]
    channels, slab_planes, cells = pre_norm.shape
    cell_total = slab_planes * cells * groups
    padded = -(-(cells + depth) // LANES) * LANES

    deep_bf = deep_gradient(out_grad, w_up)
    deep_bf, pre_norm, act_out, fine_input = lax.optimization_barrier(
        (deep_bf, pre_norm, act_out, fine_input)
    )
    deep_bf = deep_bf.reshape(slabs, channels, cells)
    grad_vals = lax.all_to_all(deep_bf, "slab", split_axis=0, concat_axis=0, tiled=True)

    values = pre_norm.transpose(1, 0, 2)
    acts = act_out.transpose(1, 0, 2)
    values, acts = lax.optimization_barrier((values, acts))
    edge_values, edge_acts = from_next(jnp.stack((values[:, :, :depth], acts[:, :, :depth])), "grp")
    first_row = grad_vals[:, :, :depth]
    masks = [(2 << n) - 1 for n in range(groups.bit_length() - 1)]

    wide_values = values.astype(jnp.float32)
    first_sum = jnp.sum(wide_values, axis=(0, 2))
    second_sum = jnp.sum(wide_values * wide_values, axis=(0, 2))

    own_total = slab_planes * cells
    own_mean, own_inv = own_moments(first_sum, second_sum, own_total)
    masked_bf = jnp.where(acts > 0, grad_vals, jnp.zeros_like(grad_vals))
    masked = masked_bf.astype(jnp.float32)
    own_normed = (wide_values - own_mean[None, :, None]) * own_inv[None, :, None]
    parts = grp_parts(
        jnp.stack(
            (
                first_sum,
                second_sum,
                jnp.sum(masked, axis=(0, 2)),
                jnp.sum(masked * own_normed, axis=(0, 2)),
            ),
            axis=1,
        )
    )
    edge_grads = [
        lax.ppermute(first_row, "grp", [(i, i ^ mask) for i in range(groups)]) for mask in masks
    ]
    grp = lax.axis_index("grp")
    edge_masked = jnp.zeros_like(first_row)
    for mask, grads in zip(masks, edge_grads):
        edge_masked = jnp.where((grp ^ (grp + 1) == mask) & (edge_acts > 0), grads, edge_masked)
    inner = (grp < groups - 1).astype(jnp.float32).reshape(1)
    vmem = pl.BlockSpec(memory_space=pltpu.VMEM)
    packed = channels % 32 == 0 and 2 * depth == LANES
    act_shape = (slab_planes, channels, padded)
    if packed:
        act_shape = (slab_planes, channels * cells // LANES + channels // 2, LANES)
    direct = packed and slabs <= 8
    blocks = slab_planes if direct else 1
    smem = pl.BlockSpec(memory_space=pltpu.SMEM)
    slab = lax.axis_index("slab").astype(jnp.int32).reshape(1)
    *act_grads, totals = pl.pallas_call(
        functools.partial(norm_kernel, own_total, cell_total, len(parts), direct),
        in_specs=[vmem] * (len(parts) + 1) + [smem] * 2 + [vmem] * 4,
        out_specs=[vmem] * (blocks + 1),
        out_shape=[jax.ShapeDtypeStruct(act_shape[1:] if direct else act_shape, jnp.bfloat16)] * blocks
        + [jax.ShapeDtypeStruct((channels, 2), jnp.float32)],
        compiler_params=pltpu.CompilerParams(vmem_limit_bytes=12 << 20),
        cost_estimate=pl.CostEstimate(
            flops=8 * values.size, bytes_accessed=8 * values.size, transcendentals=0
        ),
        name="act_gradient",
    )(*parts, norm_gain[:, None], inner, slab, values, masked_bf, edge_values, edge_masked)
    grad_gain = totals[:, 0]
    grad_shift = totals[:, 1]
    if direct:
        for mask in sorted(range(1, slabs), key=lambda mask: -(mask >> 1)):
            act_grads[mask] = lax.ppermute(
                act_grads[mask], "slab", [(i, i ^ mask) for i in range(slabs)]
            )
        here = pl.pallas_call(
            place_kernel,
            in_specs=[smem] + [vmem] * slabs,
            out_specs=vmem,
            out_shape=jax.ShapeDtypeStruct(act_shape, jnp.bfloat16),
            compiler_params=pltpu.CompilerParams(vmem_limit_bytes=12 << 20),
            name="place_blocks",
        )(slab, *act_grads)
    else:
        here = lax.all_to_all(act_grads[0], "slab", split_axis=0, concat_axis=0, tiled=True)
    if not packed:
        here = here.reshape(width_deep, padded)
    grad_scale = 1.0 / math.sqrt(cell_total)
    bits = place_bits()
    stages = [tuple(range(b, min(b + 2, bits))) for b in range(3, bits, 2)]
    row = tuple((0, ky) for ky in range(3))
    jobs = ((tuple((1, ky) for ky in range(3)), 1), (row, 2))
    parts = tap_sums(here, fine_input, depth, grad_scale, jobs, (width_deep, padded))
    parts, here_again = lax.optimization_barrier((parts, here))
    last_parts, middle_parts = parts
    after = from_next(here, "slab")
    grad_input = input_plane(0, (here_again,), (1,), w_down, fine_input.shape, padded)
    grad_input, fine_again = lax.optimization_barrier((grad_input, fine_input))
    shifted = shifted_fine(fine_again, fine_input.shape[0] - 1)
    (parts,) = tap_sums(after, shifted, depth, grad_scale, ((row, 1),), (width_deep, padded))
    kept, last_kept, parts = lax.optimization_barrier((middle_parts[0], last_parts[0], parts))
    middle_taps = exchange_parts((kept, *middle_parts[1:]), 2)
    last_taps = exchange_parts((last_kept, *last_parts[1:]), 1)
    first_taps = exchange_parts(parts, 1)
    first_taps, middle_taps, last_taps, after, grad_input = lax.optimization_barrier(
        (first_taps, middle_taps, last_taps, after, grad_input)
    )
    outer_taps = exchange(jnp.concatenate((first_taps, last_taps), axis=-1), (1, 2))
    middle_taps = exchange(middle_taps, (2,))
    grad_input = input_plane(1, (here, after), (2, 0), w_down, fine_input.shape, padded, grad_input)
    taps, grad_input = lax.optimization_barrier(
        (jnp.concatenate((outer_taps, middle_taps), axis=-1), grad_input)
    )
    for stage in stages:
        taps = exchange(taps, stage)
    rows = width_deep >> bits
    taps = taps.reshape(rows, 27, width_in)
    grad_down = jnp.concatenate((taps[:, :9], taps[:, 18:], taps[:, 9:18]), axis=1).astype(jnp.float32)
    return (grad_input, grad_down, grad_gain, grad_shift)


def solution(mesh):
    return jax.shard_map(
        local,
        mesh=mesh,
        in_specs=(
            P("slab", "grp", None, None),
            P("slab", "grp", None, None),
            P("slab", None, "grp"),
            P("slab", None, "grp"),
            P("slab"),
            P(),
            P(),
        ),
        out_specs=(
            P("slab", "grp", None, None),
            P(("slab", "grp"), None, None),
            P("slab"),
            P("slab"),
        ),
        check_vma=False,
    )
```

```python
import functools
import math

import jax
import jax.numpy as jnp
from jax import lax
from jax.experimental import pallas as pl
from jax.experimental.pallas import tpu as pltpu
from jax.sharding import PartitionSpec as P

LANES = 128


def bit_pairs(slabs, groups, slab_bits, grp_bits):
    return [
        (s * groups + g, (s ^ slab_bits) * groups + (g ^ grp_bits))
        for s in range(slabs)
        for g in range(groups)
    ]


def from_next(shard, axis):
    devices = lax.axis_size(axis)
    return lax.ppermute(shard, axis, [(i, i - 1) for i in range(1, devices)])


def grp_parts(values):
    groups = lax.axis_size("grp")
    return [values] + [
        lax.ppermute(values, "grp", [(i, i ^ step) for i in range(groups)])
        for step in range(1, groups)
    ]


def pair_sum(parts):
    while len(parts) > 1:
        parts = [first + second for first, second in zip(parts[::2], parts[1::2])]
    return parts[0]


def place_bits():
    return (lax.axis_size("slab") * lax.axis_size("grp")).bit_length() - 1


def exchange(held, stage, kind=jnp.bfloat16):
    slabs = lax.axis_size("slab")
    groups = lax.axis_size("grp")
    place = lax.axis_index("slab") * groups + lax.axis_index("grp")
    dims = [place_bits() - 1 - b for b in stage]

    def pick(flips):
        array = held
        for dim, bit, flip in zip(dims, stage, flips):
            array = lax.dynamic_slice_in_dim(array, (place >> bit & 1) ^ flip, 1, dim)
        return array

    total = pick([0] * len(dims)).astype(jnp.float32)
    for code in (3, 1, 2) if len(stage) == 2 else (1,):
        flips = [code >> n & 1 for n in range(len(stage))]
        mask = sum(f << b for f, b in zip(flips, stage))
        pairs = bit_pairs(slabs, groups, mask // groups, mask % groups)
        arrived = lax.ppermute(pick(flips), ("slab", "grp"), pairs)
        total = total + arrived.astype(jnp.float32)
    return total.astype(kind)


def exchange_parts(parts, bits):
    slabs = lax.axis_size("slab")
    groups = lax.axis_size("grp")
    rows = parts[0].shape[0] >> (place_bits() - bits)
    total = parts[0].astype(jnp.float32)
    for mask, part in reversed(list(enumerate(parts[1:], 1))):
        pairs = bit_pairs(slabs, groups, mask // groups, mask % groups)
        total = total + lax.ppermute(part, ("slab", "grp"), pairs).astype(jnp.float32)
    dims = (2,) * (place_bits() - bits) + (1,) * bits
    return total.astype(jnp.bfloat16).reshape(*dims, rows, total.shape[1])


def deep_kernel(rows_ref, taps_ref, out_ref, rows, taps, wide, cells, row_sems, tap_sem):
    steps = row_sems.shape[0]
    depth = rows_ref.shape[2] // 2
    width = rows_ref.shape[3]
    step = rows_ref.shape[1] // steps
    count = step // 2 * depth
    taps_copy = pltpu.make_async_copy(taps_ref, taps, tap_sem)
    copies = [
        pltpu.make_async_copy(
            rows_ref.at[:, pl.ds(n * step, step)], rows.at[:, pl.ds(n * step, step)], row_sems.at[n]
        )
        for n in range(steps)
    ]
    copies[0].start()
    taps_copy.start()
    for copy in copies[1:]:
        copy.start()

    def split(n):
        for pair in range(step // 2):
            for px in range(2):
                for py in range(2):
                    tap = 4 * px + 2 * py
                    slot = wide.at[pair * 4 + px * 2 + py]
                    slot[...] = rows[px, n * step + 2 * pair + py].astype(jnp.float32)
                    for pz in range(2):
                        cells[
                            n % 2,
                            pair * depth : (pair + 1) * depth,
                            (tap + pz) * width : (tap + pz + 1) * width,
                        ] = slot[pl.ds(pz, depth, stride=2), :].astype(jnp.bfloat16)

    def multiply(n):
        sums = lax.dot_general(
            jnp.concatenate([taps[p] for p in range(8)], axis=1),
            cells[n % 2],
            (((1,), (1,)), ((), ())),
            preferred_element_type=jnp.float32,
        )
        out_ref[:, n * count : (n + 1) * count] = sums.astype(jnp.bfloat16)

    for n, copy in enumerate(copies):
        copy.wait()
        if n == 1:
            taps_copy.wait()
        if n:
            multiply(n - 1)
        split(n)
    multiply(steps - 1)


def deep_gradient(out_grad, w_up):
    _, rows, fine_depth, width_in = out_grad.shape
    width_deep = w_up.shape[1]
    cells = rows * fine_depth // 4
    steps = rows // 16
    return pl.pallas_call(
        deep_kernel,
        in_specs=[pl.BlockSpec(memory_space=pltpu.HBM)] * 2,
        out_specs=pl.BlockSpec(memory_space=pltpu.VMEM),
        out_shape=jax.ShapeDtypeStruct((width_deep, cells), jnp.bfloat16),
        scratch_shapes=[
            pltpu.VMEM(out_grad.shape, jnp.bfloat16),
            pltpu.VMEM(w_up.shape, jnp.bfloat16),
            pltpu.VMEM((rows // steps * 2, fine_depth, width_in), jnp.float32),
            pltpu.VMEM((2, cells // steps, 8 * width_in), jnp.bfloat16),
            pltpu.SemaphoreType.DMA((steps,)),
            pltpu.SemaphoreType.DMA,
        ],
        compiler_params=pltpu.CompilerParams(vmem_limit_bytes=60 << 20),
        cost_estimate=pl.CostEstimate(
            flops=2 * 8 * cells * width_deep * width_in,
            bytes_accessed=2 * (out_grad.size + w_up.size + width_deep * cells),
            transcendentals=0,
        ),
        name="deep_gradient",
    )(out_grad, w_up)


def shifted_kernel(fine_ref, out_ref, wide):
    planes, fine_rows, fine_depth, width = fine_ref.shape
    depth = fine_depth // 2
    cells = fine_rows // 2 * depth
    zeros = jnp.zeros((depth, out_ref.shape[1]), jnp.bfloat16)
    wide[:, 0:8, :] = jnp.zeros((wide.shape[0], 8, width), jnp.float32)
    out_ref[cells : cells + depth, :] = zeros
    out_ref[2 * cells + depth :, :] = zeros

    def row(y, carry):
        for px in range(planes):
            for py in range(2):
                slot = wide.at[2 * px + py]
                slot[8:, :] = fine_ref[px, 2 * y + py].astype(jnp.float32)
                start = pl.multiple_of(y * depth + py * (cells + depth), depth)
                for kz in range(3):
                    column = (3 * px + kz) * width
                    out_ref[pl.ds(start, depth), column : column + width] = slot[
                        pl.ds(7 + kz, depth, stride=2), :
                    ].astype(jnp.bfloat16)
        return carry

    lax.fori_loop(0, fine_rows // 2, row, 0)


def shifted_fine(fine_input, first):
    planes, fine_rows, fine_depth, width = fine_input.shape
    planes -= first
    depth = fine_depth // 2
    shape = shifted_shape(fine_input, planes)
    return pl.pallas_call(
        shifted_kernel,
        grid=(1,),
        in_specs=[
            pl.BlockSpec((planes, fine_rows, fine_depth, width), lambda i: (first // planes, 0, 0, 0))
        ],
        out_specs=pl.BlockSpec(shape, lambda i: (0, 0)),
        out_shape=jax.ShapeDtypeStruct(shape, jnp.bfloat16),
        scratch_shapes=[pltpu.VMEM((2 * planes, fine_depth + 8, width), jnp.float32)],
        compiler_params=pltpu.CompilerParams(vmem_limit_bytes=16 << 20),
        cost_estimate=pl.CostEstimate(flops=0, bytes_accessed=0, transcendentals=0),
        name="shifted_fine",
    )(fine_input)


def block_of(ref, block, width_deep):
    if len(ref.shape) == 2:
        return ref[:, block * LANES : (block + 1) * LANES]
    slabs = ref.shape[0]
    channels = width_deep // slabs
    start = block * channels
    if start + channels <= ref.shape[1]:
        return jnp.concatenate([ref[t, start : start + channels, :] for t in range(slabs)], axis=0)
    left = lax.broadcasted_iota(jnp.int32, (channels // 2, LANES), 1) < LANES // 2
    pieces = []
    for t in range(slabs):
        both = ref[t, start:, :].astype(jnp.float32)
        for half in (both, pltpu.roll(both, LANES // 2, 1)):
            pieces.append(jnp.where(left, half, 0.0))
    return jnp.concatenate(pieces, axis=0).astype(jnp.bfloat16)


def tap_kernel(scale, depth, rows, jobs, own_ref, packed_ref, shifted_ref, *refs):
    *out_refs, grads_ref = refs
    for block in range(grads_ref.shape[1] // LANES):
        columns = slice(block * LANES, (block + 1) * LANES)
        grads_ref[:, columns] = block_of(packed_ref, block, grads_ref.shape[0])
    cells = (shifted_ref.shape[0] - 2 * depth) // 2
    width = 3 * LANES
    starts = (cells, 0, cells + depth)
    for pieces, bits in jobs:
        count = 1 << bits if rows else 1
        outs, out_refs = out_refs[:count], out_refs[count:]
        for place, (px, ky) in enumerate(pieces):
            span = grads_ref.shape[1] if ky == 0 else cells
            sums = scale * jnp.dot(
                grads_ref[:, :span],
                shifted_ref[starts[ky] : starts[ky] + span, px * width : (px + 1) * width],
                preferred_element_type=jnp.float32,
            )
            parts = [sums]
            if rows:
                sums = sums.reshape(-1, count, rows, width)
                parts = [sums[:, n].reshape(-1, width) for n in range(count)]
                for bit in range(bits):
                    own = (own_ref[0] >> bit & 1) > 0
                    parts = [
                        jnp.where(own, parts[n ^ (1 << bit)], part) for n, part in enumerate(parts)
                    ]
            for out_ref, part in zip(outs, parts):
                out_ref[:, place * width : (place + 1) * width] = part.astype(jnp.bfloat16)


def shift_and_tap_kernel(scale, depth, rows, jobs, own_ref, grads_ref, fine_ref, *refs):
    *out_refs, shifted, wide, grads = refs
    shifted_kernel(fine_ref, shifted, wide)
    tap_kernel(scale, depth, rows, jobs, own_ref, grads_ref, shifted, *out_refs, grads)


def shifted_shape(fine_input, planes):
    _, fine_rows, fine_depth, width = fine_input.shape
    return ((fine_rows + 2) * (fine_depth // 2), planes * 3 * width)


def tap_sums(grads, source, depth, scale, jobs, shape):
    width_deep, padded = shape
    scratch = []
    kernel = tap_kernel
    if source.ndim == 4:
        kernel = shift_and_tap_kernel
        planes, _, fine_depth, width = source.shape
        scratch = [
            pltpu.VMEM(shifted_shape(source, planes), jnp.bfloat16),
            pltpu.VMEM((2 * planes, fine_depth + 8, width), jnp.float32),
        ]
    widths = [3 * LANES * len(pieces) for pieces, _ in jobs]
    rows = width_deep >> place_bits()
    place = lax.axis_index("slab") * lax.axis_size("grp") + lax.axis_index("grp")
    inside = rows % 8 == 0
    counts = [1 << bits if inside else 1 for _, bits in jobs]
    outs = [
        jax.ShapeDtypeStruct((width_deep // count, columns), jnp.bfloat16)
        for count, columns in zip(counts, widths)
        for _ in range(count)
    ]
    arrays = pl.pallas_call(
        functools.partial(kernel, scale, depth, rows if inside else 0, jobs),
        in_specs=[pl.BlockSpec(memory_space=pltpu.SMEM)]
        + [pl.BlockSpec(memory_space=pltpu.VMEM)] * 2,
        out_specs=[pl.BlockSpec(memory_space=pltpu.VMEM)] * len(outs),
        out_shape=outs,
        scratch_shapes=[*scratch, pltpu.VMEM(shape, jnp.bfloat16)],
        compiler_params=pltpu.CompilerParams(vmem_limit_bytes=(61 if scratch else 20) << 20),
        cost_estimate=pl.CostEstimate(
            flops=2 * width_deep * padded * sum(widths),
            bytes_accessed=2 * (width_deep * padded + (padded + width_deep) * sum(widths)),
            transcendentals=0,
        ),
        name="tap_sums",
    )(place.astype(jnp.int32).reshape(1), grads, source)
    results = []
    for (_, bits), count, columns in zip(jobs, counts, widths):
        parts, arrays = tuple(arrays[:count]), arrays[count:]
        if not inside:
            held = parts[0].reshape(-1, 1 << bits, rows, columns)
            own = place & ((1 << bits) - 1)
            parts = tuple(
                lax.dynamic_index_in_dim(held, own ^ n, 1, False).reshape(-1, columns)
                for n in range(1 << bits)
            )
        results.append(parts)
    return results


def input_kernel(taps_of, *refs):
    grads_refs = refs[: len(taps_of)]
    taps_ref = refs[len(taps_of)]
    out_ref, turned, product, wide = refs[-4:]
    width = taps_ref.shape[1]
    fine_rows, fine_depth = out_ref.shape[1:3]
    depth = fine_depth // 2
    padded = turned.shape[1]
    for slot, ref in enumerate(grads_refs):
        for block in range(padded // LANES):
            rows = slice(block * LANES, (block + 1) * LANES)
            turned[slot, rows, :] = block_of(ref, block, turned.shape[2]).T
    for ky in range(3):
        total = None
        for slot, kx in enumerate(taps_of):
            taps = jnp.concatenate([taps_ref[9 * kx + 3 * ky + kz] for kz in range(3)], axis=0)
            term = lax.dot_general(
                turned[slot],
                taps,
                (((1,), (1,)), ((), ())),
                preferred_element_type=jnp.float32,
            )
            total = term if total is None else total + term
        product[:, 3 * ky * width : (3 * ky + 3) * width] = total
    inside = lax.broadcasted_iota(jnp.int32, (depth, width), 0) < depth - 1

    def row(y, carry):
        start = pl.multiple_of(y * depth, depth)

        def at(ky, kz):
            offset = depth if ky == 0 else 0
            return product[
                pl.ds(start + offset, depth), (3 * ky + kz) * width : (3 * ky + kz + 1) * width
            ]

        for py in range(2):
            terms = (2, 0) if py else (1,)
            even, odd, following = (sum(at(ky, kz) for ky in terms) for kz in (1, 2, 0))
            following = pltpu.roll(following, depth - 1, 0)
            wide[pl.ds(0, depth, stride=2), :] = even
            wide[pl.ds(1, depth, stride=2), :] = odd + jnp.where(inside, following, 0.0)
            out_ref[0, 2 * y + py] = wide[...].astype(jnp.bfloat16)
        return carry

    lax.fori_loop(0, fine_rows // 2, row, 0)


def input_plane(px, grads, taps_of, w_down, fine_shape, padded, earlier=None):
    _, fine_rows, fine_depth, width = fine_shape
    width_deep = w_down.shape[2]
    operands = list(grads) + [w_down]
    in_specs = [pl.BlockSpec(array.shape, lambda i, n=array.ndim: (0,) * n) for array in grads]
    in_specs.append(pl.BlockSpec(w_down.shape, lambda i: (0, 0, 0)))
    aliases = {}
    if earlier is not None:
        aliases = {len(operands): 0}
        operands.append(earlier)
        in_specs.append(pl.BlockSpec(memory_space=pl.ANY))
    return pl.pallas_call(
        functools.partial(input_kernel, taps_of),
        grid=(1,),
        in_specs=in_specs,
        out_specs=pl.BlockSpec((1, fine_rows, fine_depth, width), lambda i: (px, 0, 0, 0)),
        out_shape=jax.ShapeDtypeStruct(fine_shape, jnp.bfloat16),
        input_output_aliases=aliases,
        scratch_shapes=[
            pltpu.VMEM((len(grads), padded, width_deep), jnp.bfloat16),
            pltpu.VMEM((padded, 9 * width), jnp.float32),
            pltpu.VMEM((fine_depth, width), jnp.float32),
        ],
        compiler_params=pltpu.CompilerParams(vmem_limit_bytes=20 << 20),
        cost_estimate=pl.CostEstimate(flops=0, bytes_accessed=0, transcendentals=0),
        name="input_gradient",
    )(*operands)


def mean_and_variance(first_sum, second_sum, count):
    mean = first_sum / count
    return mean, second_sum / count - mean * mean


def own_moments(first_sum, second_sum, count):
    mean, variance = mean_and_variance(first_sum, second_sum, count)
    return mean, lax.rsqrt(jnp.maximum(variance, 0.0) + 1e-05)


def norm_kernel(own_total, cell_total, parts, direct, *refs):
    part_refs, refs = refs[:parts], refs[parts:]
    gain_ref, inner_ref, slab_ref, values_ref, masked_ref, edge_values_ref, edge_masked_ref = refs[:7]
    *out_refs, totals_ref = refs[7:]
    planes, channels, cells = values_ref.shape
    depth = edge_values_ref.shape[2]

    def columns(array):
        return [array[:, n : n + 1] for n in range(array.shape[1])]

    each = [ref[...] for ref in part_refs]
    sums = columns(pair_sum(each))
    mean, variance = mean_and_variance(sums[0], sums[1], cell_total)
    inv_std = lax.rsqrt(variance + 1e-05)

    def normed_total(part):
        own_mean, own_inv = own_moments(part[0], part[1], own_total)
        return inv_std * (part[3] / own_inv + (own_mean - mean) * part[2])

    shift = sums[2] / cell_total
    slope = pair_sum([normed_total(columns(part)) for part in each]) / cell_total
    totals_ref[:, 0:1] = slope
    totals_ref[:, 1:2] = shift
    gain = gain_ref[...] * inv_std
    edge_gain = gain * inner_ref[0]

    def grad_of(values, masked, gain):
        normed = (values.astype(jnp.float32) - mean) * inv_std
        return gain * (masked.astype(jnp.float32) - shift - normed * slope)

    for n in range(planes):
        plane = n ^ slab_ref[0] if direct else n
        out_ref = out_refs[n] if direct else out_refs[0].at[n]
        main = grad_of(values_ref[plane], masked_ref[plane], gain).astype(jnp.bfloat16)
        edge = grad_of(edge_values_ref[plane], edge_masked_ref[plane], edge_gain)
        if out_ref.shape[1] > LANES:
            spare = jnp.zeros((channels, out_ref.shape[1] - cells - depth), jnp.float32)
            out_ref[:, 0:cells] = main
            out_ref[:, cells:] = jnp.concatenate((edge, spare), axis=1).astype(jnp.bfloat16)
            continue
        for block in range(cells // LANES):
            out_ref[block * channels : (block + 1) * channels, :] = main[
                :, block * LANES : (block + 1) * LANES
            ]
        half = channels // 2
        out_ref[cells // LANES * channels :, :] = jnp.concatenate(
            (edge[:half], edge[half:]), axis=1
        ).astype(jnp.bfloat16)


def place_kernel(slab_ref, *refs):
    *block_refs, out_ref = refs
    for n, block_ref in enumerate(block_refs):
        out_ref[n ^ slab_ref[0]] = block_ref[...]


def local(fine_input, out_grad, pre_norm, act_out, norm_gain, w_down, w_up):
    slabs = lax.axis_size("slab")
    groups = lax.axis_size("grp")
    fine_rows, fine_depth, width_in = fine_input.shape[1:]
    depth = fine_depth // 2
    width_deep = w_up.shape[1]
    channels, slab_planes, cells = pre_norm.shape
    cell_total = slab_planes * cells * groups
    padded = -(-(cells + depth) // LANES) * LANES

    deep_bf = deep_gradient(out_grad, w_up)
    deep_bf, pre_norm, act_out, fine_input = lax.optimization_barrier(
        (deep_bf, pre_norm, act_out, fine_input)
    )
    deep_bf = deep_bf.reshape(slabs, channels, cells)
    grad_vals = lax.all_to_all(deep_bf, "slab", split_axis=0, concat_axis=0, tiled=True)

    values = pre_norm.transpose(1, 0, 2)
    acts = act_out.transpose(1, 0, 2)
    values, acts = lax.optimization_barrier((values, acts))
    edge_values, edge_acts = from_next(jnp.stack((values[:, :, :depth], acts[:, :, :depth])), "grp")
    first_row = grad_vals[:, :, :depth]
    masks = [(2 << n) - 1 for n in range(groups.bit_length() - 1)]

    wide_values = values.astype(jnp.float32)
    first_sum = jnp.sum(wide_values, axis=(0, 2))
    second_sum = jnp.sum(wide_values * wide_values, axis=(0, 2))

    own_total = slab_planes * cells
    own_mean, own_inv = own_moments(first_sum, second_sum, own_total)
    masked_bf = jnp.where(acts > 0, grad_vals, jnp.zeros_like(grad_vals))
    masked = masked_bf.astype(jnp.float32)
    own_normed = (wide_values - own_mean[None, :, None]) * own_inv[None, :, None]
    parts = grp_parts(
        jnp.stack(
            (
                first_sum,
                second_sum,
                jnp.sum(masked, axis=(0, 2)),
                jnp.sum(masked * own_normed, axis=(0, 2)),
            ),
            axis=1,
        )
    )
    edge_grads = [
        lax.ppermute(first_row, "grp", [(i, i ^ mask) for i in range(groups)]) for mask in masks
    ]
    grp = lax.axis_index("grp")
    edge_masked = jnp.zeros_like(first_row)
    for mask, grads in zip(masks, edge_grads):
        edge_masked = jnp.where((grp ^ (grp + 1) == mask) & (edge_acts > 0), grads, edge_masked)
    inner = (grp < groups - 1).astype(jnp.float32).reshape(1)
    vmem = pl.BlockSpec(memory_space=pltpu.VMEM)
    packed = channels % 32 == 0 and 2 * depth == LANES
    act_shape = (slab_planes, channels, padded)
    if packed:
        act_shape = (slab_planes, channels * cells // LANES + channels // 2, LANES)
    direct = packed and slabs <= 8
    blocks = slab_planes if direct else 1
    smem = pl.BlockSpec(memory_space=pltpu.SMEM)
    slab = lax.axis_index("slab").astype(jnp.int32).reshape(1)
    *act_grads, totals = pl.pallas_call(
        functools.partial(norm_kernel, own_total, cell_total, len(parts), direct),
        in_specs=[vmem] * (len(parts) + 1) + [smem] * 2 + [vmem] * 4,
        out_specs=[vmem] * (blocks + 1),
        out_shape=[jax.ShapeDtypeStruct(act_shape[1:] if direct else act_shape, jnp.bfloat16)] * blocks
        + [jax.ShapeDtypeStruct((channels, 2), jnp.float32)],
        compiler_params=pltpu.CompilerParams(vmem_limit_bytes=12 << 20),
        cost_estimate=pl.CostEstimate(
            flops=8 * values.size, bytes_accessed=8 * values.size, transcendentals=0
        ),
        name="act_gradient",
    )(*parts, norm_gain[:, None], inner, slab, values, masked_bf, edge_values, edge_masked)
    grad_gain = totals[:, 0]
    grad_shift = totals[:, 1]
    if direct:
        for mask in sorted(range(1, slabs), key=lambda mask: -(mask >> 1)):
            act_grads[mask] = lax.ppermute(
                act_grads[mask], "slab", [(i, i ^ mask) for i in range(slabs)]
            )
        here = pl.pallas_call(
            place_kernel,
            in_specs=[smem] + [vmem] * slabs,
            out_specs=vmem,
            out_shape=jax.ShapeDtypeStruct(act_shape, jnp.bfloat16),
            compiler_params=pltpu.CompilerParams(vmem_limit_bytes=12 << 20),
            name="place_blocks",
        )(slab, *act_grads)
    else:
        here = lax.all_to_all(act_grads[0], "slab", split_axis=0, concat_axis=0, tiled=True)
    if not packed:
        here = here.reshape(width_deep, padded)
    grad_scale = 1.0 / math.sqrt(cell_total)
    bits = place_bits()
    stages = [tuple(range(b, min(b + 2, bits))) for b in range(3, bits, 2)]
    row = tuple((0, ky) for ky in range(3))
    jobs = ((tuple((1, ky) for ky in range(3)), 1), (row, 2))
    parts = tap_sums(here, fine_input, depth, grad_scale, jobs, (width_deep, padded))
    parts, here_again = lax.optimization_barrier((parts, here))
    last_parts, middle_parts = parts
    after = from_next(here, "slab")
    grad_input = input_plane(0, (here_again,), (1,), w_down, fine_input.shape, padded)
    grad_input, fine_again = lax.optimization_barrier((grad_input, fine_input))
    shifted = shifted_fine(fine_again, fine_input.shape[0] - 1)
    (parts,) = tap_sums(after, shifted, depth, grad_scale, ((row, 1),), (width_deep, padded))
    kept, last_kept, parts = lax.optimization_barrier((middle_parts[0], last_parts[0], parts))
    middle_taps = exchange_parts((kept, *middle_parts[1:]), 2)
    last_taps = exchange_parts((last_kept, *last_parts[1:]), 1)
    first_taps = exchange_parts(parts, 1)
    first_taps, middle_taps, last_taps, after, grad_input = lax.optimization_barrier(
        (first_taps, middle_taps, last_taps, after, grad_input)
    )
    outer_taps = exchange(jnp.concatenate((first_taps, last_taps), axis=-1), (1, 2))
    middle_taps = exchange(middle_taps, (2,))
    grad_input = input_plane(1, (here, after), (2, 0), w_down, fine_input.shape, padded, grad_input)
    taps, grad_input = lax.optimization_barrier(
        (jnp.concatenate((outer_taps, middle_taps), axis=-1), grad_input)
    )
    for stage in stages:
        taps = exchange(taps, stage, jnp.float32 if stage is stages[-1] else jnp.bfloat16)
    rows = width_deep >> bits
    taps = taps.reshape(rows, 27, width_in)
    grad_down = jnp.concatenate((taps[:, :9], taps[:, 18:], taps[:, 9:18]), axis=1).astype(jnp.float32)
    return (grad_input, grad_down, grad_gain, grad_shift)


def solution(mesh):
    return jax.shard_map(
        local,
        mesh=mesh,
        in_specs=(
            P("slab", "grp", None, None),
            P("slab", "grp", None, None),
            P("slab", None, "grp"),
            P("slab", None, "grp"),
            P("slab"),
            P(),
            P(),
        ),
        out_specs=(
            P("slab", "grp", None, None),
            P(("slab", "grp"), None, None),
            P("slab"),
            P("slab"),
        ),
        check_vma=False,
    )
```

```python
import functools
import math

import jax
import jax.numpy as jnp
from jax import lax
from jax.experimental import pallas as pl
from jax.experimental.pallas import tpu as pltpu
from jax.sharding import PartitionSpec as P

LANES = 128


def bit_pairs(slabs, groups, slab_bits, grp_bits):
    return [
        (s * groups + g, (s ^ slab_bits) * groups + (g ^ grp_bits))
        for s in range(slabs)
        for g in range(groups)
    ]


def from_next(shard, axis):
    devices = lax.axis_size(axis)
    return lax.ppermute(shard, axis, [(i, i - 1) for i in range(1, devices)])


def grp_parts(values):
    groups = lax.axis_size("grp")
    return [values] + [
        lax.ppermute(values, "grp", [(i, i ^ step) for i in range(groups)])
        for step in range(1, groups)
    ]


def pair_sum(parts):
    while len(parts) > 1:
        parts = [first + second for first, second in zip(parts[::2], parts[1::2])]
    return parts[0]


def place_bits():
    return (lax.axis_size("slab") * lax.axis_size("grp")).bit_length() - 1


def exchange(held, stage, kind=jnp.bfloat16):
    slabs = lax.axis_size("slab")
    groups = lax.axis_size("grp")
    place = lax.axis_index("slab") * groups + lax.axis_index("grp")
    dims = [place_bits() - 1 - b for b in stage]

    def pick(flips):
        array = held
        for dim, bit, flip in zip(dims, stage, flips):
            array = lax.dynamic_slice_in_dim(array, (place >> bit & 1) ^ flip, 1, dim)
        return array

    total = pick([0] * len(dims)).astype(jnp.float32)
    for code in (3, 1, 2) if len(stage) == 2 else (1,):
        flips = [code >> n & 1 for n in range(len(stage))]
        mask = sum(f << b for f, b in zip(flips, stage))
        pairs = bit_pairs(slabs, groups, mask // groups, mask % groups)
        arrived = lax.ppermute(pick(flips), ("slab", "grp"), pairs)
        total = total + arrived.astype(jnp.float32)
    return total.astype(kind)


def exchange_parts(parts, bits):
    slabs = lax.axis_size("slab")
    groups = lax.axis_size("grp")
    rows = parts[0].shape[0] >> (place_bits() - bits)
    total = parts[0].astype(jnp.float32)
    for mask, part in reversed(list(enumerate(parts[1:], 1))):
        pairs = bit_pairs(slabs, groups, mask // groups, mask % groups)
        total = total + lax.ppermute(part, ("slab", "grp"), pairs).astype(jnp.float32)
    dims = (2,) * (place_bits() - bits) + (1,) * bits
    return total.astype(jnp.bfloat16).reshape(*dims, rows, total.shape[1])


def deep_kernel(rows_ref, taps_ref, out_ref, rows, taps, wide, cells, row_sems, tap_sem):
    steps = row_sems.shape[0]
    depth = rows_ref.shape[2] // 2
    width = rows_ref.shape[3]
    step = rows_ref.shape[1] // steps
    count = step // 2 * depth
    taps_copy = pltpu.make_async_copy(taps_ref, taps, tap_sem)
    copies = [
        pltpu.make_async_copy(
            rows_ref.at[:, pl.ds(n * step, step)], rows.at[:, pl.ds(n * step, step)], row_sems.at[n]
        )
        for n in range(steps)
    ]
    copies[0].start()
    taps_copy.start()
    for copy in copies[1:]:
        copy.start()

    def split(n):
        for pair in range(step // 2):
            for px in range(2):
                for py in range(2):
                    tap = 4 * px + 2 * py
                    slot = wide.at[pair * 4 + px * 2 + py]
                    slot[...] = rows[px, n * step + 2 * pair + py].astype(jnp.float32)
                    for pz in range(2):
                        cells[
                            n % 2,
                            pair * depth : (pair + 1) * depth,
                            (tap + pz) * width : (tap + pz + 1) * width,
                        ] = slot[pl.ds(pz, depth, stride=2), :].astype(jnp.bfloat16)

    def multiply(n):
        sums = lax.dot_general(
            jnp.concatenate([taps[p] for p in range(8)], axis=1),
            cells[n % 2],
            (((1,), (1,)), ((), ())),
            preferred_element_type=jnp.float32,
        )
        out_ref[:, n * count : (n + 1) * count] = sums.astype(jnp.bfloat16)

    for n, copy in enumerate(copies):
        copy.wait()
        if n == 1:
            taps_copy.wait()
        if n:
            multiply(n - 1)
        split(n)
    multiply(steps - 1)


def deep_gradient(out_grad, w_up):
    _, rows, fine_depth, width_in = out_grad.shape
    width_deep = w_up.shape[1]
    cells = rows * fine_depth // 4
    steps = rows // 16
    return pl.pallas_call(
        deep_kernel,
        in_specs=[pl.BlockSpec(memory_space=pltpu.HBM)] * 2,
        out_specs=pl.BlockSpec(memory_space=pltpu.VMEM),
        out_shape=jax.ShapeDtypeStruct((width_deep, cells), jnp.bfloat16),
        scratch_shapes=[
            pltpu.VMEM(out_grad.shape, jnp.bfloat16),
            pltpu.VMEM(w_up.shape, jnp.bfloat16),
            pltpu.VMEM((rows // steps * 2, fine_depth, width_in), jnp.float32),
            pltpu.VMEM((2, cells // steps, 8 * width_in), jnp.bfloat16),
            pltpu.SemaphoreType.DMA((steps,)),
            pltpu.SemaphoreType.DMA,
        ],
        compiler_params=pltpu.CompilerParams(vmem_limit_bytes=60 << 20),
        cost_estimate=pl.CostEstimate(
            flops=2 * 8 * cells * width_deep * width_in,
            bytes_accessed=2 * (out_grad.size + w_up.size + width_deep * cells),
            transcendentals=0,
        ),
        name="deep_gradient",
    )(out_grad, w_up)


def shifted_kernel(fine_ref, out_ref, wide):
    planes, fine_rows, fine_depth, width = fine_ref.shape
    depth = fine_depth // 2
    cells = fine_rows // 2 * depth
    zeros = jnp.zeros((depth, out_ref.shape[1]), jnp.bfloat16)
    wide[:, 0:8, :] = jnp.zeros((wide.shape[0], 8, width), jnp.float32)
    out_ref[cells : cells + depth, :] = zeros
    out_ref[2 * cells + depth :, :] = zeros

    def row(y, carry):
        for px in range(planes):
            for py in range(2):
                slot = wide.at[2 * px + py]
                slot[8:, :] = fine_ref[px, 2 * y + py].astype(jnp.float32)
                start = pl.multiple_of(y * depth + py * (cells + depth), depth)
                for kz in range(3):
                    column = (3 * px + kz) * width
                    out_ref[pl.ds(start, depth), column : column + width] = slot[
                        pl.ds(7 + kz, depth, stride=2), :
                    ].astype(jnp.bfloat16)
        return carry

    lax.fori_loop(0, fine_rows // 2, row, 0)


def shifted_fine(fine_input, first):
    planes, fine_rows, fine_depth, width = fine_input.shape
    planes -= first
    depth = fine_depth // 2
    shape = shifted_shape(fine_input, planes)
    return pl.pallas_call(
        shifted_kernel,
        grid=(1,),
        in_specs=[
            pl.BlockSpec((planes, fine_rows, fine_depth, width), lambda i: (first // planes, 0, 0, 0))
        ],
        out_specs=pl.BlockSpec(shape, lambda i: (0, 0)),
        out_shape=jax.ShapeDtypeStruct(shape, jnp.bfloat16),
        scratch_shapes=[pltpu.VMEM((2 * planes, fine_depth + 8, width), jnp.float32)],
        compiler_params=pltpu.CompilerParams(vmem_limit_bytes=16 << 20),
        cost_estimate=pl.CostEstimate(flops=0, bytes_accessed=0, transcendentals=0),
        name="shifted_fine",
    )(fine_input)


def block_of(ref, block, width_deep):
    if len(ref.shape) == 2:
        return ref[:, block * LANES : (block + 1) * LANES]
    slabs = ref.shape[0]
    channels = width_deep // slabs
    start = block * channels
    if start + channels <= ref.shape[1]:
        return jnp.concatenate([ref[t, start : start + channels, :] for t in range(slabs)], axis=0)
    left = lax.broadcasted_iota(jnp.int32, (channels // 2, LANES), 1) < LANES // 2
    pieces = []
    for t in range(slabs):
        both = ref[t, start:, :].astype(jnp.float32)
        for half in (both, pltpu.roll(both, LANES // 2, 1)):
            pieces.append(jnp.where(left, half, 0.0))
    return jnp.concatenate(pieces, axis=0).astype(jnp.bfloat16)


def tap_kernel(scale, depth, rows, jobs, own_ref, packed_ref, shifted_ref, *refs):
    *out_refs, grads_ref = refs
    for block in range(grads_ref.shape[1] // LANES):
        columns = slice(block * LANES, (block + 1) * LANES)
        grads_ref[:, columns] = block_of(packed_ref, block, grads_ref.shape[0])
    cells = (shifted_ref.shape[0] - 2 * depth) // 2
    width = 3 * LANES
    starts = (cells, 0, cells + depth)
    for pieces, bits in jobs:
        count = 1 << bits if rows else 1
        outs, out_refs = out_refs[:count], out_refs[count:]
        for place, (px, ky) in enumerate(pieces):
            span = grads_ref.shape[1] if ky == 0 else cells
            sums = scale * jnp.dot(
                grads_ref[:, :span],
                shifted_ref[starts[ky] : starts[ky] + span, px * width : (px + 1) * width],
                preferred_element_type=jnp.float32,
            )
            parts = [sums]
            if rows:
                sums = sums.reshape(-1, count, rows, width)
                parts = [sums[:, n].reshape(-1, width) for n in range(count)]
                for bit in range(bits):
                    own = (own_ref[0] >> bit & 1) > 0
                    parts = [
                        jnp.where(own, parts[n ^ (1 << bit)], part) for n, part in enumerate(parts)
                    ]
            for out_ref, part in zip(outs, parts):
                out_ref[:, place * width : (place + 1) * width] = part.astype(jnp.bfloat16)


def shift_and_tap_kernel(scale, depth, rows, jobs, own_ref, grads_ref, fine_ref, *refs):
    *out_refs, shifted, wide, grads = refs
    shifted_kernel(fine_ref, shifted, wide)
    tap_kernel(scale, depth, rows, jobs, own_ref, grads_ref, shifted, *out_refs, grads)


def shifted_shape(fine_input, planes):
    _, fine_rows, fine_depth, width = fine_input.shape
    return ((fine_rows + 2) * (fine_depth // 2), planes * 3 * width)


def tap_sums(grads, source, depth, scale, jobs, shape):
    width_deep, padded = shape
    scratch = []
    kernel = tap_kernel
    if source.ndim == 4:
        kernel = shift_and_tap_kernel
        planes, _, fine_depth, width = source.shape
        scratch = [
            pltpu.VMEM(shifted_shape(source, planes), jnp.bfloat16),
            pltpu.VMEM((2 * planes, fine_depth + 8, width), jnp.float32),
        ]
    widths = [3 * LANES * len(pieces) for pieces, _ in jobs]
    rows = width_deep >> place_bits()
    place = lax.axis_index("slab") * lax.axis_size("grp") + lax.axis_index("grp")
    inside = rows % 8 == 0
    counts = [1 << bits if inside else 1 for _, bits in jobs]
    outs = [
        jax.ShapeDtypeStruct((width_deep // count, columns), jnp.bfloat16)
        for count, columns in zip(counts, widths)
        for _ in range(count)
    ]
    arrays = pl.pallas_call(
        functools.partial(kernel, scale, depth, rows if inside else 0, jobs),
        in_specs=[pl.BlockSpec(memory_space=pltpu.SMEM)]
        + [pl.BlockSpec(memory_space=pltpu.VMEM)] * 2,
        out_specs=[pl.BlockSpec(memory_space=pltpu.VMEM)] * len(outs),
        out_shape=outs,
        scratch_shapes=[*scratch, pltpu.VMEM(shape, jnp.bfloat16)],
        compiler_params=pltpu.CompilerParams(vmem_limit_bytes=(61 if scratch else 40) << 20),
        cost_estimate=pl.CostEstimate(
            flops=2 * width_deep * padded * sum(widths),
            bytes_accessed=2 * (width_deep * padded + (padded + width_deep) * sum(widths)),
            transcendentals=0,
        ),
        name="tap_sums",
    )(place.astype(jnp.int32).reshape(1), grads, source)
    results = []
    for (_, bits), count, columns in zip(jobs, counts, widths):
        parts, arrays = tuple(arrays[:count]), arrays[count:]
        if not inside:
            held = parts[0].reshape(-1, 1 << bits, rows, columns)
            own = place & ((1 << bits) - 1)
            parts = tuple(
                lax.dynamic_index_in_dim(held, own ^ n, 1, False).reshape(-1, columns)
                for n in range(1 << bits)
            )
        results.append(parts)
    return results


def input_kernel(taps_of, *refs):
    grads_refs = refs[: len(taps_of)]
    taps_ref = refs[len(taps_of)]
    out_ref, turned, product, wide = refs[-4:]
    width = taps_ref.shape[1]
    fine_rows, fine_depth = out_ref.shape[1:3]
    depth = fine_depth // 2
    padded = turned.shape[1]
    for slot, ref in enumerate(grads_refs):
        for block in range(padded // LANES):
            rows = slice(block * LANES, (block + 1) * LANES)
            turned[slot, rows, :] = block_of(ref, block, turned.shape[2]).T
    for ky in range(3):
        total = None
        for slot, kx in enumerate(taps_of):
            taps = jnp.concatenate([taps_ref[9 * kx + 3 * ky + kz] for kz in range(3)], axis=0)
            term = lax.dot_general(
                turned[slot],
                taps,
                (((1,), (1,)), ((), ())),
                preferred_element_type=jnp.float32,
            )
            total = term if total is None else total + term
        product[:, 3 * ky * width : (3 * ky + 3) * width] = total
    inside = lax.broadcasted_iota(jnp.int32, (depth, width), 0) < depth - 1

    def row(y, carry):
        start = pl.multiple_of(y * depth, depth)

        def at(ky, kz):
            offset = depth if ky == 0 else 0
            return product[
                pl.ds(start + offset, depth), (3 * ky + kz) * width : (3 * ky + kz + 1) * width
            ]

        for py in range(2):
            terms = (2, 0) if py else (1,)
            even, odd, following = (sum(at(ky, kz) for ky in terms) for kz in (1, 2, 0))
            following = pltpu.roll(following, depth - 1, 0)
            wide[pl.ds(0, depth, stride=2), :] = even
            wide[pl.ds(1, depth, stride=2), :] = odd + jnp.where(inside, following, 0.0)
            out_ref[0, 2 * y + py] = wide[...].astype(jnp.bfloat16)
        return carry

    lax.fori_loop(0, fine_rows // 2, row, 0)


def input_plane(px, grads, taps_of, w_down, fine_shape, padded, earlier=None):
    _, fine_rows, fine_depth, width = fine_shape
    width_deep = w_down.shape[2]
    operands = list(grads) + [w_down]
    in_specs = [pl.BlockSpec(array.shape, lambda i, n=array.ndim: (0,) * n) for array in grads]
    in_specs.append(pl.BlockSpec(w_down.shape, lambda i: (0, 0, 0)))
    aliases = {}
    if earlier is not None:
        aliases = {len(operands): 0}
        operands.append(earlier)
        in_specs.append(pl.BlockSpec(memory_space=pl.ANY))
    return pl.pallas_call(
        functools.partial(input_kernel, taps_of),
        grid=(1,),
        in_specs=in_specs,
        out_specs=pl.BlockSpec((1, fine_rows, fine_depth, width), lambda i: (px, 0, 0, 0)),
        out_shape=jax.ShapeDtypeStruct(fine_shape, jnp.bfloat16),
        input_output_aliases=aliases,
        scratch_shapes=[
            pltpu.VMEM((len(grads), padded, width_deep), jnp.bfloat16),
            pltpu.VMEM((padded, 9 * width), jnp.float32),
            pltpu.VMEM((fine_depth, width), jnp.float32),
        ],
        compiler_params=pltpu.CompilerParams(vmem_limit_bytes=20 << 20),
        cost_estimate=pl.CostEstimate(flops=0, bytes_accessed=0, transcendentals=0),
        name="input_gradient",
    )(*operands)


def mean_and_variance(first_sum, second_sum, count):
    mean = first_sum / count
    return mean, second_sum / count - mean * mean


def own_moments(first_sum, second_sum, count):
    mean, variance = mean_and_variance(first_sum, second_sum, count)
    return mean, lax.rsqrt(jnp.maximum(variance, 0.0) + 1e-05)


def norm_kernel(own_total, cell_total, parts, direct, *refs):
    part_refs, refs = refs[:parts], refs[parts:]
    gain_ref, inner_ref, slab_ref, values_ref, masked_ref, edge_values_ref, edge_masked_ref = refs[:7]
    *out_refs, totals_ref = refs[7:]
    planes, channels, cells = values_ref.shape
    depth = edge_values_ref.shape[2]

    def columns(array):
        return [array[:, n : n + 1] for n in range(array.shape[1])]

    each = [ref[...] for ref in part_refs]
    sums = columns(pair_sum(each))
    mean, variance = mean_and_variance(sums[0], sums[1], cell_total)
    inv_std = lax.rsqrt(variance + 1e-05)

    def normed_total(part):
        own_mean, own_inv = own_moments(part[0], part[1], own_total)
        return inv_std * (part[3] / own_inv + (own_mean - mean) * part[2])

    shift = sums[2] / cell_total
    slope = pair_sum([normed_total(columns(part)) for part in each]) / cell_total
    totals_ref[:, 0:1] = slope
    totals_ref[:, 1:2] = shift
    gain = gain_ref[...] * inv_std
    edge_gain = gain * inner_ref[0]

    def grad_of(values, masked, gain):
        normed = (values.astype(jnp.float32) - mean) * inv_std
        return gain * (masked.astype(jnp.float32) - shift - normed * slope)

    for n in range(planes):
        plane = n ^ slab_ref[0] if direct else n
        out_ref = out_refs[n] if direct else out_refs[0].at[n]
        main = grad_of(values_ref[plane], masked_ref[plane], gain).astype(jnp.bfloat16)
        edge = grad_of(edge_values_ref[plane], edge_masked_ref[plane], edge_gain)
        if out_ref.shape[1] > LANES:
            spare = jnp.zeros((channels, out_ref.shape[1] - cells - depth), jnp.float32)
            out_ref[:, 0:cells] = main
            out_ref[:, cells:] = jnp.concatenate((edge, spare), axis=1).astype(jnp.bfloat16)
            continue
        for block in range(cells // LANES):
            out_ref[block * channels : (block + 1) * channels, :] = main[
                :, block * LANES : (block + 1) * LANES
            ]
        half = channels // 2
        out_ref[cells // LANES * channels :, :] = jnp.concatenate(
            (edge[:half], edge[half:]), axis=1
        ).astype(jnp.bfloat16)


def place_kernel(slab_ref, *refs):
    *block_refs, out_ref = refs
    for n, block_ref in enumerate(block_refs):
        out_ref[n ^ slab_ref[0]] = block_ref[...]


def local(fine_input, out_grad, pre_norm, act_out, norm_gain, w_down, w_up):
    slabs = lax.axis_size("slab")
    groups = lax.axis_size("grp")
    fine_rows, fine_depth, width_in = fine_input.shape[1:]
    depth = fine_depth // 2
    width_deep = w_up.shape[1]
    channels, slab_planes, cells = pre_norm.shape
    cell_total = slab_planes * cells * groups
    padded = -(-(cells + depth) // LANES) * LANES

    deep_bf = deep_gradient(out_grad, w_up)
    deep_bf, pre_norm, act_out, fine_input = lax.optimization_barrier(
        (deep_bf, pre_norm, act_out, fine_input)
    )
    deep_bf = deep_bf.reshape(slabs, channels, cells)
    grad_vals = lax.all_to_all(deep_bf, "slab", split_axis=0, concat_axis=0, tiled=True)

    values = pre_norm.transpose(1, 0, 2)
    acts = act_out.transpose(1, 0, 2)
    values, acts = lax.optimization_barrier((values, acts))
    edge_values, edge_acts = from_next(jnp.stack((values[:, :, :depth], acts[:, :, :depth])), "grp")
    first_row = grad_vals[:, :, :depth]
    masks = [(2 << n) - 1 for n in range(groups.bit_length() - 1)]

    wide_values = values.astype(jnp.float32)
    first_sum = jnp.sum(wide_values, axis=(0, 2))
    second_sum = jnp.sum(wide_values * wide_values, axis=(0, 2))

    own_total = slab_planes * cells
    own_mean, own_inv = own_moments(first_sum, second_sum, own_total)
    masked_bf = jnp.where(acts > 0, grad_vals, jnp.zeros_like(grad_vals))
    masked = masked_bf.astype(jnp.float32)
    own_normed = (wide_values - own_mean[None, :, None]) * own_inv[None, :, None]
    parts = grp_parts(
        jnp.stack(
            (
                first_sum,
                second_sum,
                jnp.sum(masked, axis=(0, 2)),
                jnp.sum(masked * own_normed, axis=(0, 2)),
            ),
            axis=1,
        )
    )
    edge_grads = [
        lax.ppermute(first_row, "grp", [(i, i ^ mask) for i in range(groups)]) for mask in masks
    ]
    grp = lax.axis_index("grp")
    edge_masked = jnp.zeros_like(first_row)
    for mask, grads in zip(masks, edge_grads):
        edge_masked = jnp.where((grp ^ (grp + 1) == mask) & (edge_acts > 0), grads, edge_masked)
    inner = (grp < groups - 1).astype(jnp.float32).reshape(1)
    vmem = pl.BlockSpec(memory_space=pltpu.VMEM)
    packed = channels % 32 == 0 and 2 * depth == LANES
    act_shape = (slab_planes, channels, padded)
    if packed:
        act_shape = (slab_planes, channels * cells // LANES + channels // 2, LANES)
    direct = packed and slabs <= 8
    blocks = slab_planes if direct else 1
    smem = pl.BlockSpec(memory_space=pltpu.SMEM)
    slab = lax.axis_index("slab").astype(jnp.int32).reshape(1)
    *act_grads, totals = pl.pallas_call(
        functools.partial(norm_kernel, own_total, cell_total, len(parts), direct),
        in_specs=[vmem] * (len(parts) + 1) + [smem] * 2 + [vmem] * 4,
        out_specs=[vmem] * (blocks + 1),
        out_shape=[jax.ShapeDtypeStruct(act_shape[1:] if direct else act_shape, jnp.bfloat16)] * blocks
        + [jax.ShapeDtypeStruct((channels, 2), jnp.float32)],
        compiler_params=pltpu.CompilerParams(vmem_limit_bytes=12 << 20),
        cost_estimate=pl.CostEstimate(
            flops=8 * values.size, bytes_accessed=8 * values.size, transcendentals=0
        ),
        name="act_gradient",
    )(*parts, norm_gain[:, None], inner, slab, values, masked_bf, edge_values, edge_masked)
    grad_gain = totals[:, 0]
    grad_shift = totals[:, 1]
    if direct:
        for mask in sorted(range(1, slabs), key=lambda mask: -(mask >> 1)):
            act_grads[mask] = lax.ppermute(
                act_grads[mask], "slab", [(i, i ^ mask) for i in range(slabs)]
            )
        here = pl.pallas_call(
            place_kernel,
            in_specs=[smem] + [vmem] * slabs,
            out_specs=vmem,
            out_shape=jax.ShapeDtypeStruct(act_shape, jnp.bfloat16),
            compiler_params=pltpu.CompilerParams(vmem_limit_bytes=12 << 20),
            name="place_blocks",
        )(slab, *act_grads)
    else:
        here = lax.all_to_all(act_grads[0], "slab", split_axis=0, concat_axis=0, tiled=True)
    if not packed:
        here = here.reshape(width_deep, padded)
    grad_scale = 1.0 / math.sqrt(cell_total)
    bits = place_bits()
    stages = [tuple(range(b, min(b + 2, bits))) for b in range(3, bits, 2)]
    row = tuple((0, ky) for ky in range(3))
    jobs = ((tuple((1, ky) for ky in range(3)), 1), (row, 2))
    parts = tap_sums(here, fine_input, depth, grad_scale, jobs, (width_deep, padded))
    parts, here_again = lax.optimization_barrier((parts, here))
    last_parts, middle_parts = parts
    after = from_next(here, "slab")
    grad_input = input_plane(0, (here_again,), (1,), w_down, fine_input.shape, padded)
    grad_input, fine_again = lax.optimization_barrier((grad_input, fine_input))
    shifted = shifted_fine(fine_again, fine_input.shape[0] - 1)
    (parts,) = tap_sums(after, shifted, depth, grad_scale, ((row, 1),), (width_deep, padded))
    kept, last_kept, parts = lax.optimization_barrier((middle_parts[0], last_parts[0], parts))
    middle_taps = exchange_parts((kept, *middle_parts[1:]), 2)
    last_taps = exchange_parts((last_kept, *last_parts[1:]), 1)
    first_taps = exchange_parts(parts, 1)
    first_taps, middle_taps, last_taps, after, grad_input = lax.optimization_barrier(
        (first_taps, middle_taps, last_taps, after, grad_input)
    )
    outer_taps = exchange(jnp.concatenate((first_taps, last_taps), axis=-1), (1, 2))
    middle_taps = exchange(middle_taps, (2,))
    grad_input = input_plane(1, (here, after), (2, 0), w_down, fine_input.shape, padded, grad_input)
    taps, grad_input = lax.optimization_barrier(
        (jnp.concatenate((outer_taps, middle_taps), axis=-1), grad_input)
    )
    for stage in stages:
        taps = exchange(taps, stage, jnp.float32 if stage is stages[-1] else jnp.bfloat16)
    rows = width_deep >> bits
    taps = taps.reshape(rows, 27, width_in)
    grad_down = jnp.concatenate((taps[:, :9], taps[:, 18:], taps[:, 9:18]), axis=1).astype(jnp.float32)
    return (grad_input, grad_down, grad_gain, grad_shift)


def solution(mesh):
    return jax.shard_map(
        local,
        mesh=mesh,
        in_specs=(
            P("slab", "grp", None, None),
            P("slab", "grp", None, None),
            P("slab", None, "grp"),
            P("slab", None, "grp"),
            P("slab"),
            P(),
            P(),
        ),
        out_specs=(
            P("slab", "grp", None, None),
            P(("slab", "grp"), None, None),
            P("slab"),
            P("slab"),
        ),
        check_vma=False,
    )
```
